512 devices in a mesh: head: 8 (over y_hi, x), tile: 64 (over z, y_lo, core).
Axes of the slice: x: 4, y: 8 (y_hi: 2, y_lo: 4; y = y_hi * 4 + y_lo), z: 8, core: 2. Of those that a mesh axis runs over, the one named last changes fastest.
Arguments:
- queries: bfloat16 [16384, 3072], P('tile', 'head'), may hold values from -8 to 8, as said below
- keys_values: bfloat16 [16384, 2, 3072], P('tile', None, 'head'), may hold values from -8 to 8
- cond_kv: bfloat16 [512, 2, 3072], P('tile', None, 'head'), may hold values from -6 to 6
- face_mask: int32 [64, 2], P('tile'), may hold values 0 or 1
- d_out: bfloat16 [16384, 3072], P('tile', 'head'), may hold values from -6 to 6
Outputs:
- attended: bfloat16 [16384, 3072], P('tile', 'head')
- grad_queries: bfloat16 [16384, 3072], P('tile', 'head')
- grad_keys_values: bfloat16 [16384, 2, 3072], P('tile', None, 'head')
- grad_cond: float32 [512, 2, 3072], P('tile', None, 'head')
The draws below stay inside these ranges and needn't reach their ends.
Inputs may be any that keep to these rules, and one draw needn't show every extreme that they name: `queries`: query entries lie within the range.
All inputs are finite; a program needn't handle non-finite values. No bound on the sum of `face_mask` on one device may be relied on, other than what follows from the above.
Results may differ from the reference program's by a relative error of at most 0.023.
Values may be sent and summed in bfloat16 or wider, within the bound.
No kernel may reach another device: no remote copies, remote signals or barrier semaphores. Data moves between devices by JAX's collectives and lax.ppermute only.
A program may use at most 64 MiB of HBM per device.

```python
import jax
import jax.numpy as jnp
from jax import lax

HEADS = 24
HEAD_DIM = 128
TOK_DEV = 256
FACE = 128
TILES = 64
TOKENS = 16384
COND = 512
N_TILE = 64


def draw_queries(key, part):
    key = jax.random.fold_in(key, 1)
    shape = (TOKENS, HEADS * HEAD_DIM)
    return jnp.clip(jax.random.normal(key, shape, jnp.float32), -6.0, 6.0).astype(jnp.bfloat16)


def draw_keys_values(key, part):
    key = jax.random.fold_in(key, 2)
    shape = (TOKENS, 2, HEADS * HEAD_DIM)
    return jnp.clip(jax.random.normal(key, shape, jnp.float32), -6.0, 6.0).astype(jnp.bfloat16)


def set_ends(drawn, rng, low, high):
    place = [jax.random.randint(jax.random.fold_in(rng, axis), (), 0, length) for axis, length in enumerate(drawn.shape)]
    longest = drawn.shape.index(max(drawn.shape))
    next_to = place[:longest] + [(place[longest] + 1) % drawn.shape[longest]] + place[longest + 1:]
    return drawn.at[tuple(place)].set(low).at[tuple(next_to)].set(high)


def shard_levels(stream_key, extent, shards, low, top_value):
    level, own = 1.0, jax.random.fold_in(stream_key, 6)
    for position, blocks in shards:
        draws = jnp.exp(jax.random.uniform(jax.random.fold_in(own, position), (blocks,), jnp.float32, low / len(shards), top_value / len(shards)))
        level = level * jnp.repeat(draws, extent[position] // blocks).reshape([-1 if axis == position else 1 for axis in range(len(extent))])
    return level


def bell_draw(own_key, extent, scale, most, split=(), held_as=jnp.bfloat16):
    drawn = scale * jax.random.normal(own_key, extent, jnp.float32)
    if split:
        drawn = drawn * shard_levels(own_key, extent, split, -0.22, 0.18)
    return jnp.clip(drawn, -most, most).astype(held_as)


def setup_inputs(seed: int = 0) -> dict:
    key_list = jax.random.split(jax.random.key(seed), 6)
    queries = draw_queries(jax.random.fold_in(key_list[5], 71), 0)
    keys_values = draw_keys_values(jax.random.fold_in(key_list[5], 71), 0)
    cond_kv = bell_draw(key_list[2], (COND, 2, HEADS * HEAD_DIM), 1.0, 6.0, ((0, 64), (2, 8)))
    face_mask = set_ends((jax.random.randint(key_list[3], (TILES, 2), 0, 4) < 3).astype(jnp.int32), jax.random.fold_in(key_list[3], 1), 0, 1)
    d_out = bell_draw(key_list[4], (TOKENS, HEADS * HEAD_DIM), 1.0, 6.0, ((0, 64), (1, 8)))
    return dict(queries=queries, keys_values=keys_values, cond_kv=cond_kv, face_mask=face_mask, d_out=d_out)


neg_large = -1.0e30


def key_bias(near_rows, query_rows, allow_left, allow_right, total_keys):
    places = jnp.arange(total_keys)
    masked = ((places < FACE) & jnp.logical_not(allow_left)) | ((places >= FACE + query_rows) & (places < near_rows) & jnp.logical_not(allow_right))
    return jnp.where(masked, neg_large, 0.0).astype(jnp.float32)


def tile_pass(cond_total, tile_item, cond_kv):
    queries, own_rows, left_face, right_face, grad_out, allow_left, allow_right = tile_item
    query_rows = queries.shape[0]
    width = queries.shape[1]
    head_count = width // HEAD_DIM
    near_rows = 2 * FACE + query_rows
    key_rows = jnp.concatenate([left_face, own_rows, right_face, cond_kv], axis=0)
    total_keys = key_rows.shape[0]
    score_scale = HEAD_DIM ** -0.5
    query_f = queries.astype(jnp.float32).reshape(query_rows, head_count, HEAD_DIM)
    key_f = key_rows[:, 0].astype(jnp.float32).reshape(total_keys, head_count, HEAD_DIM)
    value_f = key_rows[:, 1].astype(jnp.float32).reshape(total_keys, head_count, HEAD_DIM)
    grad_f = grad_out.astype(jnp.float32).reshape(query_rows, head_count, HEAD_DIM)
    bias_row = key_bias(near_rows, query_rows, allow_left, allow_right, total_keys)
    scores = jnp.einsum('qhd,khd->hqk', query_f, key_f) * score_scale + bias_row[None, None, :]
    row_max = jnp.max(scores, axis=2, keepdims=True)
    raised = jnp.exp(scores - row_max)
    probs = raised / jnp.sum(raised, axis=2, keepdims=True)
    probs_low = lax.optimization_barrier(probs.astype(jnp.bfloat16)).astype(jnp.float32)
    attended = jnp.einsum('hqk,khd->qhd', probs_low, value_f).reshape(query_rows, width).astype(jnp.bfloat16)
    grad_p = jnp.einsum('qhd,khd->hqk', grad_f, value_f)
    delta = jnp.sum(grad_f * attended.astype(jnp.float32).reshape(query_rows, head_count, HEAD_DIM), axis=2).T
    grad_s = (probs * (grad_p - delta[:, :, None]) * score_scale).astype(jnp.bfloat16)
    grad_s = lax.optimization_barrier(grad_s).astype(jnp.float32)
    grad_q = jnp.einsum('hqk,khd->qhd', grad_s, key_f).reshape(query_rows, width).astype(jnp.bfloat16)
    grad_k = jnp.einsum('hqk,qhd->khd', grad_s, query_f).reshape(total_keys, width)
    grad_v = jnp.einsum('hqk,qhd->khd', probs_low, grad_f).reshape(total_keys, width)
    grad_kv = jnp.stack([grad_k, grad_v], axis=1)
    pieces = (attended, grad_q, grad_kv[:FACE], grad_kv[FACE:FACE + query_rows], grad_kv[FACE + query_rows:near_rows])
    return cond_total + grad_kv[near_rows:], pieces


def reference(queries, keys_values, cond_kv, face_mask, d_out):
    width = queries.shape[1]
    tiled_q = queries.reshape(N_TILE, TOK_DEV, width)
    tiled_kv = keys_values.reshape(N_TILE, TOK_DEV, 2, width)
    tiled_g = d_out.reshape(N_TILE, TOK_DEV, width)
    blank = jnp.zeros((1, FACE, 2, width), keys_values.dtype)
    left_faces = jnp.concatenate([blank, tiled_kv[:-1, TOK_DEV - FACE:]], axis=0)
    right_faces = jnp.concatenate([tiled_kv[1:, :FACE], blank], axis=0)
    tile_ids = jnp.arange(N_TILE)
    allow_left = (face_mask[:, 0] == 1) & (tile_ids > 0)
    allow_right = (face_mask[:, 1] == 1) & (tile_ids < N_TILE - 1)
    start_total = jnp.zeros((COND, 2, width), jnp.float32)
    cond_grad, pieces = lax.scan(lambda total, item: tile_pass(total, item, cond_kv), start_total, (tiled_q, tiled_kv, left_faces, right_faces, tiled_g, allow_left, allow_right))
    attended, grad_q, grad_left, grad_own, grad_right = pieces
    blank_grad = jnp.zeros((1, FACE, 2, width), jnp.float32)
    grad_own = grad_own.at[:, TOK_DEV - FACE:].add(jnp.concatenate([grad_left[1:], blank_grad], axis=0))
    grad_own = grad_own.at[:, :FACE].add(jnp.concatenate([blank_grad, grad_right[:-1]], axis=0))
    return (attended.reshape(TOKENS, width), grad_q.reshape(TOKENS, width), grad_own.reshape(TOKENS, 2, width).astype(jnp.bfloat16), cond_grad)
```

```python
import jax
import jax.numpy as jnp
from jax import lax
from jax.sharding import PartitionSpec as P

HEAD_DIM = 128
FACE = 128


neg_large = -1e30


def padded(shard, sides, width):
    for axis, dim in sides:
        size, length = (lax.axis_size(axis), shard.shape[dim])
        up = [(i, (i + 1) % size) for i in range(size - 1)]
        down = [(j, i) for i, j in up]
        last = lax.slice_in_dim(shard, length - width, length, axis=dim)
        leading = lax.slice_in_dim(shard, 0, width, axis=dim)
        before = lax.ppermute(last, axis, up)
        after = lax.ppermute(leading, axis, down)
        shard = jnp.concatenate([before, shard, after], axis=dim)
    return shard


def shifted(block, axis, distance):
    devices = range(lax.axis_size(axis))
    route = [(i - distance, i) for i in devices if i - distance in devices]
    return lax.ppermute(block, axis, route)


def place(z, y, core):
    return (z * Y_RUN + y) * CORES + core


Y_RUN = 4
CORES = 2


def y_turn(size, distance):
    return [
        (place(z, y, c), place(z, (y + distance) % Y_RUN, c))
        for z in range(size // (Y_RUN * CORES))
        for y in range(Y_RUN)
        for c in range(CORES)
    ]


def other_core(size):
    return [(t, t ^ 1) for t in range(size)]


def z_groups(size):
    depth = size // (Y_RUN * CORES)
    return [[place(z, y, c) for z in range(depth)] for y in range(Y_RUN) for c in range(CORES)]


def y_groups(size):
    depth = size // (Y_RUN * CORES)
    return [[place(z, y, c) for y in range(Y_RUN)] for z in range(depth) for c in range(CORES)]


def gather_cond(cond_kv):
    size = lax.axis_size("tile")
    rows = cond_kv.shape[0]
    flat = cond_kv.reshape(rows, -1)
    width = flat.shape[1]
    depth = size // (Y_RUN * CORES)
    run = [flat] + [lax.ppermute(flat, "tile", y_turn(size, d)) for d in range(1, Y_RUN)]
    run = jnp.concatenate(run, axis=0)
    spread = jnp.broadcast_to(run[None], (depth,) + run.shape)
    ring = lax.all_to_all(
        spread, "tile", 0, 0, axis_index_groups=z_groups(size), tiled=True
    ).reshape(-1, width)
    other = lax.ppermute(ring, "tile", other_core(size))
    return jnp.concatenate([ring, other], axis=0)


def scatter_cond(partial):
    size = lax.axis_size("tile")
    depth = size // (Y_RUN * CORES)
    width = partial.shape[1]
    half = partial.shape[0] // 2
    wide = partial.astype(jnp.bfloat16)
    other = lax.ppermute(wide[half:], "tile", other_core(size))
    mine = partial[:half] + other.astype(jnp.float32)
    blocks = mine.astype(jnp.bfloat16).reshape(depth, half // depth, width)
    ring = lax.all_to_all(blocks, "tile", 0, 0, axis_index_groups=z_groups(size), tiled=True)
    ring = jnp.sum(ring.astype(jnp.float32), axis=0)
    rows = ring.shape[0] // Y_RUN
    total = ring[:rows]
    for d in range(1, Y_RUN):
        part = ring[d * rows : (d + 1) * rows].astype(jnp.bfloat16)
        total = total + lax.ppermute(part, "tile", y_turn(size, -d)).astype(jnp.float32)
    return total.reshape(rows, 2, width // 2)


def per_device(queries, keys_values, cond_kv, face_mask, d_out):
    query_rows = queries.shape[0]
    width = queries.shape[1]
    head_count = width // HEAD_DIM
    tile_index = lax.axis_index("tile")
    tile_count = lax.axis_size("tile")
    near_rows = 2 * FACE + query_rows
    extended = padded(keys_values, (("tile", 0),), FACE)
    gathered = gather_cond(cond_kv)
    gathered = gathered.reshape(gathered.shape[0], 2, width)
    key_rows = jnp.concatenate([extended, gathered], axis=0)
    total_keys = key_rows.shape[0]
    allow_left = (face_mask[0, 0] == 1) & (tile_index > 0)
    allow_right = (face_mask[0, 1] == 1) & (tile_index < tile_count - 1)
    places = jnp.arange(total_keys)
    masked = (places < FACE) & jnp.logical_not(allow_left) | (places >= FACE + query_rows) & (
        places < near_rows
    ) & jnp.logical_not(allow_right)
    bias_row = jnp.where(masked, neg_large, 0.0).astype(jnp.float32)[None, :]
    score_scale = HEAD_DIM ** (-0.5)
    contract_last = (((1,), (1,)), ((), ()))
    contract_first = (((0,), (0,)), ((), ()))
    attended_parts = []
    grad_q_parts = []
    grad_k_parts = []
    grad_v_parts = []
    grad_s_parts = []
    probs_parts = []
    for head in range(head_count):
        lower = head * HEAD_DIM
        upper = lower + HEAD_DIM
        query_head = queries[:, lower:upper]
        key_head = key_rows[:, 0, lower:upper]
        value_head = key_rows[:, 1, lower:upper]
        grad_head = d_out[:, lower:upper]
        scores = (
            lax.dot_general(query_head, key_head, contract_last, preferred_element_type=jnp.float32)
            * score_scale
            + bias_row
        )
        row_max = jnp.max(scores, axis=1, keepdims=True)
        raised = jnp.exp(scores - row_max)
        probs = raised / jnp.sum(raised, axis=1, keepdims=True)
        probs_low = probs.astype(jnp.bfloat16)
        attended_head = jnp.dot(probs_low, value_head, preferred_element_type=jnp.float32).astype(
            jnp.bfloat16
        )
        grad_p = lax.dot_general(
            grad_head, value_head, contract_last, preferred_element_type=jnp.float32
        )
        delta = jnp.sum(
            grad_head.astype(jnp.float32) * attended_head.astype(jnp.float32), axis=1, keepdims=True
        )
        grad_s = (probs * (grad_p - delta) * score_scale).astype(jnp.bfloat16)
        grad_q_parts.append(
            jnp.dot(grad_s, key_head, preferred_element_type=jnp.float32).astype(jnp.bfloat16)
        )
        grad_k_parts.append(
            lax.dot_general(
                grad_s[:, :near_rows],
                query_head,
                contract_first,
                preferred_element_type=jnp.float32,
            )
        )
        grad_v_parts.append(
            lax.dot_general(
                probs_low[:, :near_rows],
                grad_head,
                contract_first,
                preferred_element_type=jnp.float32,
            )
        )
        attended_parts.append(attended_head)
        grad_s_parts.append(grad_s[:, near_rows:])
        probs_parts.append(probs_low[:, near_rows:])
    attended = jnp.concatenate(attended_parts, axis=1)
    grad_queries = jnp.concatenate(grad_q_parts, axis=1)
    grad_near = jnp.stack(
        [jnp.concatenate(grad_k_parts, axis=1), jnp.concatenate(grad_v_parts, axis=1)], axis=1
    )
    from_next = shifted(grad_near[:FACE].astype(jnp.bfloat16), "tile", -1).astype(jnp.float32)
    from_prev = shifted(grad_near[FACE + query_rows :].astype(jnp.bfloat16), "tile", 1).astype(
        jnp.float32
    )
    grad_own = grad_near[FACE : FACE + query_rows]
    grad_own = grad_own.at[query_rows - FACE :].add(from_next)
    grad_own = grad_own.at[:FACE].add(from_prev)
    key_grads = []
    value_grads = []
    for head in range(head_count):
        lower = head * HEAD_DIM
        upper = lower + HEAD_DIM
        part_s = grad_s_parts[head]
        part_p = probs_parts[head]
        key_grads.append(
            lax.dot_general(
                part_s, queries[:, lower:upper], contract_first, preferred_element_type=jnp.float32
            )
        )
        value_grads.append(
            lax.dot_general(
                part_p, d_out[:, lower:upper], contract_first, preferred_element_type=jnp.float32
            )
        )
    grad_cond = scatter_cond(jnp.concatenate(key_grads + value_grads, axis=1))
    return (attended, grad_queries, grad_own.astype(jnp.bfloat16), grad_cond)


def solution(mesh):
    return jax.shard_map(
        per_device,
        mesh=mesh,
        in_specs=(
            P("tile", "head"),
            P("tile", None, "head"),
            P("tile", None, "head"),
            P("tile", None),
            P("tile", "head"),
        ),
        out_specs=(
            P("tile", "head"),
            P("tile", "head"),
            P("tile", None, "head"),
            P("tile", None, "head"),
        ),
        check_vma=False,
    )
```

```python
import jax
import jax.numpy as jnp
from jax import lax
from jax.sharding import PartitionSpec as P

HEAD_DIM = 128
FACE = 128


neg_large = -1e30


def padded(shard, sides, width):
    for axis, dim in sides:
        size, length = (lax.axis_size(axis), shard.shape[dim])
        up = [(i, (i + 1) % size) for i in range(size - 1)]
        down = [(j, i) for i, j in up]
        last = lax.slice_in_dim(shard, length - width, length, axis=dim)
        leading = lax.slice_in_dim(shard, 0, width, axis=dim)
        before = lax.ppermute(last, axis, up)
        after = lax.ppermute(leading, axis, down)
        shard = jnp.concatenate([before, shard, after], axis=dim)
    return shard


def shifted(block, axis, distance):
    devices = range(lax.axis_size(axis))
    route = [(i - distance, i) for i in devices if i - distance in devices]
    return lax.ppermute(block, axis, route)


CORES = 2


def other_core(size):
    return [(t, t ^ 1) for t in range(size)]


def same_core(size):
    return [list(range(c, size, CORES)) for c in range(CORES)]


def gather_cond(cond_kv):
    size = lax.axis_size("tile")
    rows = cond_kv.shape[0]
    flat = cond_kv.reshape(rows, -1)
    width = flat.shape[1]
    spread = jnp.broadcast_to(flat[None], (size // CORES,) + flat.shape)
    half = lax.all_to_all(
        spread, "tile", 0, 0, axis_index_groups=same_core(size), tiled=True
    ).reshape(-1, width)
    other = lax.ppermute(half, "tile", other_core(size))
    return jnp.concatenate([half, other], axis=0)


def scatter_cond(partial):
    size = lax.axis_size("tile")
    width = partial.shape[1]
    chips = size // CORES
    half = partial.shape[0] // 2
    other = lax.ppermute(partial[half:].astype(jnp.bfloat16), "tile", other_core(size))
    mine = partial[:half] + other.astype(jnp.float32)
    blocks = mine.astype(jnp.bfloat16).reshape(chips, half // chips, width)
    parts = lax.all_to_all(blocks, "tile", 0, 0, axis_index_groups=same_core(size), tiled=True)
    total = jnp.sum(parts.astype(jnp.float32), axis=0)
    return total.reshape(half // chips, 2, width // 2)


def per_device(queries, keys_values, cond_kv, face_mask, d_out):
    query_rows = queries.shape[0]
    width = queries.shape[1]
    head_count = width // HEAD_DIM
    tile_index = lax.axis_index("tile")
    tile_count = lax.axis_size("tile")
    near_rows = 2 * FACE + query_rows
    extended = padded(keys_values, (("tile", 0),), FACE)
    gathered = gather_cond(cond_kv)
    gathered = gathered.reshape(gathered.shape[0], 2, width)
    key_rows = jnp.concatenate([extended, gathered], axis=0)
    total_keys = key_rows.shape[0]
    allow_left = (face_mask[0, 0] == 1) & (tile_index > 0)
    allow_right = (face_mask[0, 1] == 1) & (tile_index < tile_count - 1)
    places = jnp.arange(total_keys)
    masked = (places < FACE) & jnp.logical_not(allow_left) | (places >= FACE + query_rows) & (
        places < near_rows
    ) & jnp.logical_not(allow_right)
    bias_row = jnp.where(masked, neg_large, 0.0).astype(jnp.float32)[None, :]
    score_scale = HEAD_DIM ** (-0.5)
    contract_last = (((1,), (1,)), ((), ()))
    contract_first = (((0,), (0,)), ((), ()))
    attended_parts = []
    grad_q_parts = []
    grad_k_parts = []
    grad_v_parts = []
    grad_s_parts = []
    probs_parts = []
    for head in range(head_count):
        lower = head * HEAD_DIM
        upper = lower + HEAD_DIM
        query_head = queries[:, lower:upper]
        key_head = key_rows[:, 0, lower:upper]
        value_head = key_rows[:, 1, lower:upper]
        grad_head = d_out[:, lower:upper]
        scores = (
            lax.dot_general(query_head, key_head, contract_last, preferred_element_type=jnp.float32)
            * score_scale
            + bias_row
        )
        row_max = jnp.max(scores, axis=1, keepdims=True)
        raised = jnp.exp(scores - row_max)
        probs = raised / jnp.sum(raised, axis=1, keepdims=True)
        probs_low = probs.astype(jnp.bfloat16)
        attended_head = jnp.dot(probs_low, value_head, preferred_element_type=jnp.float32).astype(
            jnp.bfloat16
        )
        grad_p = lax.dot_general(
            grad_head, value_head, contract_last, preferred_element_type=jnp.float32
        )
        delta = jnp.sum(
            grad_head.astype(jnp.float32) * attended_head.astype(jnp.float32), axis=1, keepdims=True
        )
        grad_s = (probs * (grad_p - delta) * score_scale).astype(jnp.bfloat16)
        grad_q_parts.append(
            jnp.dot(grad_s, key_head, preferred_element_type=jnp.float32).astype(jnp.bfloat16)
        )
        grad_k_parts.append(
            lax.dot_general(
                grad_s[:, :near_rows],
                query_head,
                contract_first,
                preferred_element_type=jnp.float32,
            )
        )
        grad_v_parts.append(
            lax.dot_general(
                probs_low[:, :near_rows],
                grad_head,
                contract_first,
                preferred_element_type=jnp.float32,
            )
        )
        attended_parts.append(attended_head)
        grad_s_parts.append(grad_s[:, near_rows:])
        probs_parts.append(probs_low[:, near_rows:])
    attended = jnp.concatenate(attended_parts, axis=1)
    grad_queries = jnp.concatenate(grad_q_parts, axis=1)
    grad_near = jnp.stack(
        [jnp.concatenate(grad_k_parts, axis=1), jnp.concatenate(grad_v_parts, axis=1)], axis=1
    )
    from_next = shifted(grad_near[:FACE].astype(jnp.bfloat16), "tile", -1).astype(jnp.float32)
    from_prev = shifted(grad_near[FACE + query_rows :].astype(jnp.bfloat16), "tile", 1).astype(
        jnp.float32
    )
    grad_own = grad_near[FACE : FACE + query_rows]
    grad_own = grad_own.at[query_rows - FACE :].add(from_next)
    grad_own = grad_own.at[:FACE].add(from_prev)
    key_grads = []
    value_grads = []
    for head in range(head_count):
        lower = head * HEAD_DIM
        upper = lower + HEAD_DIM
        part_s = grad_s_parts[head]
        part_p = probs_parts[head]
        key_grads.append(
            lax.dot_general(
                part_s, queries[:, lower:upper], contract_first, preferred_element_type=jnp.float32
            )
        )
        value_grads.append(
            lax.dot_general(
                part_p, d_out[:, lower:upper], contract_first, preferred_element_type=jnp.float32
            )
        )
    grad_cond = scatter_cond(jnp.concatenate(key_grads + value_grads, axis=1))
    return (attended, grad_queries, grad_own.astype(jnp.bfloat16), grad_cond)


def solution(mesh):
    return jax.shard_map(
        per_device,
        mesh=mesh,
        in_specs=(
            P("tile", "head"),
            P("tile", None, "head"),
            P("tile", None, "head"),
            P("tile", None),
            P("tile", "head"),
        ),
        out_specs=(
            P("tile", "head"),
            P("tile", "head"),
            P("tile", None, "head"),
            P("tile", None, "head"),
        ),
        check_vma=False,
    )
```

```python
import functools

import jax
import jax.numpy as jnp
from jax import lax
from jax.experimental import pallas as pl
from jax.experimental.pallas import tpu as pltpu
from jax.sharding import PartitionSpec as P

HEAD_DIM = 128
FACE = 128
CORES = 2
SCALE = HEAD_DIM**-0.5
LOG2E = 1.4426950408889634
NEG_LARGE = -1e30
STAT_ROWS = 16

NT = (((1,), (1,)), ((), ()))
TN = (((0,), (0,)), ((), ()))


def dot(a, b, dims=(((1,), (0,)), ((), ()))):
    return lax.dot_general(a, b, dims, preferred_element_type=jnp.float32)


def other_core(size):
    return [(t, t ^ 1) for t in range(size)]


def same_core(size):
    return [list(range(c, size, CORES)) for c in range(CORES)]


def params(mib=48):
    return pltpu.CompilerParams(vmem_limit_bytes=mib * 1024 * 1024)


VMEM = pl.BlockSpec(memory_space=pltpu.VMEM)
SMEM = pl.BlockSpec(memory_space=pltpu.SMEM)


def cost(queries, keys, heads, products, size):
    return pl.CostEstimate(
        flops=2 * products * heads * queries * keys * HEAD_DIM,
        bytes_accessed=size,
        transcendentals=heads * queries * keys,
    )


def face_bias(mask_ref):
    tile = lax.axis_index("tile")
    last = lax.axis_size("tile") - 1
    lower = jnp.where((mask_ref[0, 0] == 1) & (tile > 0), 0.0, NEG_LARGE)
    upper = jnp.where((mask_ref[0, 1] == 1) & (tile < last), 0.0, NEG_LARGE)
    return lower.astype(jnp.float32), upper.astype(jnp.float32)


def lanes(head, half, width):
    return pl.ds(pl.multiple_of(half * width + head * HEAD_DIM, HEAD_DIM), HEAD_DIM)


def raised_stats(scores, grads):
    top = functools.reduce(jnp.maximum, [jnp.max(s, axis=0, keepdims=True) for s in scores])
    total = 0.0
    weighted = 0.0
    for s, g in zip(scores, grads):
        e = jnp.exp2(s - top)
        total = total + jnp.sum(e, axis=0, keepdims=True)
        weighted = weighted + jnp.sum(e * g, axis=0, keepdims=True)
    return top, total, weighted


def near_stats_kernel(mask_ref, qd_ref, own_ref, lower_ref, upper_ref, stat_ref):
    width = qd_ref.shape[1] // 2
    lower_bias, upper_bias = face_bias(mask_ref)
    for head in range(width // HEAD_DIM):
        at = [pl.ds(half * width + head * HEAD_DIM, HEAD_DIM) for half in range(2)]
        q, d = qd_ref[:, at[0]], qd_ref[:, at[1]]
        scores, grads = [], []
        for ref, bias in ((lower_ref, lower_bias), (own_ref, None), (upper_ref, upper_bias)):
            s = dot(ref[:, at[0]], q, NT) * (SCALE * LOG2E)
            scores.append(s if bias is None else s + bias)
            grads.append(dot(ref[:, at[1]], d, NT))
        for i, row in enumerate(raised_stats(scores, grads)):
            stat_ref[pl.ds(3 * head + i, 1), :] = row


def near_stats(mask, qd, own, lower, upper):
    rows, width = qd.shape
    heads = width // 2 // HEAD_DIM
    return pl.pallas_call(
        near_stats_kernel,
        out_shape=jax.ShapeDtypeStruct((STAT_ROWS, rows), jnp.float32),
        in_specs=[SMEM, VMEM, VMEM, VMEM, VMEM],
        out_specs=VMEM,
        compiler_params=params(),
        cost_estimate=cost(rows, rows + 2 * FACE, heads, 2, 5 * qd.size),
        name="near_stats",
    )(mask, qd, own, lower, upper)


def cond_stats_kernel(qd_ref, far_ref, cond_ref, stat_ref):
    rows, width = qd_ref.shape
    width = width // 2
    for head in range(width // HEAD_DIM):
        at = [pl.ds(half * width + head * HEAD_DIM, HEAD_DIM) for half in range(2)]
        key, value = cond_ref[:, at[0]], cond_ref[:, at[1]]
        for side, ref in enumerate((qd_ref, far_ref)):
            s = dot(key, ref[:, at[0]], NT) * (SCALE * LOG2E)
            g = dot(value, ref[:, at[1]], NT)
            for i, row in enumerate(raised_stats([s], [g])):
                stat_ref[side, pl.ds(3 * head + i, 1), :] = row


def cond_stats(qd, far, cond):
    rows, width = qd.shape
    heads = width // 2 // HEAD_DIM
    return pl.pallas_call(
        cond_stats_kernel,
        out_shape=jax.ShapeDtypeStruct((2, STAT_ROWS, rows), jnp.float32),
        in_specs=[VMEM, VMEM, VMEM],
        out_specs=VMEM,
        compiler_params=params(),
        cost_estimate=cost(2 * rows, cond.shape[0], heads, 2, 6 * qd.size),
        name="cond_stats",
    )(qd, far, cond)


def cond_grads_kernel(qd_ref, far_ref, cond_ref, near_ref, mine_ref, their_ref, out_ref):
    rows, width = qd_ref.shape
    width = width // 2
    for head in range(width // HEAD_DIM):
        at = [pl.ds(half * width + head * HEAD_DIM, HEAD_DIM) for half in range(2)]
        key, value = cond_ref[:, at[0]], cond_ref[:, at[1]]
        grad_k = 0.0
        grad_v = 0.0
        for side, ref in enumerate((qd_ref, far_ref)):
            near = near_ref if side == 0 else their_ref.at[0]
            parts = [
                [r[pl.ds(3 * head + i, 1), :] for i in range(3)]
                for r in (near, mine_ref.at[side], their_ref.at[2 - side])
            ]
            top = functools.reduce(jnp.maximum, [p[0] for p in parts])
            total = sum(p[1] * jnp.exp2(p[0] - top) for p in parts)
            weighted = sum(p[2] * jnp.exp2(p[0] - top) for p in parts)
            level = top + jnp.log2(total)
            delta = weighted / total
            q, d = ref[:, at[0]], ref[:, at[1]]
            p = jnp.exp2(dot(key, q, NT) * (SCALE * LOG2E) - level)
            g = dot(value, d, NT)
            grad_s = (p * (g - delta)).astype(jnp.bfloat16)
            grad_k = grad_k + dot(grad_s, q)
            grad_v = grad_v + dot(p.astype(jnp.bfloat16), d)
        out_ref[:, at[0]] = (grad_k * SCALE).astype(out_ref.dtype)
        out_ref[:, at[1]] = grad_v.astype(out_ref.dtype)


def cond_grads(qd, far, cond, near, mine, theirs):
    rows, width = qd.shape
    heads = width // 2 // HEAD_DIM
    return pl.pallas_call(
        cond_grads_kernel,
        out_shape=jax.ShapeDtypeStruct(cond.shape, jnp.bfloat16),
        in_specs=[VMEM] * 6,
        out_specs=VMEM,
        compiler_params=params(),
        cost_estimate=cost(2 * rows, cond.shape[0], heads, 4, 8 * qd.size),
        name="cond_grads",
    )(qd, far, cond, near, mine, theirs)


def own_kernel(
    mask_ref, qd_ref, own_ref, lower_ref, upper_ref, cond_ref, far_cond_ref,
    att_ref, dq_ref, down_ref, keep_ref, up_ref,
):
    width = qd_ref.shape[1] // 2
    lower_bias, upper_bias = face_bias(mask_ref)

    def one(head, _):
        at = [lanes(head, half, width) for half in range(2)]
        q, d = qd_ref[:, at[0]], qd_ref[:, at[1]]
        segments = (
            (lower_ref, lower_bias, down_ref),
            (own_ref, None, keep_ref),
            (upper_ref, upper_bias, up_ref),
            (cond_ref, None, None),
            (far_cond_ref, None, None),
        )
        scores = []
        for ref, bias, _out in segments:
            s = dot(ref[:, at[0]], q, NT) * (SCALE * LOG2E)
            scores.append(s if bias is None else s + bias)
        top = functools.reduce(jnp.maximum, [jnp.max(s, axis=0, keepdims=True) for s in scores])
        raised = [jnp.exp2(s - top) for s in scores]
        total = sum(jnp.sum(e, axis=0, keepdims=True) for e in raised)
        inverse = 1.0 / total
        probs = [e * inverse for e in raised]
        low = [p.astype(jnp.bfloat16) for p in probs]
        att = sum(dot(ref[:, at[1]], p, TN) for (ref, _b, _o), p in zip(segments, low))
        att = att.astype(jnp.bfloat16)
        d_cols = d.astype(jnp.float32).T
        delta = jnp.sum(d_cols * att.astype(jnp.float32), axis=0, keepdims=True)
        att_ref[:, at[0]] = att.astype(jnp.float32).T.astype(jnp.bfloat16)
        dq = 0.0
        for (ref, _b, out), p, pl_ in zip(segments, probs, low):
            g = dot(ref[:, at[1]], d, NT)
            grad_s = (p * (g - delta) * SCALE).astype(jnp.bfloat16)
            dq = dq + dot(ref[:, at[0]], grad_s, TN)
            if out is not None:
                out[:, at[0]] = dot(grad_s, q).astype(out.dtype)
                out[:, at[1]] = dot(pl_, d).astype(out.dtype)
        dq_ref[:, at[0]] = dq.T.astype(jnp.bfloat16)
        return 0

    lax.fori_loop(0, width // HEAD_DIM, one, 0)


def own_pass(mask, qd, own, lower, upper, cond, far_cond):
    rows, width = qd.shape
    heads = width // 2 // HEAD_DIM
    keys = rows + 2 * FACE + 2 * cond.shape[0]
    half = jax.ShapeDtypeStruct((rows, width // 2), jnp.bfloat16)
    face = jax.ShapeDtypeStruct((FACE, width), jnp.bfloat16)
    return pl.pallas_call(
        own_kernel,
        out_shape=(half, half, face, jax.ShapeDtypeStruct((rows, width), jnp.float32), face),
        in_specs=[SMEM] + [VMEM] * 6,
        out_specs=(VMEM,) * 5,
        compiler_params=params(),
        cost_estimate=cost(rows, keys, heads, 5, 16 * qd.size),
        name="own_pass",
    )(mask, qd, own, lower, upper, cond, far_cond)


def per_device(queries, keys_values, cond_kv, face_mask, d_out):
    size = lax.axis_size("tile")
    rows, width = queries.shape
    chips = size // CORES
    cond_rows = cond_kv.shape[0]
    swap = other_core(size)
    up = [(i, i + 1) for i in range(size - 1)]
    down = [(i + 1, i) for i in range(size - 1)]

    flat = cond_kv.reshape(cond_rows, 2 * width)
    spread = jnp.broadcast_to(flat[None], (chips,) + flat.shape)
    cond = lax.all_to_all(spread, "tile", 0, 0, axis_index_groups=same_core(size), tiled=True)
    cond = cond.reshape(chips * cond_rows, 2 * width)

    qd = jnp.concatenate([queries, d_out], axis=1)
    own = keys_values.reshape(rows, 2 * width)
    far = lax.ppermute(qd, "tile", swap)
    lower = lax.ppermute(own[rows - FACE :], "tile", up)
    upper = lax.ppermute(own[:FACE], "tile", down)
    near = near_stats(face_mask, qd, own, lower, upper)

    mine = cond_stats(qd, far, cond)
    theirs = lax.ppermute(jnp.concatenate([near[None], mine], axis=0), "tile", swap)
    far_cond = lax.ppermute(cond, "tile", swap)
    grads = cond_grads(qd, far, cond, near, mine, theirs)
    blocks = grads.reshape(chips, cond_rows, 2 * width)
    parts = lax.all_to_all(blocks, "tile", 0, 0, axis_index_groups=same_core(size), tiled=True)
    grad_cond = jnp.sum(parts.astype(jnp.float32), axis=0).reshape(cond_rows, 2, width)

    attended, grad_q, to_prev, keep, to_next = own_pass(
        face_mask, qd, own, lower, upper, cond, far_cond
    )
    from_next = lax.ppermute(to_prev, "tile", down).astype(jnp.float32)
    from_prev = lax.ppermute(to_next, "tile", up).astype(jnp.float32)
    keep = keep + jnp.concatenate([from_prev, from_next], axis=0)
    grad_kv = keep.astype(jnp.bfloat16).reshape(rows, 2, width)
    return attended, grad_q, grad_kv, grad_cond


def solution(mesh):
    return jax.shard_map(
        per_device,
        mesh=mesh,
        in_specs=(
            P("tile", "head"),
            P("tile", None, "head"),
            P("tile", None, "head"),
            P("tile", None),
            P("tile", "head"),
        ),
        out_specs=(
            P("tile", "head"),
            P("tile", "head"),
            P("tile", None, "head"),
            P("tile", None, "head"),
        ),
        check_vma=False,
    )
```

```python
import functools

import jax
import jax.numpy as jnp
from jax import lax
from jax.experimental import pallas as pl
from jax.experimental.pallas import tpu as pltpu
from jax.sharding import PartitionSpec as P

HEAD_DIM = 128
FACE = 128
CORES = 2
SCALE = HEAD_DIM**-0.5
LOG2E = 1.4426950408889634
NEG_LARGE = -1e30
STAT_ROWS = 16

NT = (((1,), (1,)), ((), ()))
TN = (((0,), (0,)), ((), ()))


def dot(a, b, dims=(((1,), (0,)), ((), ()))):
    return lax.dot_general(a, b, dims, preferred_element_type=jnp.float32)


def other_core(size):
    return [(t, t ^ 1) for t in range(size)]


def same_core(size):
    return [list(range(c, size, CORES)) for c in range(CORES)]


def params(mib=48):
    return pltpu.CompilerParams(vmem_limit_bytes=mib * 1024 * 1024)


VMEM = pl.BlockSpec(memory_space=pltpu.VMEM)
SMEM = pl.BlockSpec(memory_space=pltpu.SMEM)


def spread_kernel(cond_ref, out_ref):
    rows, _, width = cond_ref.shape
    flat = jnp.concatenate([cond_ref[:, 0, :], cond_ref[:, 1, :]], axis=1)
    out_ref[...] = jnp.broadcast_to(flat[None], out_ref.shape)


def spread(cond_kv, copies):
    rows, _, width = cond_kv.shape
    return pl.pallas_call(
        spread_kernel,
        out_shape=jax.ShapeDtypeStruct((copies, rows, 2 * width), cond_kv.dtype),
        in_specs=[VMEM],
        out_specs=VMEM,
        compiler_params=params(),
        name="spread",
    )(cond_kv)


def total_kernel(parts_ref, out_ref):
    width = out_ref.shape[2]
    total = jnp.sum(parts_ref[...].astype(jnp.float32), axis=0)
    out_ref[:, 0, :] = total[:, :width]
    out_ref[:, 1, :] = total[:, width:]


def total(parts):
    _, rows, width = parts.shape
    return pl.pallas_call(
        total_kernel,
        out_shape=jax.ShapeDtypeStruct((rows, 2, width // 2), jnp.float32),
        in_specs=[VMEM],
        out_specs=VMEM,
        compiler_params=params(),
        name="total",
    )(parts)


def cost(queries, keys, heads, products, size):
    return pl.CostEstimate(
        flops=2 * products * heads * queries * keys * HEAD_DIM,
        bytes_accessed=size,
        transcendentals=heads * queries * keys,
    )


def face_bias(mask_ref):
    tile = lax.axis_index("tile")
    last = lax.axis_size("tile") - 1
    lower = jnp.where((mask_ref[0, 0] == 1) & (tile > 0), 0.0, NEG_LARGE)
    upper = jnp.where((mask_ref[0, 1] == 1) & (tile < last), 0.0, NEG_LARGE)
    return lower.astype(jnp.float32), upper.astype(jnp.float32)


def raised_stats(scores, grads):
    top = functools.reduce(jnp.maximum, [jnp.max(s, axis=0, keepdims=True) for s in scores])
    total = 0.0
    weighted = 0.0
    for s, g in zip(scores, grads):
        e = jnp.exp2(s - top)
        total = total + jnp.sum(e, axis=0, keepdims=True)
        weighted = weighted + jnp.sum(e * g, axis=0, keepdims=True)
    return top, total, weighted


def near_stats_kernel(mask_ref, qd_ref, own_ref, lower_ref, upper_ref, stat_ref):
    width = qd_ref.shape[1] // 2
    lower_bias, upper_bias = face_bias(mask_ref)
    for head in range(width // HEAD_DIM):
        at = [pl.ds(half * width + head * HEAD_DIM, HEAD_DIM) for half in range(2)]
        q, d = qd_ref[:, at[0]], qd_ref[:, at[1]]
        scores, grads = [], []
        for ref, bias in ((lower_ref, lower_bias), (own_ref, None), (upper_ref, upper_bias)):
            s = dot(ref[:, at[0]], q, NT) * (SCALE * LOG2E)
            scores.append(s if bias is None else s + bias)
            grads.append(dot(ref[:, at[1]], d, NT))
        for i, row in enumerate(raised_stats(scores, grads)):
            stat_ref[pl.ds(3 * head + i, 1), :] = row


def near_stats(mask, qd, own, lower, upper):
    rows, width = qd.shape
    heads = width // 2 // HEAD_DIM
    return pl.pallas_call(
        near_stats_kernel,
        out_shape=jax.ShapeDtypeStruct((STAT_ROWS, rows), jnp.float32),
        in_specs=[SMEM, VMEM, VMEM, VMEM, VMEM],
        out_specs=VMEM,
        compiler_params=params(),
        cost_estimate=cost(rows, rows + 2 * FACE, heads, 2, 5 * qd.size),
        name="near_stats",
    )(mask, qd, own, lower, upper)


def cond_stats_kernel(qd_ref, far_ref, cond_ref, stat_ref):
    rows, width = qd_ref.shape
    width = width // 2
    for head in range(width // HEAD_DIM):
        at = [pl.ds(half * width + head * HEAD_DIM, HEAD_DIM) for half in range(2)]
        key, value = cond_ref[:, at[0]], cond_ref[:, at[1]]
        for side, ref in enumerate((qd_ref, far_ref)):
            s = dot(key, ref[:, at[0]], NT) * (SCALE * LOG2E)
            g = dot(value, ref[:, at[1]], NT)
            for i, row in enumerate(raised_stats([s], [g])):
                stat_ref[side, pl.ds(3 * head + i, 1), :] = row


def cond_stats(qd, far, cond):
    rows, width = qd.shape
    heads = width // 2 // HEAD_DIM
    return pl.pallas_call(
        cond_stats_kernel,
        out_shape=jax.ShapeDtypeStruct((2, STAT_ROWS, rows), jnp.float32),
        in_specs=[VMEM, VMEM, VMEM],
        out_specs=VMEM,
        compiler_params=params(),
        cost_estimate=cost(2 * rows, cond.shape[0], heads, 2, 6 * qd.size),
        name="cond_stats",
    )(qd, far, cond)


def cond_grads_kernel(qd_ref, far_ref, cond_ref, near_ref, mine_ref, their_ref, out_ref, row_ref):
    rows, width = qd_ref.shape
    width = width // 2
    for head in range(width // HEAD_DIM):
        at = [pl.ds(half * width + head * HEAD_DIM, HEAD_DIM) for half in range(2)]
        key, value = cond_ref[:, at[0]], cond_ref[:, at[1]]
        grad_k = 0.0
        grad_v = 0.0
        for side, ref in enumerate((qd_ref, far_ref)):
            near = near_ref if side == 0 else their_ref.at[0]
            parts = [
                [r[pl.ds(3 * head + i, 1), :] for i in range(3)]
                for r in (near, mine_ref.at[side], their_ref.at[2 - side])
            ]
            top = functools.reduce(jnp.maximum, [p[0] for p in parts])
            total = sum(p[1] * jnp.exp2(p[0] - top) for p in parts)
            weighted = sum(p[2] * jnp.exp2(p[0] - top) for p in parts)
            level = top + jnp.log2(total)
            delta = weighted / total
            if side == 0:
                row_ref[pl.ds(2 * head, 1), :] = level
                row_ref[pl.ds(2 * head + 1, 1), :] = delta
            q, d = ref[:, at[0]], ref[:, at[1]]
            p = jnp.exp2(dot(key, q, NT) * (SCALE * LOG2E) - level)
            g = dot(value, d, NT)
            grad_s = (p * (g - delta)).astype(jnp.bfloat16)
            grad_k = grad_k + dot(grad_s, q)
            grad_v = grad_v + dot(p.astype(jnp.bfloat16), d)
        out_ref[:, at[0]] = (grad_k * SCALE).astype(out_ref.dtype)
        out_ref[:, at[1]] = grad_v.astype(out_ref.dtype)


def cond_grads(qd, far, cond, near, mine, theirs):
    rows, width = qd.shape
    heads = width // 2 // HEAD_DIM
    return pl.pallas_call(
        cond_grads_kernel,
        out_shape=(
            jax.ShapeDtypeStruct(cond.shape, jnp.bfloat16),
            jax.ShapeDtypeStruct((STAT_ROWS, rows), jnp.float32),
        ),
        in_specs=[VMEM] * 6,
        out_specs=(VMEM, VMEM),
        compiler_params=params(),
        cost_estimate=cost(2 * rows, cond.shape[0], heads, 4, 8 * qd.size),
        name="cond_grads",
    )(qd, far, cond, near, mine, theirs)


def head_pass(key, value, q, d, level, delta, bias=None):
    s = dot(key, q, NT) * (SCALE * LOG2E)
    if bias is not None:
        s = s + bias
    p = jnp.exp2(s - level)
    grad_s = (p * (dot(value, d, NT) - delta)).astype(jnp.bfloat16)
    return p.astype(jnp.bfloat16), grad_s


def face_kernel(mask_ref, qd_ref, row_ref, lower_ref, upper_ref, down_ref, up_ref, sum_ref):
    width = qd_ref.shape[1] // 2
    biases = face_bias(mask_ref)
    for head in range(width // HEAD_DIM):
        at = [pl.ds(half * width + head * HEAD_DIM, HEAD_DIM) for half in range(2)]
        q, d = qd_ref[:, at[0]], qd_ref[:, at[1]]
        level, delta = [row_ref[pl.ds(2 * head + i, 1), :] for i in range(2)]
        att = 0.0
        grad_q = 0.0
        for ref, out, bias in zip((lower_ref, upper_ref), (down_ref, up_ref), biases):
            key, value = ref[:, at[0]], ref[:, at[1]]
            p, grad_s = head_pass(key, value, q, d, level, delta, bias)
            out[:, at[0]] = (dot(grad_s, q) * SCALE).astype(out.dtype)
            out[:, at[1]] = dot(p, d).astype(out.dtype)
            att = att + dot(value, p, TN)
            grad_q = grad_q + dot(key, grad_s, TN)
        sum_ref[at[1], :] = att
        sum_ref[at[0], :] = grad_q


def face_pass(mask, qd, row_stats, lower, upper):
    rows, width = qd.shape
    heads = width // 2 // HEAD_DIM
    face = jax.ShapeDtypeStruct((FACE, width), jnp.bfloat16)
    return pl.pallas_call(
        face_kernel,
        out_shape=(face, face, jax.ShapeDtypeStruct((width, rows), jnp.float32)),
        in_specs=[SMEM] + [VMEM] * 4,
        out_specs=(VMEM,) * 3,
        compiler_params=params(),
        cost_estimate=cost(rows, 2 * FACE, heads, 6, 10 * qd.size),
        name="face_pass",
    )(mask, qd, row_stats, lower, upper)


def own_kernel(qd_ref, row_ref, own_ref, cond_ref, far_ref, sum_ref, att_ref, dq_ref, keep_ref):
    width = qd_ref.shape[1] // 2
    for head in range(width // HEAD_DIM):
        at = [pl.ds(half * width + head * HEAD_DIM, HEAD_DIM) for half in range(2)]
        q, d = qd_ref[:, at[0]], qd_ref[:, at[1]]
        level, delta = [row_ref[pl.ds(2 * head + i, 1), :] for i in range(2)]
        att = sum_ref[at[1], :]
        grad_q = sum_ref[at[0], :]
        for ref in (own_ref, cond_ref, far_ref):
            key, value = ref[:, at[0]], ref[:, at[1]]
            p, grad_s = head_pass(key, value, q, d, level, delta)
            if ref is own_ref:
                keep_ref[:, at[0]] = dot(grad_s, q) * SCALE
                keep_ref[:, at[1]] = dot(p, d)
            att = att + dot(value, p, TN)
            grad_q = grad_q + dot(key, grad_s, TN)
        att_ref[:, at[0]] = att.T.astype(jnp.bfloat16)
        dq_ref[:, at[0]] = (grad_q * SCALE).T.astype(jnp.bfloat16)


def own_pass(qd, row_stats, own, cond, far_cond, sums):
    rows, width = qd.shape
    heads = width // 2 // HEAD_DIM
    keys = rows + 2 * cond.shape[0]
    half = jax.ShapeDtypeStruct((rows, width // 2), jnp.bfloat16)
    return pl.pallas_call(
        own_kernel,
        out_shape=(half, half, jax.ShapeDtypeStruct((rows, width), jnp.float32)),
        in_specs=[VMEM] * 6,
        out_specs=(VMEM,) * 3,
        compiler_params=params(),
        cost_estimate=cost(rows, keys, heads, 5, 16 * qd.size),
        name="own_pass",
    )(qd, row_stats, own, cond, far_cond, sums)


def per_device(queries, keys_values, cond_kv, face_mask, d_out):
    size = lax.axis_size("tile")
    rows, width = queries.shape
    chips = size // CORES
    cond_rows = cond_kv.shape[0]
    swap = other_core(size)
    up = [(i, i + 1) for i in range(size - 1)]
    down = [(i + 1, i) for i in range(size - 1)]

    copies = spread(cond_kv, chips)
    cond = lax.all_to_all(copies, "tile", 0, 0, axis_index_groups=same_core(size), tiled=True)
    cond = cond.reshape(chips * cond_rows, 2 * width)

    qd = jnp.concatenate([queries, d_out], axis=1)
    own = keys_values.reshape(rows, 2 * width)
    far = lax.ppermute(qd, "tile", swap)
    lower = lax.ppermute(own[rows - FACE :], "tile", up)
    upper = lax.ppermute(own[:FACE], "tile", down)
    near = near_stats(face_mask, qd, own, lower, upper)

    mine = cond_stats(qd, far, cond)
    theirs = lax.ppermute(jnp.concatenate([near[None], mine], axis=0), "tile", swap)
    grads, row_stats = cond_grads(qd, far, cond, near, mine, theirs)
    blocks = grads.reshape(chips, cond_rows, 2 * width)
    parts = lax.all_to_all(blocks, "tile", 0, 0, axis_index_groups=same_core(size), tiled=True)
    grad_cond = total(parts)

    late_cond, row_stats = lax.optimization_barrier((cond, row_stats))
    far_cond = lax.ppermute(late_cond, "tile", swap)
    to_prev, to_next, sums = face_pass(face_mask, qd, row_stats, lower, upper)
    from_next = lax.ppermute(to_prev, "tile", down).astype(jnp.float32)
    from_prev = lax.ppermute(to_next, "tile", up).astype(jnp.float32)
    attended, grad_q, keep = own_pass(qd, row_stats, own, cond, far_cond, sums)
    keep = keep + jnp.concatenate([from_prev, from_next], axis=0)
    grad_kv = keep.astype(jnp.bfloat16).reshape(rows, 2, width)
    return attended, grad_q, grad_kv, grad_cond


def solution(mesh):
    return jax.shard_map(
        per_device,
        mesh=mesh,
        in_specs=(
            P("tile", "head"),
            P("tile", None, "head"),
            P("tile", None, "head"),
            P("tile", None),
            P("tile", "head"),
        ),
        out_specs=(
            P("tile", "head"),
            P("tile", "head"),
            P("tile", None, "head"),
            P("tile", None, "head"),
        ),
        check_vma=False,
    )
```

```python
import functools

import jax
import jax.numpy as jnp
from jax import lax
from jax.experimental import pallas as pl
from jax.experimental.pallas import tpu as pltpu
from jax.sharding import PartitionSpec as P

HEAD_DIM = 128
FACE = 128
CORES = 2
RUN = 4
SCALE = HEAD_DIM**-0.5
LOG2E = 1.4426950408889634
NEG_LARGE = -1e30
STAT_ROWS = 16

NT = (((1,), (1,)), ((), ()))
TN = (((0,), (0,)), ((), ()))


def dot(a, b, dims=(((1,), (0,)), ((), ()))):
    return lax.dot_general(a, b, dims, preferred_element_type=jnp.float32)


def other_core(size):
    return [(t, t ^ 1) for t in range(size)]


def run_groups(size):
    step = RUN * CORES
    along_y = [list(range(z + c, z + step, CORES)) for z in range(0, size, step) for c in range(CORES)]
    along_z = [list(range(first, size, step)) for first in range(step)]
    return along_y, along_z


def params(mib=48):
    return pltpu.CompilerParams(vmem_limit_bytes=mib * 1024 * 1024)


VMEM = pl.BlockSpec(memory_space=pltpu.VMEM)
SMEM = pl.BlockSpec(memory_space=pltpu.SMEM)


def cost(queries, keys, heads, products, size):
    return pl.CostEstimate(
        flops=2 * products * heads * queries * keys * HEAD_DIM,
        bytes_accessed=size,
        transcendentals=heads * queries * keys,
    )


def face_bias(mask_ref):
    tile = lax.axis_index("tile")
    last = lax.axis_size("tile") - 1
    lower = jnp.where((mask_ref[0, 0] == 1) & (tile > 0), 0.0, NEG_LARGE)
    upper = jnp.where((mask_ref[0, 1] == 1) & (tile < last), 0.0, NEG_LARGE)
    return lower.astype(jnp.float32), upper.astype(jnp.float32)


def raised_stats(scores, grads):
    top = functools.reduce(jnp.maximum, [jnp.max(s, axis=0, keepdims=True) for s in scores])
    total = 0.0
    weighted = 0.0
    for s, g in zip(scores, grads):
        e = jnp.exp2(s - top)
        total = total + jnp.sum(e, axis=0, keepdims=True)
        weighted = weighted + jnp.sum(e * g, axis=0, keepdims=True)
    return top, total, weighted


def near_stats_kernel(mask_ref, qd_ref, own_ref, lower_ref, upper_ref, stat_ref):
    width = qd_ref.shape[1] // 2
    lower_bias, upper_bias = face_bias(mask_ref)
    for head in range(width // HEAD_DIM):
        at = [pl.ds(half * width + head * HEAD_DIM, HEAD_DIM) for half in range(2)]
        q, d = qd_ref[:, at[0]], qd_ref[:, at[1]]
        scores, grads = [], []
        for ref, bias in ((lower_ref, lower_bias), (own_ref, None), (upper_ref, upper_bias)):
            s = dot(ref[:, at[0]], q, NT) * (SCALE * LOG2E)
            scores.append(s if bias is None else s + bias)
            grads.append(dot(ref[:, at[1]], d, NT))
        for i, row in enumerate(raised_stats(scores, grads)):
            stat_ref[pl.ds(3 * head + i, 1), :] = row


def near_stats(mask, qd, own, lower, upper):
    rows, width = qd.shape
    heads = width // 2 // HEAD_DIM
    return pl.pallas_call(
        near_stats_kernel,
        out_shape=jax.ShapeDtypeStruct((STAT_ROWS, rows), jnp.float32),
        in_specs=[SMEM, VMEM, VMEM, VMEM, VMEM],
        out_specs=VMEM,
        compiler_params=params(),
        cost_estimate=cost(rows, rows + 2 * FACE, heads, 2, 5 * qd.size),
        name="near_stats",
    )(mask, qd, own, lower, upper)


def cond_stats_kernel(qd_ref, far_ref, cond_ref, stat_ref):
    rows, width = qd_ref.shape
    width = width // 2
    for head in range(width // HEAD_DIM):
        at = [pl.ds(half * width + head * HEAD_DIM, HEAD_DIM) for half in range(2)]
        key, value = cond_ref[:, at[0]], cond_ref[:, at[1]]
        for side, ref in enumerate((qd_ref, far_ref)):
            s = dot(key, ref[:, at[0]], NT) * (SCALE * LOG2E)
            g = dot(value, ref[:, at[1]], NT)
            for i, row in enumerate(raised_stats([s], [g])):
                stat_ref[side, pl.ds(3 * head + i, 1), :] = row


def cond_stats(qd, far, cond):
    rows, width = qd.shape
    heads = width // 2 // HEAD_DIM
    return pl.pallas_call(
        cond_stats_kernel,
        out_shape=jax.ShapeDtypeStruct((2, STAT_ROWS, rows), jnp.float32),
        in_specs=[VMEM, VMEM, VMEM],
        out_specs=VMEM,
        compiler_params=params(),
        cost_estimate=cost(2 * rows, cond.shape[0], heads, 2, 6 * qd.size),
        name="cond_stats",
    )(qd, far, cond)


def cond_grads_kernel(qd_ref, far_ref, cond_ref, near_ref, mine_ref, their_ref, out_ref, row_ref):
    rows, width = qd_ref.shape
    width = width // 2
    for head in range(width // HEAD_DIM):
        at = [pl.ds(half * width + head * HEAD_DIM, HEAD_DIM) for half in range(2)]
        key, value = cond_ref[:, at[0]], cond_ref[:, at[1]]
        grad_k = 0.0
        grad_v = 0.0
        for side, ref in enumerate((qd_ref, far_ref)):
            near = near_ref if side == 0 else their_ref.at[0]
            parts = [
                [r[pl.ds(3 * head + i, 1), :] for i in range(3)]
                for r in (near, mine_ref.at[side], their_ref.at[2 - side])
            ]
            top = functools.reduce(jnp.maximum, [p[0] for p in parts])
            total = sum(p[1] * jnp.exp2(p[0] - top) for p in parts)
            weighted = sum(p[2] * jnp.exp2(p[0] - top) for p in parts)
            level = top + jnp.log2(total)
            delta = weighted / total
            if side == 0:
                row_ref[pl.ds(2 * head, 1), :] = level
                row_ref[pl.ds(2 * head + 1, 1), :] = delta
            q, d = ref[:, at[0]], ref[:, at[1]]
            p = jnp.exp2(dot(key, q, NT) * (SCALE * LOG2E) - level)
            g = dot(value, d, NT)
            grad_s = (p * (g - delta)).astype(jnp.bfloat16)
            grad_k = grad_k + dot(grad_s, q)
            grad_v = grad_v + dot(p.astype(jnp.bfloat16), d)
        out_ref[:, at[0]] = (grad_k * SCALE).astype(out_ref.dtype)
        out_ref[:, at[1]] = grad_v.astype(out_ref.dtype)


def cond_grads(qd, far, cond, near, mine, theirs):
    rows, width = qd.shape
    heads = width // 2 // HEAD_DIM
    return pl.pallas_call(
        cond_grads_kernel,
        out_shape=(
            jax.ShapeDtypeStruct(cond.shape, jnp.bfloat16),
            jax.ShapeDtypeStruct((STAT_ROWS, rows), jnp.float32),
        ),
        in_specs=[VMEM] * 6,
        out_specs=(VMEM, VMEM),
        compiler_params=params(),
        cost_estimate=cost(2 * rows, cond.shape[0], heads, 4, 8 * qd.size),
        name="cond_grads",
    )(qd, far, cond, near, mine, theirs)


def head_pass(key, value, q, d, level, delta, bias=None):
    s = dot(key, q, NT) * (SCALE * LOG2E)
    if bias is not None:
        s = s + bias
    p = jnp.exp2(s - level)
    grad_s = (p * (dot(value, d, NT) - delta)).astype(jnp.bfloat16)
    return p.astype(jnp.bfloat16), grad_s


def face_kernel(mask_ref, qd_ref, row_ref, lower_ref, upper_ref, down_ref, up_ref, sum_ref):
    width = qd_ref.shape[1] // 2
    biases = face_bias(mask_ref)
    for head in range(width // HEAD_DIM):
        at = [pl.ds(half * width + head * HEAD_DIM, HEAD_DIM) for half in range(2)]
        q, d = qd_ref[:, at[0]], qd_ref[:, at[1]]
        level, delta = [row_ref[pl.ds(2 * head + i, 1), :] for i in range(2)]
        att = 0.0
        grad_q = 0.0
        for ref, out, bias in zip((lower_ref, upper_ref), (down_ref, up_ref), biases):
            key, value = ref[:, at[0]], ref[:, at[1]]
            p, grad_s = head_pass(key, value, q, d, level, delta, bias)
            out[:, at[0]] = (dot(grad_s, q) * SCALE).astype(out.dtype)
            out[:, at[1]] = dot(p, d).astype(out.dtype)
            att = att + dot(value, p, TN)
            grad_q = grad_q + dot(key, grad_s, TN)
        sum_ref[at[1], :] = att
        sum_ref[at[0], :] = grad_q


def face_pass(mask, qd, row_stats, lower, upper):
    rows, width = qd.shape
    heads = width // 2 // HEAD_DIM
    face = jax.ShapeDtypeStruct((FACE, width), jnp.bfloat16)
    return pl.pallas_call(
        face_kernel,
        out_shape=(face, face, jax.ShapeDtypeStruct((width, rows), jnp.float32)),
        in_specs=[SMEM] + [VMEM] * 4,
        out_specs=(VMEM,) * 3,
        compiler_params=params(),
        cost_estimate=cost(rows, 2 * FACE, heads, 6, 10 * qd.size),
        name="face_pass",
    )(mask, qd, row_stats, lower, upper)


def own_kernel(qd_ref, row_ref, own_ref, cond_ref, far_ref, sum_ref, att_ref, dq_ref, keep_ref):
    width = qd_ref.shape[1] // 2
    for head in range(width // HEAD_DIM):
        at = [pl.ds(half * width + head * HEAD_DIM, HEAD_DIM) for half in range(2)]
        q, d = qd_ref[:, at[0]], qd_ref[:, at[1]]
        level, delta = [row_ref[pl.ds(2 * head + i, 1), :] for i in range(2)]
        att = sum_ref[at[1], :]
        grad_q = sum_ref[at[0], :]
        for ref in (own_ref, cond_ref, far_ref):
            key, value = ref[:, at[0]], ref[:, at[1]]
            p, grad_s = head_pass(key, value, q, d, level, delta)
            if ref is own_ref:
                keep_ref[:, at[0]] = dot(grad_s, q) * SCALE
                keep_ref[:, at[1]] = dot(p, d)
            att = att + dot(value, p, TN)
            grad_q = grad_q + dot(key, grad_s, TN)
        att_ref[:, at[0]] = att.T.astype(jnp.bfloat16)
        dq_ref[:, at[0]] = (grad_q * SCALE).T.astype(jnp.bfloat16)


def own_pass(qd, row_stats, own, cond, far_cond, sums):
    rows, width = qd.shape
    heads = width // 2 // HEAD_DIM
    keys = rows + 2 * cond.shape[0]
    half = jax.ShapeDtypeStruct((rows, width // 2), jnp.bfloat16)
    return pl.pallas_call(
        own_kernel,
        out_shape=(half, half, jax.ShapeDtypeStruct((rows, width), jnp.float32)),
        in_specs=[VMEM] * 6,
        out_specs=(VMEM,) * 3,
        compiler_params=params(),
        cost_estimate=cost(rows, keys, heads, 5, 16 * qd.size),
        name="own_pass",
    )(qd, row_stats, own, cond, far_cond, sums)


def per_device(queries, keys_values, cond_kv, face_mask, d_out):
    size = lax.axis_size("tile")
    rows, width = queries.shape
    cond_rows = cond_kv.shape[0]
    swap = other_core(size)
    up = [(i, i + 1) for i in range(size - 1)]
    down = [(i + 1, i) for i in range(size - 1)]

    along_y, along_z = run_groups(size)
    copies = jnp.broadcast_to(cond_kv[None], (RUN,) + cond_kv.shape)
    run = lax.all_to_all(copies, "tile", 0, 0, axis_index_groups=along_y, tiled=True)
    run = run.reshape(RUN * cond_rows, 2 * width)
    cond = lax.all_gather(run, "tile", axis=0, axis_index_groups=along_z, tiled=True)

    qd = jnp.concatenate([queries, d_out], axis=1)
    own = keys_values.reshape(rows, 2 * width)
    far = lax.ppermute(qd, "tile", swap)
    lower = lax.ppermute(own[rows - FACE :], "tile", up)
    upper = lax.ppermute(own[:FACE], "tile", down)
    near = near_stats(face_mask, qd, own, lower, upper)

    mine = cond_stats(qd, far, cond)
    theirs = lax.ppermute(jnp.concatenate([near[None], mine], axis=0), "tile", swap)
    grads, row_stats = cond_grads(qd, far, cond, near, mine, theirs)
    grads = lax.psum_scatter(
        grads, "tile", scatter_dimension=0, axis_index_groups=along_z, tiled=True
    )
    blocks = grads.reshape(RUN, cond_rows, 2, width)
    parts = lax.all_to_all(blocks, "tile", 0, 0, axis_index_groups=along_y, tiled=True)
    grad_cond = jnp.sum(parts.astype(jnp.float32), axis=0)

    late_cond, row_stats = lax.optimization_barrier((cond, row_stats))
    far_cond = lax.ppermute(late_cond, "tile", swap)
    to_prev, to_next, sums = face_pass(face_mask, qd, row_stats, lower, upper)
    from_next = lax.ppermute(to_prev, "tile", down).astype(jnp.float32)
    from_prev = lax.ppermute(to_next, "tile", up).astype(jnp.float32)
    attended, grad_q, keep = own_pass(qd, row_stats, own, cond, far_cond, sums)
    keep = keep + jnp.concatenate([from_prev, from_next], axis=0)
    grad_kv = keep.astype(jnp.bfloat16).reshape(rows, 2, width)
    return attended, grad_q, grad_kv, grad_cond


def solution(mesh):
    return jax.shard_map(
        per_device,
        mesh=mesh,
        in_specs=(
            P("tile", "head"),
            P("tile", None, "head"),
            P("tile", None, "head"),
            P("tile", None),
            P("tile", "head"),
        ),
        out_specs=(
            P("tile", "head"),
            P("tile", "head"),
            P("tile", None, "head"),
            P("tile", None, "head"),
        ),
        check_vma=False,
    )
```

```python
import functools

import jax
import jax.numpy as jnp
from jax import lax
from jax.experimental import pallas as pl
from jax.experimental.pallas import tpu as pltpu
from jax.sharding import PartitionSpec as P

HEAD_DIM = 128
FACE = 128
CORES = 2
RUN = 4
SCALE = HEAD_DIM**-0.5
LOG2E = 1.4426950408889634
NEG_LARGE = -1e30
STAT_ROWS = 16

NT = (((1,), (1,)), ((), ()))
TN = (((0,), (0,)), ((), ()))


def dot(a, b, dims=(((1,), (0,)), ((), ()))):
    return lax.dot_general(a, b, dims, preferred_element_type=jnp.float32)


def other_core(size):
    return [(t, t ^ 1) for t in range(size)]


def run_groups(size):
    step = RUN * CORES
    along_y = [list(range(z + c, z + step, CORES)) for z in range(0, size, step) for c in range(CORES)]
    along_z = [list(range(first, size, step)) for first in range(step)]
    return along_y, along_z


def params(mib=48):
    return pltpu.CompilerParams(vmem_limit_bytes=mib * 1024 * 1024)


VMEM = pl.BlockSpec(memory_space=pltpu.VMEM)
SMEM = pl.BlockSpec(memory_space=pltpu.SMEM)


def cost(queries, keys, heads, products, size):
    return pl.CostEstimate(
        flops=2 * products * heads * queries * keys * HEAD_DIM,
        bytes_accessed=size,
        transcendentals=heads * queries * keys,
    )


def face_bias(mask_ref):
    tile = lax.axis_index("tile")
    last = lax.axis_size("tile") - 1
    lower = jnp.where((mask_ref[0, 0] == 1) & (tile > 0), 0.0, NEG_LARGE)
    upper = jnp.where((mask_ref[0, 1] == 1) & (tile < last), 0.0, NEG_LARGE)
    return lower.astype(jnp.float32), upper.astype(jnp.float32)


def raised_stats(scores, grads):
    top = functools.reduce(jnp.maximum, [jnp.max(s, axis=0, keepdims=True) for s in scores])
    total = 0.0
    weighted = 0.0
    for s, g in zip(scores, grads):
        e = jnp.exp2(s - top)
        total = total + jnp.sum(e, axis=0, keepdims=True)
        weighted = weighted + jnp.sum(e * g, axis=0, keepdims=True)
    return top, total, weighted


def near_stats_kernel(mask_ref, qd_ref, own_ref, lower_ref, upper_ref, stat_ref):
    width = qd_ref.shape[1] // 2
    lower_bias, upper_bias = face_bias(mask_ref)
    for head in range(width // HEAD_DIM):
        at = [pl.ds(half * width + head * HEAD_DIM, HEAD_DIM) for half in range(2)]
        q, d = qd_ref[:, at[0]], qd_ref[:, at[1]]
        scores, grads = [], []
        for ref, bias in ((lower_ref, lower_bias), (own_ref, None), (upper_ref, upper_bias)):
            s = dot(ref[:, at[0]], q, NT) * (SCALE * LOG2E)
            scores.append(s if bias is None else s + bias)
            grads.append(dot(ref[:, at[1]], d, NT))
        for i, row in enumerate(raised_stats(scores, grads)):
            stat_ref[pl.ds(3 * head + i, 1), :] = row


def near_stats(mask, qd, own, lower, upper):
    rows, width = qd.shape
    heads = width // 2 // HEAD_DIM
    return pl.pallas_call(
        near_stats_kernel,
        out_shape=jax.ShapeDtypeStruct((STAT_ROWS, rows), jnp.float32),
        in_specs=[SMEM, VMEM, VMEM, VMEM, VMEM],
        out_specs=VMEM,
        compiler_params=params(),
        cost_estimate=cost(rows, rows + 2 * FACE, heads, 2, 5 * qd.size),
        name="near_stats",
    )(mask, qd, own, lower, upper)


def cond_stats_kernel(qd_ref, far_ref, cond_ref, stat_ref):
    rows, width = qd_ref.shape
    width = width // 2
    for head in range(width // HEAD_DIM):
        at = [pl.ds(half * width + head * HEAD_DIM, HEAD_DIM) for half in range(2)]
        key, value = cond_ref[:, at[0]], cond_ref[:, at[1]]
        for side, ref in enumerate((qd_ref, far_ref)):
            s = dot(key, ref[:, at[0]], NT) * (SCALE * LOG2E)
            g = dot(value, ref[:, at[1]], NT)
            for i, row in enumerate(raised_stats([s], [g])):
                stat_ref[side, pl.ds(3 * head + i, 1), :] = row


def cond_stats(qd, far, cond):
    rows, width = qd.shape
    heads = width // 2 // HEAD_DIM
    return pl.pallas_call(
        cond_stats_kernel,
        out_shape=jax.ShapeDtypeStruct((2, STAT_ROWS, rows), jnp.float32),
        in_specs=[VMEM, VMEM, VMEM],
        out_specs=VMEM,
        compiler_params=params(),
        cost_estimate=cost(2 * rows, cond.shape[0], heads, 2, 6 * qd.size),
        name="cond_stats",
    )(qd, far, cond)


def cond_grads_kernel(qd_ref, far_ref, cond_ref, near_ref, mine_ref, their_ref, out_ref, row_ref):
    rows, width = qd_ref.shape
    width = width // 2
    for head in range(width // HEAD_DIM):
        at = [pl.ds(half * width + head * HEAD_DIM, HEAD_DIM) for half in range(2)]
        key, value = cond_ref[:, at[0]], cond_ref[:, at[1]]
        grad_k = 0.0
        grad_v = 0.0
        for side, ref in enumerate((qd_ref, far_ref)):
            near = near_ref if side == 0 else their_ref.at[0]
            parts = [
                [r[pl.ds(3 * head + i, 1), :] for i in range(3)]
                for r in (near, mine_ref.at[side], their_ref.at[2 - side])
            ]
            top = functools.reduce(jnp.maximum, [p[0] for p in parts])
            total = sum(p[1] * jnp.exp2(p[0] - top) for p in parts)
            weighted = sum(p[2] * jnp.exp2(p[0] - top) for p in parts)
            level = top + jnp.log2(total)
            delta = weighted / total
            if side == 0:
                row_ref[pl.ds(2 * head, 1), :] = level
                row_ref[pl.ds(2 * head + 1, 1), :] = delta
            q, d = ref[:, at[0]], ref[:, at[1]]
            p = jnp.exp2(dot(key, q, NT) * (SCALE * LOG2E) - level)
            g = dot(value, d, NT)
            grad_s = (p * (g - delta)).astype(jnp.bfloat16)
            grad_k = grad_k + dot(grad_s, q)
            grad_v = grad_v + dot(p.astype(jnp.bfloat16), d)
        out_ref[:, at[0]] = (grad_k * SCALE).astype(out_ref.dtype)
        out_ref[:, at[1]] = grad_v.astype(out_ref.dtype)


def cond_grads(qd, far, cond, near, mine, theirs):
    rows, width = qd.shape
    heads = width // 2 // HEAD_DIM
    return pl.pallas_call(
        cond_grads_kernel,
        out_shape=(
            jax.ShapeDtypeStruct(cond.shape, jnp.bfloat16),
            jax.ShapeDtypeStruct((STAT_ROWS, rows), jnp.float32),
        ),
        in_specs=[VMEM] * 6,
        out_specs=(VMEM, VMEM),
        compiler_params=params(),
        cost_estimate=cost(2 * rows, cond.shape[0], heads, 4, 8 * qd.size),
        name="cond_grads",
    )(qd, far, cond, near, mine, theirs)


def head_pass(key, value, q, d, level, delta, bias=None):
    s = dot(key, q, NT) * (SCALE * LOG2E)
    if bias is not None:
        s = s + bias
    p = jnp.exp2(s - level)
    grad_s = (p * (dot(value, d, NT) - delta)).astype(jnp.bfloat16)
    return p.astype(jnp.bfloat16), grad_s


def face_kernel(mask_ref, qd_ref, row_ref, lower_ref, upper_ref, down_ref, up_ref, sum_ref):
    width = qd_ref.shape[1] // 2
    biases = face_bias(mask_ref)
    for head in range(width // HEAD_DIM):
        at = [pl.ds(half * width + head * HEAD_DIM, HEAD_DIM) for half in range(2)]
        q, d = qd_ref[:, at[0]], qd_ref[:, at[1]]
        level, delta = [row_ref[pl.ds(2 * head + i, 1), :] for i in range(2)]
        att = 0.0
        grad_q = 0.0
        for ref, out, bias in zip((lower_ref, upper_ref), (down_ref, up_ref), biases):
            key, value = ref[:, at[0]], ref[:, at[1]]
            p, grad_s = head_pass(key, value, q, d, level, delta, bias)
            out[:, at[0]] = (dot(grad_s, q) * SCALE).astype(out.dtype)
            out[:, at[1]] = dot(p, d).astype(out.dtype)
            att = att + dot(value, p, TN)
            grad_q = grad_q + dot(key, grad_s, TN)
        sum_ref[at[1], :] = att
        sum_ref[at[0], :] = grad_q


def face_pass(mask, qd, row_stats, lower, upper):
    rows, width = qd.shape
    heads = width // 2 // HEAD_DIM
    face = jax.ShapeDtypeStruct((FACE, width), jnp.bfloat16)
    return pl.pallas_call(
        face_kernel,
        out_shape=(face, face, jax.ShapeDtypeStruct((width, rows), jnp.float32)),
        in_specs=[SMEM] + [VMEM] * 4,
        out_specs=(VMEM,) * 3,
        compiler_params=params(),
        cost_estimate=cost(rows, 2 * FACE, heads, 6, 10 * qd.size),
        name="face_pass",
    )(mask, qd, row_stats, lower, upper)


def own_kernel(qd_ref, row_ref, own_ref, cond_ref, far_ref, sum_ref, att_ref, dq_ref, keep_ref):
    width = qd_ref.shape[1] // 2
    for head in range(width // HEAD_DIM):
        at = [pl.ds(half * width + head * HEAD_DIM, HEAD_DIM) for half in range(2)]
        q, d = qd_ref[:, at[0]], qd_ref[:, at[1]]
        level, delta = [row_ref[pl.ds(2 * head + i, 1), :] for i in range(2)]
        att = sum_ref[at[1], :]
        grad_q = sum_ref[at[0], :]
        for ref in (own_ref, cond_ref, far_ref):
            key, value = ref[:, at[0]], ref[:, at[1]]
            p, grad_s = head_pass(key, value, q, d, level, delta)
            if ref is own_ref:
                keep_ref[:, at[0]] = dot(grad_s, q) * SCALE
                keep_ref[:, at[1]] = dot(p, d)
            att = att + dot(value, p, TN)
            grad_q = grad_q + dot(key, grad_s, TN)
        att_ref[:, at[0]] = att.T.astype(jnp.bfloat16)
        dq_ref[:, at[0]] = (grad_q * SCALE).T.astype(jnp.bfloat16)


def own_pass(qd, row_stats, own, cond, far_cond, sums):
    rows, width = qd.shape
    heads = width // 2 // HEAD_DIM
    keys = rows + 2 * cond.shape[0]
    half = jax.ShapeDtypeStruct((rows, width // 2), jnp.bfloat16)
    return pl.pallas_call(
        own_kernel,
        out_shape=(half, half, jax.ShapeDtypeStruct((rows, width), jnp.float32)),
        in_specs=[VMEM] * 6,
        out_specs=(VMEM,) * 3,
        compiler_params=params(),
        cost_estimate=cost(rows, keys, heads, 5, 16 * qd.size),
        name="own_pass",
    )(qd, row_stats, own, cond, far_cond, sums)


def per_device(queries, keys_values, cond_kv, face_mask, d_out):
    size = lax.axis_size("tile")
    rows, width = queries.shape
    cond_rows = cond_kv.shape[0]
    swap = other_core(size)
    up = [(i, i + 1) for i in range(size - 1)]
    down = [(i + 1, i) for i in range(size - 1)]

    along_y, along_z = run_groups(size)
    copies = jnp.broadcast_to(cond_kv[None], (RUN,) + cond_kv.shape)
    run = lax.all_to_all(copies, "tile", 0, 0, axis_index_groups=along_y, tiled=True)
    run = run.reshape(RUN * cond_rows, 2 * width)
    depth = size // (RUN * CORES)
    copies = jnp.broadcast_to(run[None], (depth,) + run.shape)
    cond = lax.all_to_all(copies, "tile", 0, 0, axis_index_groups=along_z, tiled=True)
    cond = cond.reshape(depth * RUN * cond_rows, 2 * width)

    qd = jnp.concatenate([queries, d_out], axis=1)
    own = keys_values.reshape(rows, 2 * width)
    far = lax.ppermute(qd, "tile", swap)
    lower = lax.ppermute(own[rows - FACE :], "tile", up)
    upper = lax.ppermute(own[:FACE], "tile", down)
    near = near_stats(face_mask, qd, own, lower, upper)

    mine = cond_stats(qd, far, cond)
    theirs = lax.ppermute(jnp.concatenate([near[None], mine], axis=0), "tile", swap)
    grads, row_stats = cond_grads(qd, far, cond, near, mine, theirs)
    blocks = grads.reshape(depth, RUN * cond_rows, 2 * width)
    parts = lax.all_to_all(blocks, "tile", 0, 0, axis_index_groups=along_z, tiled=True)
    grads = jnp.sum(parts.astype(jnp.float32), axis=0).astype(jnp.bfloat16)
    blocks = grads.reshape(RUN, cond_rows, 2, width)
    parts = lax.all_to_all(blocks, "tile", 0, 0, axis_index_groups=along_y, tiled=True)
    grad_cond = jnp.sum(parts.astype(jnp.float32), axis=0)

    late_cond, row_stats = lax.optimization_barrier((cond, row_stats))
    far_cond = lax.ppermute(late_cond, "tile", swap)
    to_prev, to_next, sums = face_pass(face_mask, qd, row_stats, lower, upper)
    from_next = lax.ppermute(to_prev, "tile", down).astype(jnp.float32)
    from_prev = lax.ppermute(to_next, "tile", up).astype(jnp.float32)
    attended, grad_q, keep = own_pass(qd, row_stats, own, cond, far_cond, sums)
    keep = keep + jnp.concatenate([from_prev, from_next], axis=0)
    grad_kv = keep.astype(jnp.bfloat16).reshape(rows, 2, width)
    return attended, grad_q, grad_kv, grad_cond


def solution(mesh):
    return jax.shard_map(
        per_device,
        mesh=mesh,
        in_specs=(
            P("tile", "head"),
            P("tile", None, "head"),
            P("tile", None, "head"),
            P("tile", None),
            P("tile", "head"),
        ),
        out_specs=(
            P("tile", "head"),
            P("tile", "head"),
            P("tile", None, "head"),
            P("tile", None, "head"),
        ),
        check_vma=False,
    )
```

```python
import functools

import jax
import jax.numpy as jnp
from jax import lax
from jax.experimental import pallas as pl
from jax.experimental.pallas import tpu as pltpu
from jax.sharding import PartitionSpec as P

HEAD_DIM = 128
FACE = 128
CORES = 2
SCALE = HEAD_DIM**-0.5
LOG2E = 1.4426950408889634
NEG_LARGE = -1e30
STAT_ROWS = 16

NT = (((1,), (1,)), ((), ()))
TN = (((0,), (0,)), ((), ()))


def dot(a, b, dims=(((1,), (0,)), ((), ()))):
    return lax.dot_general(a, b, dims, preferred_element_type=jnp.float32)


def other_core(size):
    return [(t, t ^ 1) for t in range(size)]


def same_core(size):
    return [list(range(c, size, CORES)) for c in range(CORES)]


def params(mib=48):
    return pltpu.CompilerParams(vmem_limit_bytes=mib * 1024 * 1024)


VMEM = pl.BlockSpec(memory_space=pltpu.VMEM)
SMEM = pl.BlockSpec(memory_space=pltpu.SMEM)


def spread_kernel(cond_ref, out_ref):
    rows, _, width = cond_ref.shape
    flat = jnp.concatenate([cond_ref[:, 0, :], cond_ref[:, 1, :]], axis=1)
    out_ref[...] = jnp.broadcast_to(flat[None], out_ref.shape)


def spread(cond_kv, copies):
    rows, _, width = cond_kv.shape
    return pl.pallas_call(
        spread_kernel,
        out_shape=jax.ShapeDtypeStruct((copies, rows, 2 * width), cond_kv.dtype),
        in_specs=[VMEM],
        out_specs=VMEM,
        compiler_params=params(),
        name="spread",
    )(cond_kv)


def total_kernel(parts_ref, out_ref):
    width = out_ref.shape[2]
    total = jnp.sum(parts_ref[...].astype(jnp.float32), axis=0)
    out_ref[:, 0, :] = total[:, :width]
    out_ref[:, 1, :] = total[:, width:]


def total(parts):
    _, rows, width = parts.shape
    return pl.pallas_call(
        total_kernel,
        out_shape=jax.ShapeDtypeStruct((rows, 2, width // 2), jnp.float32),
        in_specs=[VMEM],
        out_specs=VMEM,
        compiler_params=params(),
        name="total",
    )(parts)


def cost(queries, keys, heads, products, size):
    return pl.CostEstimate(
        flops=2 * products * heads * queries * keys * HEAD_DIM,
        bytes_accessed=size,
        transcendentals=heads * queries * keys,
    )


def face_bias(mask_ref):
    tile = lax.axis_index("tile")
    last = lax.axis_size("tile") - 1
    lower = jnp.where((mask_ref[0, 0] == 1) & (tile > 0), 0.0, NEG_LARGE)
    upper = jnp.where((mask_ref[0, 1] == 1) & (tile < last), 0.0, NEG_LARGE)
    even = tile % CORES == 0
    inner = jnp.where(even, upper, lower)
    outer = jnp.where(even, lower, upper)
    return inner.astype(jnp.float32), outer.astype(jnp.float32)


def columns(head, width):
    return [pl.ds(half * width + head * HEAD_DIM, HEAD_DIM) for half in range(2)]


def raised_stats(scores, grads):
    top = functools.reduce(jnp.maximum, [jnp.max(s, axis=0, keepdims=True) for s in scores])
    total = 0.0
    weighted = 0.0
    for s, g in zip(scores, grads):
        e = jnp.exp2(s - top)
        total = total + jnp.sum(e, axis=0, keepdims=True)
        weighted = weighted + jnp.sum(e * g, axis=0, keepdims=True)
    return top, total, weighted


def near_stats_kernel(mask_ref, pack_ref, own_ref, swap_ref, outer_ref, stat_ref):
    rows = stat_ref.shape[1]
    width = pack_ref.shape[1] // 2
    inner_bias, outer_bias = face_bias(mask_ref)
    for head in range(width // HEAD_DIM):
        at = columns(head, width)
        q, d = pack_ref[:rows, at[0]], pack_ref[:rows, at[1]]
        near = (
            (swap_ref.at[rows:], inner_bias),
            (own_ref, None),
            (outer_ref, outer_bias),
        )
        scores, grads = [], []
        for ref, bias in near:
            s = dot(ref[:, at[0]], q, NT) * (SCALE * LOG2E)
            scores.append(s if bias is None else s + bias)
            grads.append(dot(ref[:, at[1]], d, NT))
        for i, row in enumerate(raised_stats(scores, grads)):
            stat_ref[pl.ds(3 * head + i, 1), :] = row


def near_stats(mask, pack, own, swap, outer):
    rows, width = own.shape
    return pl.pallas_call(
        near_stats_kernel,
        out_shape=jax.ShapeDtypeStruct((STAT_ROWS, rows), jnp.float32),
        in_specs=[SMEM, VMEM, VMEM, VMEM, VMEM],
        out_specs=VMEM,
        compiler_params=params(),
        cost_estimate=pl.CostEstimate(
            flops=30_000_000_000, bytes_accessed=5 * own.size, transcendentals=0
        ),
        name="near_stats",
    )(mask, pack, own, swap, outer)


def cond_stats_kernel(pack_ref, swap_ref, cond_ref, near_ref, stat_ref):
    rows = near_ref.shape[1]
    width = pack_ref.shape[1] // 2
    stat_ref[0] = near_ref[...]
    for head in range(width // HEAD_DIM):
        at = columns(head, width)
        key, value = cond_ref[:, at[0]], cond_ref[:, at[1]]
        for side, ref in enumerate((pack_ref, swap_ref)):
            s = dot(key, ref[:rows, at[0]], NT) * (SCALE * LOG2E)
            g = dot(value, ref[:rows, at[1]], NT)
            for i, row in enumerate(raised_stats([s], [g])):
                stat_ref[1 + side, pl.ds(3 * head + i, 1), :] = row


def cond_stats(pack, swap, cond, near):
    rows = near.shape[1]
    heads = pack.shape[1] // 2 // HEAD_DIM
    return pl.pallas_call(
        cond_stats_kernel,
        out_shape=jax.ShapeDtypeStruct((3, STAT_ROWS, rows), jnp.float32),
        in_specs=[VMEM] * 4,
        out_specs=VMEM,
        compiler_params=params(),
        cost_estimate=cost(2 * rows, cond.shape[0], heads, 2, 6 * pack.size),
        name="cond_stats",
    )(pack, swap, cond, near)


def head_pass(key, value, q, d, level, delta, bias=None):
    s = dot(key, q, NT) * (SCALE * LOG2E)
    if bias is not None:
        s = s + bias
    p = jnp.exp2(s - level)
    grad_s = (p * (dot(value, d, NT) - delta)).astype(jnp.bfloat16)
    return p.astype(jnp.bfloat16), grad_s


def grads_kernel(
    mask_ref, pack_ref, swap_ref, outer_ref, cond_ref, mine_ref, their_ref,
    out_ref, outer_out_ref, back_ref, row_ref,
):
    rows = row_ref.shape[1]
    width = pack_ref.shape[1] // 2
    cond_rows = cond_ref.shape[0]
    inner_bias, outer_bias = face_bias(mask_ref)
    back_ref[:cond_rows, :] = cond_ref[...]
    faces = (
        (swap_ref.at[rows:], inner_bias, back_ref.at[cond_rows:]),
        (outer_ref, outer_bias, outer_out_ref),
    )
    for head in range(width // HEAD_DIM):
        at = columns(head, width)
        key, value = cond_ref[:, at[0]], cond_ref[:, at[1]]
        grad_k = 0.0
        grad_v = 0.0
        for side, ref in enumerate((pack_ref, swap_ref)):
            home, away = (mine_ref, their_ref) if side == 0 else (their_ref, mine_ref)
            parts = [
                [r[pl.ds(3 * head + i, 1), :] for i in range(3)]
                for r in (home.at[0], home.at[1], away.at[2])
            ]
            top = functools.reduce(jnp.maximum, [p[0] for p in parts])
            total = sum(p[1] * jnp.exp2(p[0] - top) for p in parts)
            weighted = sum(p[2] * jnp.exp2(p[0] - top) for p in parts)
            level = top + jnp.log2(total)
            delta = weighted / total
            q, d = ref[:rows, at[0]], ref[:rows, at[1]]
            p, grad_s = head_pass(key, value, q, d, level, delta)
            grad_k = grad_k + dot(grad_s, q)
            grad_v = grad_v + dot(p, d)
            if side == 0:
                row_ref[pl.ds(2 * head, 1), :] = level
                row_ref[pl.ds(2 * head + 1, 1), :] = delta
                for face, bias, out in faces:
                    p, grad_s = head_pass(face[:, at[0]], face[:, at[1]], q, d, level, delta, bias)
                    out[:, at[0]] = (dot(grad_s, q) * SCALE).astype(out.dtype)
                    out[:, at[1]] = dot(p, d).astype(out.dtype)
        out_ref[:, at[0]] = (grad_k * SCALE).astype(out_ref.dtype)
        out_ref[:, at[1]] = grad_v.astype(out_ref.dtype)


def grads_pass(mask, pack, swap, outer, cond, mine, theirs):
    rows = mine.shape[2]
    width = pack.shape[1]
    heads = width // 2 // HEAD_DIM
    return pl.pallas_call(
        grads_kernel,
        out_shape=(
            jax.ShapeDtypeStruct(cond.shape, jnp.bfloat16),
            jax.ShapeDtypeStruct(outer.shape, jnp.bfloat16),
            jax.ShapeDtypeStruct((cond.shape[0] + FACE, width), jnp.bfloat16),
            jax.ShapeDtypeStruct((STAT_ROWS, rows), jnp.float32),
        ),
        in_specs=[SMEM] + [VMEM] * 6,
        out_specs=(VMEM,) * 4,
        compiler_params=params(),
        cost_estimate=cost(rows, 2 * cond.shape[0] + 2 * FACE, heads, 4, 8 * pack.size),
        name="grads_pass",
    )(mask, pack, swap, outer, cond, mine, theirs)


def own_kernel(
    mask_ref, pack_ref, row_ref, own_ref, swap_ref, outer_ref, cond_ref, back_ref,
    att_ref, dq_ref, keep_ref,
):
    rows = row_ref.shape[1]
    width = pack_ref.shape[1] // 2
    cond_rows = cond_ref.shape[0]
    inner_bias, outer_bias = face_bias(mask_ref)
    segments = (
        (own_ref, None),
        (swap_ref.at[rows:], inner_bias),
        (outer_ref, outer_bias),
        (cond_ref, None),
        (back_ref.at[:cond_rows], None),
    )
    for head in range(width // HEAD_DIM):
        at = columns(head, width)
        q, d = pack_ref[:rows, at[0]], pack_ref[:rows, at[1]]
        level, delta = [row_ref[pl.ds(2 * head + i, 1), :] for i in range(2)]
        att = 0.0
        grad_q = 0.0
        for ref, bias in segments:
            key, value = ref[:, at[0]], ref[:, at[1]]
            p, grad_s = head_pass(key, value, q, d, level, delta, bias)
            if ref is own_ref:
                keep_ref[:, at[0]] = dot(grad_s, q) * SCALE
                keep_ref[:, at[1]] = dot(p, d)
            att = att + dot(value, p, TN)
            grad_q = grad_q + dot(key, grad_s, TN)
        att_ref[:, at[0]] = att.T.astype(jnp.bfloat16)
        dq_ref[:, at[0]] = (grad_q * SCALE).T.astype(jnp.bfloat16)


def own_pass(mask, pack, row_stats, own, swap, outer, cond, back):
    rows, width = own.shape
    heads = width // 2 // HEAD_DIM
    keys = rows + 2 * FACE + 2 * cond.shape[0]
    half = jax.ShapeDtypeStruct((rows, width // 2), jnp.bfloat16)
    return pl.pallas_call(
        own_kernel,
        out_shape=(half, half, jax.ShapeDtypeStruct((rows, width), jnp.float32)),
        in_specs=[SMEM] + [VMEM] * 7,
        out_specs=(VMEM,) * 3,
        compiler_params=params(),
        cost_estimate=cost(rows, keys, heads, 5, 16 * own.size),
        name="own_pass",
    )(mask, pack, row_stats, own, swap, outer, cond, back)


def per_device(queries, keys_values, cond_kv, face_mask, d_out):
    size = lax.axis_size("tile")
    rows, width = queries.shape
    chips = size // CORES
    cond_rows = cond_kv.shape[0]
    even = lax.axis_index("tile") % CORES == 0
    swap_cores = other_core(size)
    across = [(t, t + 1) for t in range(1, size - 1, CORES)]
    across += [(b, a) for a, b in across]

    copies = spread(cond_kv, chips)
    cond = lax.all_to_all(copies, "tile", 0, 0, axis_index_groups=same_core(size), tiled=True)
    cond = cond.reshape(chips * cond_rows, 2 * width)

    own = keys_values.reshape(rows, 2 * width)
    first, last = own[:FACE], own[rows - FACE :]
    outer = lax.ppermute(jnp.where(even, first, last), "tile", across)
    qd = jnp.concatenate([queries, d_out], axis=1)
    pack = jnp.concatenate([qd, jnp.where(even, last, first)], axis=0)
    swap = lax.ppermute(pack, "tile", swap_cores)
    near = near_stats(face_mask, pack, own, swap, outer)

    mine = cond_stats(pack, swap, cond, near)
    theirs = lax.ppermute(mine, "tile", swap_cores)
    grads, to_outer, back, row_stats = grads_pass(
        face_mask, pack, swap, outer, cond, mine, theirs
    )
    blocks = grads.reshape(chips, cond_rows, 2 * width)
    parts = lax.all_to_all(blocks, "tile", 0, 0, axis_index_groups=same_core(size), tiled=True)
    grad_cond = total(parts)

    from_outer = lax.ppermute(to_outer, "tile", across)
    back = lax.ppermute(back, "tile", swap_cores)
    attended, grad_q, keep = own_pass(
        face_mask, pack, row_stats, own, swap, outer, cond, back
    )
    from_inner = back[back.shape[0] - FACE :]
    low = jnp.where(even, from_outer, from_inner).astype(jnp.float32)
    high = jnp.where(even, from_inner, from_outer).astype(jnp.float32)
    keep = keep + jnp.concatenate([low, high], axis=0)
    grad_kv = keep.astype(jnp.bfloat16).reshape(rows, 2, width)
    return attended, grad_q, grad_kv, grad_cond


def solution(mesh):
    return jax.shard_map(
        per_device,
        mesh=mesh,
        in_specs=(
            P("tile", "head"),
            P("tile", None, "head"),
            P("tile", None, "head"),
            P("tile", None),
            P("tile", "head"),
        ),
        out_specs=(
            P("tile", "head"),
            P("tile", "head"),
            P("tile", None, "head"),
            P("tile", None, "head"),
        ),
        check_vma=False,
    )
```

```python
import functools

import jax
import jax.numpy as jnp
from jax import lax
from jax.experimental import pallas as pl
from jax.experimental.pallas import tpu as pltpu
from jax.sharding import PartitionSpec as P

HEAD_DIM = 128
FACE = 128
CORES = 2
SCALE = HEAD_DIM**-0.5
LOG2E = 1.4426950408889634
NEG_LARGE = -1e30
STAT_ROWS = 16

NT = (((1,), (1,)), ((), ()))
TN = (((0,), (0,)), ((), ()))


def dot(a, b, dims=(((1,), (0,)), ((), ()))):
    return lax.dot_general(a, b, dims, preferred_element_type=jnp.float32)


def other_core(size):
    return [(t, t ^ 1) for t in range(size)]


def same_core(size):
    return [list(range(c, size, CORES)) for c in range(CORES)]


def params(mib=16):
    return pltpu.CompilerParams(vmem_limit_bytes=mib * 1024 * 1024)


VMEM = pl.BlockSpec(memory_space=pltpu.VMEM)
HBM = pl.BlockSpec(memory_space=pltpu.HBM)
STAY_BACK = pl.CostEstimate(flops=4_000_000_000, bytes_accessed=0, transcendentals=0)
SMEM = pl.BlockSpec(memory_space=pltpu.SMEM)


def spread_kernel(cond_ref, out_ref, sems):
    copies = [
        pltpu.make_async_copy(cond_ref, out_ref.at[i], sems.at[i]) for i in range(out_ref.shape[0])
    ]
    for copy in copies:
        copy.start()
    for copy in copies:
        copy.wait()


def spread(cond_kv, copies):
    return pl.pallas_call(
        spread_kernel,
        out_shape=jax.ShapeDtypeStruct((copies,) + cond_kv.shape, cond_kv.dtype),
        in_specs=[HBM],
        out_specs=HBM,
        scratch_shapes=[pltpu.SemaphoreType.DMA((copies,))],
        compiler_params=params(),
        name="spread",
    )(cond_kv)


def pack_kernel(q_ref, d_ref, own_ref, out_ref):
    rows, width = q_ref.shape
    even = lax.axis_index("tile") % CORES == 0
    start = pl.multiple_of(jnp.where(even, rows - FACE, 0), FACE)
    out_ref[:rows, :width] = q_ref[...]
    out_ref[:rows, width:] = d_ref[...]
    out_ref[rows:, :] = own_ref[pl.ds(start, FACE), :]


def pack_queries(queries, d_out, own):
    rows, width = own.shape
    return pl.pallas_call(
        pack_kernel,
        out_shape=jax.ShapeDtypeStruct((rows + FACE, width), own.dtype),
        in_specs=[VMEM] * 3,
        out_specs=VMEM,
        compiler_params=params(),
        cost_estimate=STAY_BACK,
        name="pack_queries",
    )(queries, d_out, own)


def back_kernel(cond_ref, inner_ref, out_ref):
    rows = cond_ref.shape[0]
    out_ref[:rows, :] = cond_ref[...]
    out_ref[rows:, :] = inner_ref[...]


def pack_back(cond, inner):
    rows = cond.shape[0] + inner.shape[0]
    return pl.pallas_call(
        back_kernel,
        out_shape=jax.ShapeDtypeStruct((rows, cond.shape[1]), cond.dtype),
        in_specs=[VMEM] * 2,
        out_specs=VMEM,
        compiler_params=params(),
        cost_estimate=STAY_BACK,
        name="pack_back",
    )(cond, inner)


def total_kernel(parts_ref, out_ref):
    width = out_ref.shape[2]
    total = jnp.sum(parts_ref[...].astype(jnp.float32), axis=0)
    out_ref[:, 0, :] = total[:, :width]
    out_ref[:, 1, :] = total[:, width:]


def total(parts):
    _, rows, width = parts.shape
    return pl.pallas_call(
        total_kernel,
        out_shape=jax.ShapeDtypeStruct((rows, 2, width // 2), jnp.float32),
        in_specs=[VMEM],
        out_specs=VMEM,
        compiler_params=params(),
        name="total",
    )(parts)


def cost(queries, keys, heads, products, size):
    return pl.CostEstimate(
        flops=2 * products * heads * queries * keys * HEAD_DIM,
        bytes_accessed=size,
        transcendentals=heads * queries * keys,
    )


def face_bias(mask_ref):
    tile = lax.axis_index("tile")
    last = lax.axis_size("tile") - 1
    lower = jnp.where((mask_ref[0, 0] == 1) & (tile > 0), 0.0, NEG_LARGE)
    upper = jnp.where((mask_ref[0, 1] == 1) & (tile < last), 0.0, NEG_LARGE)
    even = tile % CORES == 0
    inner = jnp.where(even, upper, lower)
    outer = jnp.where(even, lower, upper)
    return inner.astype(jnp.float32), outer.astype(jnp.float32)


def columns(head, width):
    return [pl.ds(half * width + head * HEAD_DIM, HEAD_DIM) for half in range(2)]


def raised_stats(scores, grads):
    top = functools.reduce(jnp.maximum, [jnp.max(s, axis=0, keepdims=True) for s in scores])
    total = 0.0
    weighted = 0.0
    for s, g in zip(scores, grads):
        e = jnp.exp2(s - top)
        total = total + jnp.sum(e, axis=0, keepdims=True)
        weighted = weighted + jnp.sum(e * g, axis=0, keepdims=True)
    return top, total, weighted


def near_stats_kernel(mask_ref, pack_ref, own_ref, swap_ref, outer_ref, stat_ref):
    rows = stat_ref.shape[1]
    width = pack_ref.shape[1] // 2
    inner_bias, outer_bias = face_bias(mask_ref)
    for head in range(width // HEAD_DIM):
        at = columns(head, width)
        q, d = pack_ref[:rows, at[0]], pack_ref[:rows, at[1]]
        near = (
            (swap_ref.at[rows:], inner_bias),
            (own_ref, None),
            (outer_ref, outer_bias),
        )
        scores, grads = [], []
        for ref, bias in near:
            s = dot(ref[:, at[0]], q, NT) * (SCALE * LOG2E)
            scores.append(s if bias is None else s + bias)
            grads.append(dot(ref[:, at[1]], d, NT))
        for i, row in enumerate(raised_stats(scores, grads)):
            stat_ref[pl.ds(3 * head + i, 1), :] = row


def near_stats(mask, pack, own, swap, outer):
    rows, width = own.shape
    return pl.pallas_call(
        near_stats_kernel,
        out_shape=jax.ShapeDtypeStruct((STAT_ROWS, rows), jnp.float32),
        in_specs=[SMEM, VMEM, VMEM, VMEM, VMEM],
        out_specs=VMEM,
        compiler_params=params(),
        cost_estimate=cost(rows, rows + 2 * FACE, width // 2 // HEAD_DIM, 2, 5 * own.size),
        name="near_stats",
    )(mask, pack, own, swap, outer)


def cond_stats_kernel(pack_ref, swap_ref, cond_ref, near_ref, stat_ref):
    rows = near_ref.shape[1]
    width = pack_ref.shape[1] // 2
    stat_ref[0] = near_ref[...]
    for head in range(width // HEAD_DIM):
        at = columns(head, width)
        key, value = cond_ref[:, at[0]], cond_ref[:, at[1]]
        for side, ref in enumerate((pack_ref, swap_ref)):
            s = dot(key, ref[:rows, at[0]], NT) * (SCALE * LOG2E)
            g = dot(value, ref[:rows, at[1]], NT)
            for i, row in enumerate(raised_stats([s], [g])):
                stat_ref[1 + side, pl.ds(3 * head + i, 1), :] = row


def cond_stats(pack, swap, cond, near):
    rows = near.shape[1]
    heads = pack.shape[1] // 2 // HEAD_DIM
    return pl.pallas_call(
        cond_stats_kernel,
        out_shape=jax.ShapeDtypeStruct((3, STAT_ROWS, rows), jnp.float32),
        in_specs=[VMEM] * 4,
        out_specs=VMEM,
        compiler_params=params(),
        cost_estimate=cost(2 * rows, cond.shape[0], heads, 2, 6 * pack.size),
        name="cond_stats",
    )(pack, swap, cond, near)


def head_pass(key, value, q, d, level, delta, bias=None):
    s = dot(key, q, NT) * (SCALE * LOG2E)
    if bias is not None:
        s = s + bias
    p = jnp.exp2(s - level)
    grad_s = (p * (dot(value, d, NT) - delta)).astype(jnp.bfloat16)
    return p.astype(jnp.bfloat16), grad_s


def grads_kernel(pack_ref, swap_ref, cond_ref, mine_ref, their_ref, out_ref, row_ref):
    rows = row_ref.shape[1]
    width = pack_ref.shape[1] // 2
    for head in range(width // HEAD_DIM):
        at = columns(head, width)
        key, value = cond_ref[:, at[0]], cond_ref[:, at[1]]
        grad_k = 0.0
        grad_v = 0.0
        for side, ref in enumerate((pack_ref, swap_ref)):
            home, away = (mine_ref, their_ref) if side == 0 else (their_ref, mine_ref)
            parts = [
                [r[pl.ds(3 * head + i, 1), :] for i in range(3)]
                for r in (home.at[0], home.at[1], away.at[2])
            ]
            top = functools.reduce(jnp.maximum, [p[0] for p in parts])
            total = sum(p[1] * jnp.exp2(p[0] - top) for p in parts)
            weighted = sum(p[2] * jnp.exp2(p[0] - top) for p in parts)
            level = top + jnp.log2(total)
            delta = weighted / total
            q, d = ref[:rows, at[0]], ref[:rows, at[1]]
            p, grad_s = head_pass(key, value, q, d, level, delta)
            grad_k = grad_k + dot(grad_s, q)
            grad_v = grad_v + dot(p, d)
            if side == 0:
                row_ref[pl.ds(2 * head, 1), :] = level
                row_ref[pl.ds(2 * head + 1, 1), :] = delta
        out_ref[:, at[0]] = (grad_k * SCALE).astype(out_ref.dtype)
        out_ref[:, at[1]] = grad_v.astype(out_ref.dtype)


def grads_pass(pack, swap, cond, mine, theirs):
    rows = mine.shape[2]
    heads = pack.shape[1] // 2 // HEAD_DIM
    return pl.pallas_call(
        grads_kernel,
        out_shape=(
            jax.ShapeDtypeStruct(cond.shape, jnp.bfloat16),
            jax.ShapeDtypeStruct((STAT_ROWS, rows), jnp.float32),
        ),
        in_specs=[VMEM] * 5,
        out_specs=(VMEM,) * 2,
        compiler_params=params(),
        cost_estimate=cost(2 * rows, cond.shape[0], heads, 4, 8 * pack.size),
        name="grads_pass",
    )(pack, swap, cond, mine, theirs)


def face_kernel(mask_ref, pack_ref, row_ref, swap_ref, outer_ref, to_inner_ref, to_outer_ref):
    rows = row_ref.shape[1]
    width = pack_ref.shape[1] // 2
    inner_bias, outer_bias = face_bias(mask_ref)
    faces = (
        (swap_ref.at[rows:], inner_bias, to_inner_ref),
        (outer_ref, outer_bias, to_outer_ref),
    )
    for head in range(width // HEAD_DIM):
        at = columns(head, width)
        q, d = pack_ref[:rows, at[0]], pack_ref[:rows, at[1]]
        level, delta = [row_ref[pl.ds(2 * head + i, 1), :] for i in range(2)]
        for face, bias, out in faces:
            p, grad_s = head_pass(face[:, at[0]], face[:, at[1]], q, d, level, delta, bias)
            out[:, at[0]] = (dot(grad_s, q) * SCALE).astype(out.dtype)
            out[:, at[1]] = dot(p, d).astype(out.dtype)


def face_pass(mask, pack, row_stats, swap, outer):
    rows = row_stats.shape[1]
    heads = pack.shape[1] // 2 // HEAD_DIM
    face = jax.ShapeDtypeStruct(outer.shape, jnp.bfloat16)
    return pl.pallas_call(
        face_kernel,
        out_shape=(face, face),
        in_specs=[SMEM] + [VMEM] * 4,
        out_specs=(VMEM,) * 2,
        compiler_params=params(),
        cost_estimate=cost(rows, 2 * FACE, heads, 4, 6 * pack.size),
        name="face_pass",
    )(mask, pack, row_stats, swap, outer)


def own_kernel(
    mask_ref, pack_ref, row_ref, own_ref, swap_ref, outer_ref, cond_ref, back_ref,
    att_ref, dq_ref, keep_ref,
):
    rows = row_ref.shape[1]
    width = pack_ref.shape[1] // 2
    cond_rows = cond_ref.shape[0]
    inner_bias, outer_bias = face_bias(mask_ref)
    segments = (
        (own_ref, None),
        (swap_ref.at[rows:], inner_bias),
        (outer_ref, outer_bias),
        (cond_ref, None),
        (back_ref.at[:cond_rows], None),
    )
    for head in range(width // HEAD_DIM):
        at = columns(head, width)
        q, d = pack_ref[:rows, at[0]], pack_ref[:rows, at[1]]
        level, delta = [row_ref[pl.ds(2 * head + i, 1), :] for i in range(2)]
        att = 0.0
        grad_q = 0.0
        for ref, bias in segments:
            key, value = ref[:, at[0]], ref[:, at[1]]
            p, grad_s = head_pass(key, value, q, d, level, delta, bias)
            if ref is own_ref:
                keep_ref[:, at[0]] = dot(grad_s, q) * SCALE
                keep_ref[:, at[1]] = dot(p, d)
            att = att + dot(value, p, TN)
            grad_q = grad_q + dot(key, grad_s, TN)
        att_ref[:, at[0]] = att.T.astype(jnp.bfloat16)
        dq_ref[:, at[0]] = (grad_q * SCALE).T.astype(jnp.bfloat16)


def own_pass(mask, pack, row_stats, own, swap, outer, cond, back):
    rows, width = own.shape
    heads = width // 2 // HEAD_DIM
    keys = rows + 2 * FACE + 2 * cond.shape[0]
    half = jax.ShapeDtypeStruct((rows, width // 2), jnp.bfloat16)
    return pl.pallas_call(
        own_kernel,
        out_shape=(half, half, jax.ShapeDtypeStruct((rows, width), jnp.float32)),
        in_specs=[SMEM] + [VMEM] * 7,
        out_specs=(VMEM,) * 3,
        compiler_params=params(),
        cost_estimate=cost(rows, keys, heads, 5, 16 * own.size),
        name="own_pass",
    )(mask, pack, row_stats, own, swap, outer, cond, back)


def per_device(queries, keys_values, cond_kv, face_mask, d_out):
    size = lax.axis_size("tile")
    rows, width = queries.shape
    chips = size // CORES
    cond_rows = cond_kv.shape[0]
    even = lax.axis_index("tile") % CORES == 0
    swap_cores = other_core(size)
    across = [(t, t + 1) for t in range(1, size - 1, CORES)]
    across += [(b, a) for a, b in across]

    copies = spread(cond_kv, chips)
    cond = lax.all_to_all(copies, "tile", 0, 0, axis_index_groups=same_core(size), tiled=True)
    cond = cond.reshape(chips * cond_rows, 2 * width)

    own = lax.optimization_barrier(keys_values.reshape(rows, 2 * width))
    edge = lax.dynamic_slice_in_dim(own, jnp.where(even, 0, rows - FACE), FACE, axis=0)
    outer = lax.ppermute(edge, "tile", across)
    pack = pack_queries(queries, d_out, own)
    swap = lax.ppermute(pack, "tile", swap_cores)
    near = near_stats(face_mask, pack, own, swap, outer)

    mine = cond_stats(pack, swap, cond, near)
    theirs = lax.ppermute(mine, "tile", swap_cores)
    grads, row_stats = grads_pass(pack, swap, cond, mine, theirs)
    blocks = grads.reshape(chips, cond_rows, 2 * width)
    parts = lax.all_to_all(blocks, "tile", 0, 0, axis_index_groups=same_core(size), tiled=True)
    grad_cond = total(parts)

    to_inner, to_outer = face_pass(face_mask, pack, row_stats, swap, outer)
    from_outer = lax.ppermute(to_outer, "tile", across)
    back = lax.ppermute(pack_back(cond, to_inner), "tile", swap_cores)
    attended, grad_q, keep = own_pass(
        face_mask, pack, row_stats, own, swap, outer, cond, back
    )
    from_inner = back[back.shape[0] - FACE :]
    low = jnp.where(even, from_outer, from_inner).astype(jnp.float32)
    high = jnp.where(even, from_inner, from_outer).astype(jnp.float32)
    keep = keep + jnp.concatenate([low, high], axis=0)
    grad_kv = keep.astype(jnp.bfloat16).reshape(rows, 2, width)
    return attended, grad_q, grad_kv, grad_cond


def solution(mesh):
    return jax.shard_map(
        per_device,
        mesh=mesh,
        in_specs=(
            P("tile", "head"),
            P("tile", None, "head"),
            P("tile", None, "head"),
            P("tile", None),
            P("tile", "head"),
        ),
        out_specs=(
            P("tile", "head"),
            P("tile", "head"),
            P("tile", None, "head"),
            P("tile", None, "head"),
        ),
        check_vma=False,
    )
```

```python
import functools

import jax
import jax.numpy as jnp
from jax import lax
from jax.experimental import pallas as pl
from jax.experimental.pallas import tpu as pltpu
from jax.sharding import PartitionSpec as P

HEAD_DIM = 128
FACE = 128
CORES = 2
SCALE = HEAD_DIM**-0.5
LOG2E = 1.4426950408889634
NEG_LARGE = -1e30
STAT_ROWS = 16

NT = (((1,), (1,)), ((), ()))
TN = (((0,), (0,)), ((), ()))


def dot(a, b, dims=(((1,), (0,)), ((), ()))):
    return lax.dot_general(a, b, dims, preferred_element_type=jnp.float32)


def other_core(size):
    return [(t, t ^ 1) for t in range(size)]


def same_core(size):
    return [list(range(c, size, CORES)) for c in range(CORES)]


def params(mib=16):
    return pltpu.CompilerParams(vmem_limit_bytes=mib * 1024 * 1024)


VMEM = pl.BlockSpec(memory_space=pltpu.VMEM)
HBM = pl.BlockSpec(memory_space=pltpu.HBM)
LIGHT = pl.CostEstimate(flops=1, bytes_accessed=1, transcendentals=0)
HEAVY = pl.CostEstimate(flops=6_000_000_000, bytes_accessed=0, transcendentals=0)
SMEM = pl.BlockSpec(memory_space=pltpu.SMEM)


def spread_kernel(cond_ref, out_ref, sems):
    copies = [
        pltpu.make_async_copy(cond_ref, out_ref.at[i], sems.at[i]) for i in range(out_ref.shape[0])
    ]
    for copy in copies:
        copy.start()
    for copy in copies:
        copy.wait()


def spread(cond_kv, copies):
    return pl.pallas_call(
        spread_kernel,
        out_shape=jax.ShapeDtypeStruct((copies,) + cond_kv.shape, cond_kv.dtype),
        in_specs=[HBM],
        out_specs=HBM,
        scratch_shapes=[pltpu.SemaphoreType.DMA((copies,))],
        compiler_params=params(60),
        name="spread",
    )(cond_kv)


def pack_kernel(q_ref, d_ref, own_ref, out_ref):
    rows, width = q_ref.shape
    even = lax.axis_index("tile") % CORES == 0
    start = pl.multiple_of(jnp.where(even, rows - FACE, 0), FACE)
    out_ref[:rows, :width] = q_ref[...]
    out_ref[:rows, width:] = d_ref[...]
    out_ref[rows:, :] = own_ref[pl.ds(start, FACE), :]


def pack_queries(queries, d_out, own):
    rows, width = own.shape
    return pl.pallas_call(
        pack_kernel,
        out_shape=jax.ShapeDtypeStruct((rows + FACE, width), own.dtype),
        in_specs=[VMEM] * 3,
        out_specs=VMEM,
        compiler_params=params(),
        cost_estimate=LIGHT,
        name="pack_queries",
    )(queries, d_out, own)


def back_kernel(cond_ref, inner_ref, out_ref):
    rows = cond_ref.shape[0]
    out_ref[:rows, :] = cond_ref[...]
    out_ref[rows:, :] = inner_ref[...]


def pack_back(cond, inner):
    rows = cond.shape[0] + inner.shape[0]
    return pl.pallas_call(
        back_kernel,
        out_shape=jax.ShapeDtypeStruct((rows, cond.shape[1]), cond.dtype),
        in_specs=[VMEM] * 2,
        out_specs=VMEM,
        compiler_params=params(),
        cost_estimate=LIGHT,
        name="pack_back",
    )(cond, inner)


def total_kernel(parts_ref, out_ref):
    width = out_ref.shape[2]
    total = jnp.sum(parts_ref[...].astype(jnp.float32), axis=0)
    out_ref[:, 0, :] = total[:, :width]
    out_ref[:, 1, :] = total[:, width:]


def total(parts):
    _, rows, width = parts.shape
    return pl.pallas_call(
        total_kernel,
        out_shape=jax.ShapeDtypeStruct((rows, 2, width // 2), jnp.float32),
        in_specs=[VMEM],
        out_specs=VMEM,
        compiler_params=params(),
        name="total",
    )(parts)


def cost(queries, keys, heads, products, size):
    return pl.CostEstimate(
        flops=2 * products * heads * queries * keys * HEAD_DIM,
        bytes_accessed=size,
        transcendentals=heads * queries * keys,
    )


def face_bias(mask_ref):
    tile = lax.axis_index("tile")
    last = lax.axis_size("tile") - 1
    lower = jnp.where((mask_ref[0, 0] == 1) & (tile > 0), 0.0, NEG_LARGE)
    upper = jnp.where((mask_ref[0, 1] == 1) & (tile < last), 0.0, NEG_LARGE)
    even = tile % CORES == 0
    inner = jnp.where(even, upper, lower)
    outer = jnp.where(even, lower, upper)
    return inner.astype(jnp.float32), outer.astype(jnp.float32)


def columns(head, width):
    return [pl.ds(half * width + head * HEAD_DIM, HEAD_DIM) for half in range(2)]


def raised_stats(scores, grads):
    top = functools.reduce(jnp.maximum, [jnp.max(s, axis=0, keepdims=True) for s in scores])
    total = 0.0
    weighted = 0.0
    for s, g in zip(scores, grads):
        e = jnp.exp2(s - top)
        total = total + jnp.sum(e, axis=0, keepdims=True)
        weighted = weighted + jnp.sum(e * g, axis=0, keepdims=True)
    return top, total, weighted


def near_stats_kernel(mask_ref, pack_ref, own_ref, outer_ref, stat_ref):
    rows = stat_ref.shape[1]
    width = pack_ref.shape[1] // 2
    _, outer_bias = face_bias(mask_ref)
    for head in range(width // HEAD_DIM):
        at = columns(head, width)
        q, d = pack_ref[:rows, at[0]], pack_ref[:rows, at[1]]
        near = ((own_ref, None), (outer_ref, outer_bias))
        scores, grads = [], []
        for ref, bias in near:
            s = dot(ref[:, at[0]], q, NT) * (SCALE * LOG2E)
            scores.append(s if bias is None else s + bias)
            grads.append(dot(ref[:, at[1]], d, NT))
        for i, row in enumerate(raised_stats(scores, grads)):
            stat_ref[pl.ds(3 * head + i, 1), :] = row


def near_stats(mask, pack, own, outer):
    rows, width = own.shape
    return pl.pallas_call(
        near_stats_kernel,
        out_shape=jax.ShapeDtypeStruct((STAT_ROWS, rows), jnp.float32),
        in_specs=[SMEM, VMEM, VMEM, VMEM],
        out_specs=VMEM,
        compiler_params=params(),
        cost_estimate=HEAVY,
        name="near_stats",
    )(mask, pack, own, outer)


def cond_stats_kernel(mask_ref, pack_ref, swap_ref, cond_ref, near_ref, stat_ref):
    rows = near_ref.shape[1]
    width = pack_ref.shape[1] // 2
    inner_bias, _ = face_bias(mask_ref)
    stat_ref[0] = near_ref[...]
    for head in range(width // HEAD_DIM):
        at = columns(head, width)
        for side, ref in enumerate((pack_ref, swap_ref)):
            q, d = ref[:rows, at[0]], ref[:rows, at[1]]
            scores = [dot(cond_ref[:, at[0]], q, NT) * (SCALE * LOG2E)]
            grads = [dot(cond_ref[:, at[1]], d, NT)]
            if side == 0:
                scores.append(dot(swap_ref[rows:, at[0]], q, NT) * (SCALE * LOG2E) + inner_bias)
                grads.append(dot(swap_ref[rows:, at[1]], d, NT))
            for i, row in enumerate(raised_stats(scores, grads)):
                stat_ref[1 + side, pl.ds(3 * head + i, 1), :] = row


def cond_stats(mask, pack, swap, cond, near):
    rows = near.shape[1]
    heads = pack.shape[1] // 2 // HEAD_DIM
    return pl.pallas_call(
        cond_stats_kernel,
        out_shape=jax.ShapeDtypeStruct((3, STAT_ROWS, rows), jnp.float32),
        in_specs=[SMEM] + [VMEM] * 4,
        out_specs=VMEM,
        compiler_params=params(),
        cost_estimate=cost(2 * rows, cond.shape[0], heads, 2, 6 * pack.size),
        name="cond_stats",
    )(mask, pack, swap, cond, near)


def head_pass(key, value, q, d, level, delta, bias=None):
    s = dot(key, q, NT) * (SCALE * LOG2E)
    if bias is not None:
        s = s + bias
    p = jnp.exp2(s - level)
    grad_s = (p * (dot(value, d, NT) - delta)).astype(jnp.bfloat16)
    return p.astype(jnp.bfloat16), grad_s


def grads_kernel(pack_ref, swap_ref, cond_ref, mine_ref, their_ref, out_ref, row_ref):
    rows = row_ref.shape[1]
    width = pack_ref.shape[1] // 2
    for head in range(width // HEAD_DIM):
        at = columns(head, width)
        key, value = cond_ref[:, at[0]], cond_ref[:, at[1]]
        grad_k = 0.0
        grad_v = 0.0
        for side, ref in enumerate((pack_ref, swap_ref)):
            home, away = (mine_ref, their_ref) if side == 0 else (their_ref, mine_ref)
            parts = [
                [r[pl.ds(3 * head + i, 1), :] for i in range(3)]
                for r in (home.at[0], home.at[1], away.at[2])
            ]
            top = functools.reduce(jnp.maximum, [p[0] for p in parts])
            total = sum(p[1] * jnp.exp2(p[0] - top) for p in parts)
            weighted = sum(p[2] * jnp.exp2(p[0] - top) for p in parts)
            level = top + jnp.log2(total)
            delta = weighted / total
            q, d = ref[:rows, at[0]], ref[:rows, at[1]]
            p, grad_s = head_pass(key, value, q, d, level, delta)
            grad_k = grad_k + dot(grad_s, q)
            grad_v = grad_v + dot(p, d)
            if side == 0:
                row_ref[pl.ds(2 * head, 1), :] = level
                row_ref[pl.ds(2 * head + 1, 1), :] = delta
        out_ref[:, at[0]] = (grad_k * SCALE).astype(out_ref.dtype)
        out_ref[:, at[1]] = grad_v.astype(out_ref.dtype)


def grads_pass(pack, swap, cond, mine, theirs):
    rows = mine.shape[2]
    heads = pack.shape[1] // 2 // HEAD_DIM
    return pl.pallas_call(
        grads_kernel,
        out_shape=(
            jax.ShapeDtypeStruct(cond.shape, jnp.bfloat16),
            jax.ShapeDtypeStruct((STAT_ROWS, rows), jnp.float32),
        ),
        in_specs=[VMEM] * 5,
        out_specs=(VMEM,) * 2,
        compiler_params=params(),
        cost_estimate=cost(2 * rows, cond.shape[0], heads, 4, 8 * pack.size),
        name="grads_pass",
    )(pack, swap, cond, mine, theirs)


def face_kernel(mask_ref, pack_ref, row_ref, swap_ref, outer_ref, to_inner_ref, to_outer_ref):
    rows = row_ref.shape[1]
    width = pack_ref.shape[1] // 2
    inner_bias, outer_bias = face_bias(mask_ref)
    faces = (
        (swap_ref.at[rows:], inner_bias, to_inner_ref),
        (outer_ref, outer_bias, to_outer_ref),
    )
    for head in range(width // HEAD_DIM):
        at = columns(head, width)
        q, d = pack_ref[:rows, at[0]], pack_ref[:rows, at[1]]
        level, delta = [row_ref[pl.ds(2 * head + i, 1), :] for i in range(2)]
        for face, bias, out in faces:
            p, grad_s = head_pass(face[:, at[0]], face[:, at[1]], q, d, level, delta, bias)
            out[:, at[0]] = (dot(grad_s, q) * SCALE).astype(out.dtype)
            out[:, at[1]] = dot(p, d).astype(out.dtype)


def face_pass(mask, pack, row_stats, swap, outer):
    rows = row_stats.shape[1]
    heads = pack.shape[1] // 2 // HEAD_DIM
    face = jax.ShapeDtypeStruct(outer.shape, jnp.bfloat16)
    return pl.pallas_call(
        face_kernel,
        out_shape=(face, face),
        in_specs=[SMEM] + [VMEM] * 4,
        out_specs=(VMEM,) * 2,
        compiler_params=params(),
        cost_estimate=LIGHT,
        name="face_pass",
    )(mask, pack, row_stats, swap, outer)


def own_kernel(
    mask_ref, pack_ref, row_ref, own_ref, swap_ref, outer_ref, cond_ref, back_ref,
    att_ref, dq_ref, keep_ref,
):
    rows = row_ref.shape[1]
    width = pack_ref.shape[1] // 2
    cond_rows = cond_ref.shape[0]
    inner_bias, outer_bias = face_bias(mask_ref)
    segments = (
        (own_ref, None),
        (swap_ref.at[rows:], inner_bias),
        (outer_ref, outer_bias),
        (cond_ref, None),
        (back_ref.at[:cond_rows], None),
    )
    for head in range(width // HEAD_DIM):
        at = columns(head, width)
        q, d = pack_ref[:rows, at[0]], pack_ref[:rows, at[1]]
        level, delta = [row_ref[pl.ds(2 * head + i, 1), :] for i in range(2)]
        att = 0.0
        grad_q = 0.0
        for ref, bias in segments:
            key, value = ref[:, at[0]], ref[:, at[1]]
            p, grad_s = head_pass(key, value, q, d, level, delta, bias)
            if ref is own_ref:
                keep_ref[:, at[0]] = dot(grad_s, q) * SCALE
                keep_ref[:, at[1]] = dot(p, d)
            att = att + dot(value, p, TN)
            grad_q = grad_q + dot(key, grad_s, TN)
        att_ref[:, at[0]] = att.T.astype(jnp.bfloat16)
        dq_ref[:, at[0]] = (grad_q * SCALE).T.astype(jnp.bfloat16)


def own_pass(mask, pack, row_stats, own, swap, outer, cond, back):
    rows, width = own.shape
    heads = width // 2 // HEAD_DIM
    keys = rows + 2 * FACE + 2 * cond.shape[0]
    half = jax.ShapeDtypeStruct((rows, width // 2), jnp.bfloat16)
    return pl.pallas_call(
        own_kernel,
        out_shape=(half, half, jax.ShapeDtypeStruct((rows, width), jnp.float32)),
        in_specs=[SMEM] + [VMEM] * 7,
        out_specs=(VMEM,) * 3,
        compiler_params=params(),
        cost_estimate=LIGHT,
        name="own_pass",
    )(mask, pack, row_stats, own, swap, outer, cond, back)


def per_device(queries, keys_values, cond_kv, face_mask, d_out):
    size = lax.axis_size("tile")
    rows, width = queries.shape
    chips = size // CORES
    cond_rows = cond_kv.shape[0]
    even = lax.axis_index("tile") % CORES == 0
    swap_cores = other_core(size)
    across = [(t, t + 1) for t in range(1, size - 1, CORES)]
    across += [(b, a) for a, b in across]

    copies = spread(cond_kv, chips)
    cond = lax.all_to_all(copies, "tile", 0, 0, axis_index_groups=same_core(size), tiled=True)
    cond = cond.reshape(chips * cond_rows, 2 * width)

    own = lax.optimization_barrier(keys_values.reshape(rows, 2 * width))
    edge = lax.dynamic_slice_in_dim(own, jnp.where(even, 0, rows - FACE), FACE, axis=0)
    outer = lax.ppermute(edge, "tile", across)
    pack = pack_queries(queries, d_out, own)
    swap = lax.ppermute(pack, "tile", swap_cores)
    near = near_stats(face_mask, pack, own, outer)

    mine = cond_stats(face_mask, pack, swap, cond, near)
    theirs = lax.ppermute(mine, "tile", swap_cores)
    grads, row_stats = grads_pass(pack, swap, cond, mine, theirs)
    blocks = grads.reshape(chips, cond_rows, 2 * width)
    parts = lax.all_to_all(blocks, "tile", 0, 0, axis_index_groups=same_core(size), tiled=True)
    grad_cond = total(parts)

    to_inner, to_outer = face_pass(face_mask, pack, row_stats, swap, outer)
    from_outer = lax.ppermute(to_outer, "tile", across)
    back = lax.ppermute(pack_back(cond, to_inner), "tile", swap_cores)
    attended, grad_q, keep = own_pass(
        face_mask, pack, row_stats, own, swap, outer, cond, back
    )
    from_inner = back[back.shape[0] - FACE :]
    low = jnp.where(even, from_outer, from_inner).astype(jnp.float32)
    high = jnp.where(even, from_inner, from_outer).astype(jnp.float32)
    keep = keep + jnp.concatenate([low, high], axis=0)
    grad_kv = keep.astype(jnp.bfloat16).reshape(rows, 2, width)
    return attended, grad_q, grad_kv, grad_cond


def solution(mesh):
    return jax.shard_map(
        per_device,
        mesh=mesh,
        in_specs=(
            P("tile", "head"),
            P("tile", None, "head"),
            P("tile", None, "head"),
            P("tile", None),
            P("tile", "head"),
        ),
        out_specs=(
            P("tile", "head"),
            P("tile", "head"),
            P("tile", None, "head"),
            P("tile", None, "head"),
        ),
        check_vma=False,
    )
```

```python
import functools

import jax
import jax.numpy as jnp
from jax import lax
from jax.experimental import pallas as pl
from jax.experimental.pallas import tpu as pltpu
from jax.sharding import PartitionSpec as P

HEAD_DIM = 128
FACE = 128
CORES = 2
SCALE = HEAD_DIM**-0.5
LOG2E = 1.4426950408889634
NEG_LARGE = -1e30
STAT_ROWS = 16

NT = (((1,), (1,)), ((), ()))
TN = (((0,), (0,)), ((), ()))


def dot(a, b, dims=(((1,), (0,)), ((), ()))):
    return lax.dot_general(a, b, dims, preferred_element_type=jnp.float32)


def other_core(size):
    return [(t, t ^ 1) for t in range(size)]


def same_core(size):
    return [list(range(c, size, CORES)) for c in range(CORES)]


def params(mib=16):
    return pltpu.CompilerParams(vmem_limit_bytes=mib * 1024 * 1024)


VMEM = pl.BlockSpec(memory_space=pltpu.VMEM)
LIGHT = pl.CostEstimate(flops=1, bytes_accessed=1, transcendentals=0)
HEAVY = pl.CostEstimate(flops=6_000_000_000, bytes_accessed=0, transcendentals=0)
SMEM = pl.BlockSpec(memory_space=pltpu.SMEM)


def spread_kernel(cond_ref, out_ref):
    rows, _, width = cond_ref.shape
    flat = jnp.concatenate([cond_ref[:, 0, :], cond_ref[:, 1, :]], axis=1)
    out_ref[...] = jnp.broadcast_to(flat[None], out_ref.shape)


def spread(cond_kv, copies):
    rows, _, width = cond_kv.shape
    return pl.pallas_call(
        spread_kernel,
        out_shape=jax.ShapeDtypeStruct((copies, rows, 2 * width), cond_kv.dtype),
        in_specs=[VMEM],
        out_specs=VMEM,
        compiler_params=params(),
        name="spread",
    )(cond_kv)


def pack_kernel(q_ref, d_ref, own_ref, out_ref):
    rows, width = q_ref.shape
    even = lax.axis_index("tile") % CORES == 0
    start = pl.multiple_of(jnp.where(even, rows - FACE, 0), FACE)
    out_ref[:rows, :width] = q_ref[...]
    out_ref[:rows, width:] = d_ref[...]
    out_ref[rows:, :] = own_ref[pl.ds(start, FACE), :]


def pack_queries(queries, d_out, own):
    rows, width = own.shape
    return pl.pallas_call(
        pack_kernel,
        out_shape=jax.ShapeDtypeStruct((rows + FACE, width), own.dtype),
        in_specs=[VMEM] * 3,
        out_specs=VMEM,
        compiler_params=params(),
        cost_estimate=LIGHT,
        name="pack_queries",
    )(queries, d_out, own)


def total_kernel(parts_ref, out_ref):
    width = out_ref.shape[2]
    total = jnp.sum(parts_ref[...].astype(jnp.float32), axis=0)
    out_ref[:, 0, :] = total[:, :width]
    out_ref[:, 1, :] = total[:, width:]


def total(parts):
    _, rows, width = parts.shape
    return pl.pallas_call(
        total_kernel,
        out_shape=jax.ShapeDtypeStruct((rows, 2, width // 2), jnp.float32),
        in_specs=[VMEM],
        out_specs=VMEM,
        compiler_params=params(),
        name="total",
    )(parts)


def cost(queries, keys, heads, products, size):
    return pl.CostEstimate(
        flops=2 * products * heads * queries * keys * HEAD_DIM,
        bytes_accessed=size,
        transcendentals=heads * queries * keys,
    )


def face_bias(mask_ref):
    tile = lax.axis_index("tile")
    last = lax.axis_size("tile") - 1
    lower = jnp.where((mask_ref[0, 0] == 1) & (tile > 0), 0.0, NEG_LARGE)
    upper = jnp.where((mask_ref[0, 1] == 1) & (tile < last), 0.0, NEG_LARGE)
    even = tile % CORES == 0
    inner = jnp.where(even, upper, lower)
    outer = jnp.where(even, lower, upper)
    return inner.astype(jnp.float32), outer.astype(jnp.float32)


def columns(head, width):
    return [pl.ds(half * width + head * HEAD_DIM, HEAD_DIM) for half in range(2)]


def raised_stats(scores, grads):
    top = functools.reduce(jnp.maximum, [jnp.max(s, axis=0, keepdims=True) for s in scores])
    total = 0.0
    weighted = 0.0
    for s, g in zip(scores, grads):
        e = jnp.exp2(s - top)
        total = total + jnp.sum(e, axis=0, keepdims=True)
        weighted = weighted + jnp.sum(e * g, axis=0, keepdims=True)
    return top, total, weighted


def near_stats_kernel(mask_ref, pack_ref, own_ref, outer_ref, stat_ref):
    rows = stat_ref.shape[1]
    width = pack_ref.shape[1] // 2
    _, outer_bias = face_bias(mask_ref)
    for head in range(width // HEAD_DIM):
        at = columns(head, width)
        q, d = pack_ref[:rows, at[0]], pack_ref[:rows, at[1]]
        scores, grads = [], []
        for ref, bias in ((own_ref, None), (outer_ref, outer_bias)):
            s = dot(ref[:, at[0]], q, NT) * (SCALE * LOG2E)
            scores.append(s if bias is None else s + bias)
            grads.append(dot(ref[:, at[1]], d, NT))
        for i, row in enumerate(raised_stats(scores, grads)):
            stat_ref[pl.ds(3 * head + i, 1), :] = row


def near_stats(mask, pack, own, outer):
    rows, width = own.shape
    return pl.pallas_call(
        near_stats_kernel,
        out_shape=jax.ShapeDtypeStruct((STAT_ROWS, rows), jnp.float32),
        in_specs=[SMEM, VMEM, VMEM, VMEM],
        out_specs=VMEM,
        compiler_params=params(),
        cost_estimate=HEAVY,
        name="near_stats",
    )(mask, pack, own, outer)


def inner_stats_kernel(mask_ref, pack_ref, swap_ref, stat_ref):
    rows = stat_ref.shape[1]
    width = pack_ref.shape[1] // 2
    inner_bias, _ = face_bias(mask_ref)
    for head in range(width // HEAD_DIM):
        at = columns(head, width)
        s = dot(swap_ref[rows:, at[0]], pack_ref[:rows, at[0]], NT) * (SCALE * LOG2E) + inner_bias
        g = dot(swap_ref[rows:, at[1]], pack_ref[:rows, at[1]], NT)
        for i, row in enumerate(raised_stats([s], [g])):
            stat_ref[pl.ds(3 * head + i, 1), :] = row


def inner_stats(mask, pack, swap):
    rows, heads = pack.shape[0] - FACE, pack.shape[1] // 2 // HEAD_DIM
    return pl.pallas_call(
        inner_stats_kernel,
        out_shape=jax.ShapeDtypeStruct((STAT_ROWS, rows), jnp.float32),
        in_specs=[SMEM, VMEM, VMEM],
        out_specs=VMEM,
        compiler_params=params(),
        cost_estimate=cost(rows, FACE, heads, 2, 4 * pack.size),
        name="inner_stats",
    )(mask, pack, swap)


def cond_stats_kernel(pack_ref, swap_ref, cond_ref, near_ref, inner_ref, stat_ref):
    rows = near_ref.shape[1]
    width = pack_ref.shape[1] // 2
    stat_ref[0] = near_ref[...]
    stat_ref[1] = inner_ref[...]
    for head in range(width // HEAD_DIM):
        at = columns(head, width)
        key, value = cond_ref[:, at[0]], cond_ref[:, at[1]]
        for side, ref in enumerate((pack_ref, swap_ref)):
            s = dot(key, ref[:rows, at[0]], NT) * (SCALE * LOG2E)
            g = dot(value, ref[:rows, at[1]], NT)
            for i, row in enumerate(raised_stats([s], [g])):
                stat_ref[2 + side, pl.ds(3 * head + i, 1), :] = row


def cond_stats(pack, swap, cond, near, inner):
    rows = near.shape[1]
    heads = pack.shape[1] // 2 // HEAD_DIM
    return pl.pallas_call(
        cond_stats_kernel,
        out_shape=jax.ShapeDtypeStruct((4, STAT_ROWS, rows), jnp.float32),
        in_specs=[VMEM] * 5,
        out_specs=VMEM,
        compiler_params=params(),
        cost_estimate=cost(2 * rows, cond.shape[0], heads, 2, 6 * pack.size),
        name="cond_stats",
    )(pack, swap, cond, near, inner)


def head_pass(key, value, q, d, level, delta, bias=None):
    s = dot(key, q, NT) * (SCALE * LOG2E)
    if bias is not None:
        s = s + bias
    p = jnp.exp2(s - level)
    grad_s = (p * (dot(value, d, NT) - delta)).astype(jnp.bfloat16)
    return p.astype(jnp.bfloat16), grad_s


def grads_kernel(pack_ref, swap_ref, cond_ref, mine_ref, their_ref, out_ref, row_ref):
    rows = row_ref.shape[1]
    width = pack_ref.shape[1] // 2
    for head in range(width // HEAD_DIM):
        at = columns(head, width)
        key, value = cond_ref[:, at[0]], cond_ref[:, at[1]]
        grad_k = 0.0
        grad_v = 0.0
        for side, ref in enumerate((pack_ref, swap_ref)):
            home, away = (mine_ref, their_ref) if side == 0 else (their_ref, mine_ref)
            parts = [
                [r[pl.ds(3 * head + i, 1), :] for i in range(3)]
                for r in (home.at[0], home.at[1], home.at[2], away.at[3])
            ]
            top = functools.reduce(jnp.maximum, [p[0] for p in parts])
            total = sum(p[1] * jnp.exp2(p[0] - top) for p in parts)
            weighted = sum(p[2] * jnp.exp2(p[0] - top) for p in parts)
            level = top + jnp.log2(total)
            delta = weighted / total
            q, d = ref[:rows, at[0]], ref[:rows, at[1]]
            p, grad_s = head_pass(key, value, q, d, level, delta)
            grad_k = grad_k + dot(grad_s, q)
            grad_v = grad_v + dot(p, d)
            if side == 0:
                row_ref[pl.ds(2 * head, 1), :] = level
                row_ref[pl.ds(2 * head + 1, 1), :] = delta
        out_ref[:, at[0]] = (grad_k * SCALE).astype(out_ref.dtype)
        out_ref[:, at[1]] = grad_v.astype(out_ref.dtype)


def grads_pass(pack, swap, cond, mine, theirs):
    rows = mine.shape[2]
    heads = pack.shape[1] // 2 // HEAD_DIM
    return pl.pallas_call(
        grads_kernel,
        out_shape=(
            jax.ShapeDtypeStruct(cond.shape, jnp.bfloat16),
            jax.ShapeDtypeStruct((STAT_ROWS, rows), jnp.float32),
        ),
        in_specs=[VMEM] * 5,
        out_specs=(VMEM,) * 2,
        compiler_params=params(),
        cost_estimate=cost(2 * rows, cond.shape[0], heads, 4, 8 * pack.size),
        name="grads_pass",
    )(pack, swap, cond, mine, theirs)


def face_kernel(mask_ref, pack_ref, row_ref, swap_ref, outer_ref, to_inner_ref, to_outer_ref):
    rows = row_ref.shape[1]
    width = pack_ref.shape[1] // 2
    inner_bias, outer_bias = face_bias(mask_ref)
    faces = (
        (swap_ref.at[rows:], inner_bias, to_inner_ref),
        (outer_ref, outer_bias, to_outer_ref),
    )
    for head in range(width // HEAD_DIM):
        at = columns(head, width)
        q, d = pack_ref[:rows, at[0]], pack_ref[:rows, at[1]]
        level, delta = [row_ref[pl.ds(2 * head + i, 1), :] for i in range(2)]
        for face, bias, out in faces:
            p, grad_s = head_pass(face[:, at[0]], face[:, at[1]], q, d, level, delta, bias)
            out[:, at[0]] = (dot(grad_s, q) * SCALE).astype(out.dtype)
            out[:, at[1]] = dot(p, d).astype(out.dtype)


def face_pass(mask, pack, row_stats, swap, outer):
    rows = row_stats.shape[1]
    heads = pack.shape[1] // 2 // HEAD_DIM
    face = jax.ShapeDtypeStruct(outer.shape, jnp.bfloat16)
    return pl.pallas_call(
        face_kernel,
        out_shape=(face, face),
        in_specs=[SMEM] + [VMEM] * 4,
        out_specs=(VMEM,) * 2,
        compiler_params=params(),
        cost_estimate=cost(rows, 2 * FACE, heads, 6, 10 * pack.size),
        name="face_pass",
    )(mask, pack, row_stats, swap, outer)


def own_kernel(
    mask_ref, pack_ref, row_ref, own_ref, swap_ref, outer_ref, cond_ref, far_cond_ref,
    att_ref, dq_ref, keep_ref,
):
    rows = row_ref.shape[1]
    width = pack_ref.shape[1] // 2
    inner_bias, outer_bias = face_bias(mask_ref)
    segments = (
        (own_ref, None),
        (swap_ref.at[rows:], inner_bias),
        (outer_ref, outer_bias),
        (cond_ref, None),
        (far_cond_ref, None),
    )
    for head in range(width // HEAD_DIM):
        at = columns(head, width)
        q, d = pack_ref[:rows, at[0]], pack_ref[:rows, at[1]]
        level, delta = [row_ref[pl.ds(2 * head + i, 1), :] for i in range(2)]
        att = 0.0
        grad_q = 0.0
        for ref, bias in segments:
            key, value = ref[:, at[0]], ref[:, at[1]]
            p, grad_s = head_pass(key, value, q, d, level, delta, bias)
            if ref is own_ref:
                keep_ref[:, at[0]] = dot(grad_s, q) * SCALE
                keep_ref[:, at[1]] = dot(p, d)
            att = att + dot(value, p, TN)
            grad_q = grad_q + dot(key, grad_s, TN)
        att_ref[:, at[0]] = att.T.astype(jnp.bfloat16)
        dq_ref[:, at[0]] = (grad_q * SCALE).T.astype(jnp.bfloat16)


def own_pass(mask, pack, row_stats, own, swap, outer, cond, far_cond):
    rows, width = own.shape
    heads = width // 2 // HEAD_DIM
    keys = rows + 2 * FACE + 2 * cond.shape[0]
    half = jax.ShapeDtypeStruct((rows, width // 2), jnp.bfloat16)
    return pl.pallas_call(
        own_kernel,
        out_shape=(half, half, jax.ShapeDtypeStruct((rows, width), jnp.float32)),
        in_specs=[SMEM] + [VMEM] * 7,
        out_specs=(VMEM,) * 3,
        compiler_params=params(),
        cost_estimate=cost(rows, keys, heads, 5, 16 * own.size),
        name="own_pass",
    )(mask, pack, row_stats, own, swap, outer, cond, far_cond)


def per_device(queries, keys_values, cond_kv, face_mask, d_out):
    size = lax.axis_size("tile")
    rows, width = queries.shape
    chips = size // CORES
    cond_rows = cond_kv.shape[0]
    even = lax.axis_index("tile") % CORES == 0
    swap_cores = other_core(size)
    across = [(t, t + 1) for t in range(1, size - 1, CORES)]
    across += [(b, a) for a, b in across]

    copies = spread(cond_kv, chips)
    cond = lax.all_to_all(copies, "tile", 0, 0, axis_index_groups=same_core(size), tiled=True)
    cond = cond.reshape(chips * cond_rows, 2 * width)

    own = lax.optimization_barrier(keys_values.reshape(rows, 2 * width))
    edge = lax.dynamic_slice_in_dim(own, jnp.where(even, 0, rows - FACE), FACE, axis=0)
    outer = lax.ppermute(edge, "tile", across)
    pack = pack_queries(queries, d_out, own)
    swap = lax.ppermute(pack, "tile", swap_cores)
    near = near_stats(face_mask, pack, own, outer)
    inner = inner_stats(face_mask, pack, swap)

    mine = cond_stats(pack, swap, cond, near, inner)
    theirs = lax.ppermute(mine, "tile", swap_cores)
    grads, row_stats = grads_pass(pack, swap, cond, mine, theirs)
    blocks = grads.reshape(chips, cond_rows, 2 * width)
    parts = lax.all_to_all(blocks, "tile", 0, 0, axis_index_groups=same_core(size), tiled=True)
    grad_cond = total(parts)

    late_cond, row_stats = lax.optimization_barrier((cond, row_stats))
    far_cond = lax.ppermute(late_cond, "tile", swap_cores)
    to_inner, to_outer = face_pass(face_mask, pack, row_stats, swap, outer)
    from_outer = lax.ppermute(to_outer, "tile", across)
    from_inner = lax.ppermute(to_inner, "tile", swap_cores)
    attended, grad_q, keep = own_pass(
        face_mask, pack, row_stats, own, swap, outer, cond, far_cond
    )
    low = jnp.where(even, from_outer, from_inner).astype(jnp.float32)
    high = jnp.where(even, from_inner, from_outer).astype(jnp.float32)
    keep = keep + jnp.concatenate([low, high], axis=0)
    grad_kv = keep.astype(jnp.bfloat16).reshape(rows, 2, width)
    return attended, grad_q, grad_kv, grad_cond


def solution(mesh):
    return jax.shard_map(
        per_device,
        mesh=mesh,
        in_specs=(
            P("tile", "head"),
            P("tile", None, "head"),
            P("tile", None, "head"),
            P("tile", None),
            P("tile", "head"),
        ),
        out_specs=(
            P("tile", "head"),
            P("tile", "head"),
            P("tile", None, "head"),
            P("tile", None, "head"),
        ),
        check_vma=False,
    )
```

```python
import functools

import jax
import jax.numpy as jnp
from jax import lax
from jax.experimental import pallas as pl
from jax.experimental.pallas import tpu as pltpu
from jax.sharding import PartitionSpec as P

HEAD_DIM = 128
FACE = 128
CORES = 2
SCALE = HEAD_DIM**-0.5
LOG2E = 1.4426950408889634
NEG_LARGE = -1e30
STAT_ROWS = 16

NT = (((1,), (1,)), ((), ()))
TN = (((0,), (0,)), ((), ()))


def dot(a, b, dims=(((1,), (0,)), ((), ()))):
    return lax.dot_general(a, b, dims, preferred_element_type=jnp.float32)


def other_core(size):
    return [(t, t ^ 1) for t in range(size)]


def same_core(size):
    return [list(range(c, size, CORES)) for c in range(CORES)]


def params(mib=16):
    return pltpu.CompilerParams(vmem_limit_bytes=mib * 1024 * 1024)


VMEM = pl.BlockSpec(memory_space=pltpu.VMEM)
LIGHT = pl.CostEstimate(flops=1, bytes_accessed=1, transcendentals=0)
HEAVY = pl.CostEstimate(flops=6_000_000_000, bytes_accessed=0, transcendentals=0)
SMEM = pl.BlockSpec(memory_space=pltpu.SMEM)


def spread_kernel(cond_ref, out_ref):
    rows, _, width = cond_ref.shape
    flat = jnp.concatenate([cond_ref[:, 0, :], cond_ref[:, 1, :]], axis=1)
    out_ref[...] = jnp.broadcast_to(flat[None], out_ref.shape)


def spread(cond_kv, copies):
    rows, _, width = cond_kv.shape
    return pl.pallas_call(
        spread_kernel,
        out_shape=jax.ShapeDtypeStruct((copies, rows, 2 * width), cond_kv.dtype),
        in_specs=[VMEM],
        out_specs=VMEM,
        compiler_params=params(),
        name="spread",
    )(cond_kv)


def pack_kernel(q_ref, d_ref, own_ref, out_ref):
    rows, width = q_ref.shape
    even = lax.axis_index("tile") % CORES == 0
    start = pl.multiple_of(jnp.where(even, rows - FACE, 0), FACE)
    out_ref[:rows, :width] = q_ref[...]
    out_ref[:rows, width:] = d_ref[...]
    out_ref[rows:, :] = own_ref[pl.ds(start, FACE), :]


def pack_queries(queries, d_out, own):
    rows, width = own.shape
    return pl.pallas_call(
        pack_kernel,
        out_shape=jax.ShapeDtypeStruct((rows + FACE, width), own.dtype),
        in_specs=[VMEM] * 3,
        out_specs=VMEM,
        compiler_params=params(),
        cost_estimate=LIGHT,
        name="pack_queries",
    )(queries, d_out, own)


def total_kernel(parts_ref, out_ref):
    width = out_ref.shape[2]
    total = jnp.sum(parts_ref[...].astype(jnp.float32), axis=0)
    out_ref[:, 0, :] = total[:, :width]
    out_ref[:, 1, :] = total[:, width:]


def total(parts):
    _, rows, width = parts.shape
    return pl.pallas_call(
        total_kernel,
        out_shape=jax.ShapeDtypeStruct((rows, 2, width // 2), jnp.float32),
        in_specs=[VMEM],
        out_specs=VMEM,
        compiler_params=params(),
        name="total",
    )(parts)


def cost(queries, keys, heads, products, size):
    return pl.CostEstimate(
        flops=2 * products * heads * queries * keys * HEAD_DIM,
        bytes_accessed=size,
        transcendentals=heads * queries * keys,
    )


def face_bias(mask_ref):
    tile = lax.axis_index("tile")
    last = lax.axis_size("tile") - 1
    lower = jnp.where((mask_ref[0, 0] == 1) & (tile > 0), 0.0, NEG_LARGE)
    upper = jnp.where((mask_ref[0, 1] == 1) & (tile < last), 0.0, NEG_LARGE)
    even = tile % CORES == 0
    inner = jnp.where(even, upper, lower)
    outer = jnp.where(even, lower, upper)
    return inner.astype(jnp.float32), outer.astype(jnp.float32)


def columns(head, width):
    return [pl.ds(half * width + head * HEAD_DIM, HEAD_DIM) for half in range(2)]


def raised_stats(scores, grads):
    top = functools.reduce(jnp.maximum, [jnp.max(s, axis=0, keepdims=True) for s in scores])
    total = 0.0
    weighted = 0.0
    for s, g in zip(scores, grads):
        e = jnp.exp2(s - top)
        total = total + jnp.sum(e, axis=0, keepdims=True)
        weighted = weighted + jnp.sum(e * g, axis=0, keepdims=True)
    return top, total, weighted


def near_stats_kernel(mask_ref, pack_ref, own_ref, outer_ref, stat_ref):
    rows = stat_ref.shape[1]
    width = pack_ref.shape[1] // 2
    _, outer_bias = face_bias(mask_ref)
    for head in range(width // HEAD_DIM):
        at = columns(head, width)
        q, d = pack_ref[:rows, at[0]], pack_ref[:rows, at[1]]
        scores, grads = [], []
        for ref, bias in ((own_ref, None), (outer_ref, outer_bias)):
            s = dot(ref[:, at[0]], q, NT) * (SCALE * LOG2E)
            scores.append(s if bias is None else s + bias)
            grads.append(dot(ref[:, at[1]], d, NT))
        for i, row in enumerate(raised_stats(scores, grads)):
            stat_ref[pl.ds(3 * head + i, 1), :] = row


def near_stats(mask, pack, own, outer):
    rows, width = own.shape
    return pl.pallas_call(
        near_stats_kernel,
        out_shape=jax.ShapeDtypeStruct((STAT_ROWS, rows), jnp.float32),
        in_specs=[SMEM, VMEM, VMEM, VMEM],
        out_specs=VMEM,
        compiler_params=params(),
        cost_estimate=HEAVY,
        name="near_stats",
    )(mask, pack, own, outer)


def inner_stats_kernel(mask_ref, pack_ref, swap_ref, stat_ref):
    rows = stat_ref.shape[1]
    width = pack_ref.shape[1] // 2
    inner_bias, _ = face_bias(mask_ref)
    for head in range(width // HEAD_DIM):
        at = columns(head, width)
        s = dot(swap_ref[rows:, at[0]], pack_ref[:rows, at[0]], NT) * (SCALE * LOG2E) + inner_bias
        g = dot(swap_ref[rows:, at[1]], pack_ref[:rows, at[1]], NT)
        for i, row in enumerate(raised_stats([s], [g])):
            stat_ref[pl.ds(3 * head + i, 1), :] = row


def inner_stats(mask, pack, swap):
    rows, heads = pack.shape[0] - FACE, pack.shape[1] // 2 // HEAD_DIM
    return pl.pallas_call(
        inner_stats_kernel,
        out_shape=jax.ShapeDtypeStruct((STAT_ROWS, rows), jnp.float32),
        in_specs=[SMEM, VMEM, VMEM],
        out_specs=VMEM,
        compiler_params=params(),
        cost_estimate=cost(rows, FACE, heads, 2, 4 * pack.size),
        name="inner_stats",
    )(mask, pack, swap)


def cond_stats_kernel(pack_ref, swap_ref, cond_ref, near_ref, inner_ref, stat_ref):
    rows = near_ref.shape[1]
    width = pack_ref.shape[1] // 2
    stat_ref[0] = near_ref[...]
    stat_ref[1] = inner_ref[...]
    for head in range(width // HEAD_DIM):
        at = columns(head, width)
        key, value = cond_ref[:, at[0]], cond_ref[:, at[1]]
        for side, ref in enumerate((pack_ref, swap_ref)):
            s = dot(key, ref[:rows, at[0]], NT) * (SCALE * LOG2E)
            g = dot(value, ref[:rows, at[1]], NT)
            for i, row in enumerate(raised_stats([s], [g])):
                stat_ref[2 + side, pl.ds(3 * head + i, 1), :] = row


def cond_stats(pack, swap, cond, near, inner):
    rows = near.shape[1]
    heads = pack.shape[1] // 2 // HEAD_DIM
    return pl.pallas_call(
        cond_stats_kernel,
        out_shape=jax.ShapeDtypeStruct((4, STAT_ROWS, rows), jnp.float32),
        in_specs=[VMEM] * 5,
        out_specs=VMEM,
        compiler_params=params(),
        cost_estimate=cost(2 * rows, cond.shape[0], heads, 2, 6 * pack.size),
        name="cond_stats",
    )(pack, swap, cond, near, inner)


def head_pass(key, value, q, d, level, delta, bias=None):
    s = dot(key, q, NT) * (SCALE * LOG2E)
    if bias is not None:
        s = s + bias
    p = jnp.exp2(s - level)
    grad_s = (p * (dot(value, d, NT) - delta)).astype(jnp.bfloat16)
    return p.astype(jnp.bfloat16), grad_s


def grads_kernel(pack_ref, swap_ref, cond_ref, mine_ref, their_ref, out_ref, row_ref):
    rows = row_ref.shape[1]
    width = pack_ref.shape[1] // 2
    for head in range(width // HEAD_DIM):
        at = columns(head, width)
        key, value = cond_ref[:, at[0]], cond_ref[:, at[1]]
        grad_k = 0.0
        grad_v = 0.0
        for side, ref in enumerate((pack_ref, swap_ref)):
            home, away = (mine_ref, their_ref) if side == 0 else (their_ref, mine_ref)
            parts = [
                [r[pl.ds(3 * head + i, 1), :] for i in range(3)]
                for r in (home.at[0], home.at[1], home.at[2], away.at[3])
            ]
            top = functools.reduce(jnp.maximum, [p[0] for p in parts])
            total = sum(p[1] * jnp.exp2(p[0] - top) for p in parts)
            weighted = sum(p[2] * jnp.exp2(p[0] - top) for p in parts)
            level = top + jnp.log2(total)
            delta = weighted / total
            q, d = ref[:rows, at[0]], ref[:rows, at[1]]
            p, grad_s = head_pass(key, value, q, d, level, delta)
            grad_k = grad_k + dot(grad_s, q)
            grad_v = grad_v + dot(p, d)
            if side == 0:
                row_ref[pl.ds(2 * head, 1), :] = level
                row_ref[pl.ds(2 * head + 1, 1), :] = delta
        out_ref[:, at[0]] = (grad_k * SCALE).astype(out_ref.dtype)
        out_ref[:, at[1]] = grad_v.astype(out_ref.dtype)


def grads_pass(pack, swap, cond, mine, theirs):
    rows = mine.shape[2]
    heads = pack.shape[1] // 2 // HEAD_DIM
    return pl.pallas_call(
        grads_kernel,
        out_shape=(
            jax.ShapeDtypeStruct(cond.shape, jnp.bfloat16),
            jax.ShapeDtypeStruct((STAT_ROWS, rows), jnp.float32),
        ),
        in_specs=[VMEM] * 5,
        out_specs=(VMEM,) * 2,
        compiler_params=params(),
        cost_estimate=cost(2 * rows, cond.shape[0], heads, 4, 8 * pack.size),
        name="grads_pass",
    )(pack, swap, cond, mine, theirs)


def face_kernel(mask_ref, pack_ref, row_ref, swap_ref, outer_ref, to_inner_ref, to_outer_ref):
    rows = row_ref.shape[1]
    width = pack_ref.shape[1] // 2
    inner_bias, outer_bias = face_bias(mask_ref)
    faces = (
        (swap_ref.at[rows:], inner_bias, to_inner_ref),
        (outer_ref, outer_bias, to_outer_ref),
    )
    for head in range(width // HEAD_DIM):
        at = columns(head, width)
        q, d = pack_ref[:rows, at[0]], pack_ref[:rows, at[1]]
        level, delta = [row_ref[pl.ds(2 * head + i, 1), :] for i in range(2)]
        for face, bias, out in faces:
            p, grad_s = head_pass(face[:, at[0]], face[:, at[1]], q, d, level, delta, bias)
            out[:, at[0]] = (dot(grad_s, q) * SCALE).astype(out.dtype)
            out[:, at[1]] = dot(p, d).astype(out.dtype)


def face_pass(mask, pack, row_stats, swap, outer):
    rows = row_stats.shape[1]
    heads = pack.shape[1] // 2 // HEAD_DIM
    face = jax.ShapeDtypeStruct(outer.shape, jnp.bfloat16)
    return pl.pallas_call(
        face_kernel,
        out_shape=(face, face),
        in_specs=[SMEM] + [VMEM] * 4,
        out_specs=(VMEM,) * 2,
        compiler_params=params(),
        cost_estimate=cost(rows, 2 * FACE, heads, 6, 10 * pack.size),
        name="face_pass",
    )(mask, pack, row_stats, swap, outer)


def own_kernel(
    mask_ref, pack_ref, row_ref, own_ref, swap_ref, outer_ref, cond_ref, far_cond_ref,
    att_ref, dq_ref, keep_ref,
):
    rows = row_ref.shape[1]
    width = pack_ref.shape[1] // 2
    inner_bias, outer_bias = face_bias(mask_ref)
    segments = (
        (own_ref, None),
        (swap_ref.at[rows:], inner_bias),
        (outer_ref, outer_bias),
        (cond_ref, None),
        (far_cond_ref, None),
    )
    for head in range(width // HEAD_DIM):
        at = columns(head, width)
        q, d = pack_ref[:rows, at[0]], pack_ref[:rows, at[1]]
        level, delta = [row_ref[pl.ds(2 * head + i, 1), :] for i in range(2)]
        att = 0.0
        grad_q = 0.0
        for ref, bias in segments:
            key, value = ref[:, at[0]], ref[:, at[1]]
            p, grad_s = head_pass(key, value, q, d, level, delta, bias)
            if ref is own_ref:
                keep_ref[:, at[0]] = dot(grad_s, q) * SCALE
                keep_ref[:, at[1]] = dot(p, d)
            att = att + dot(value, p, TN)
            grad_q = grad_q + dot(key, grad_s, TN)
        att_ref[:, at[0]] = att.T.astype(jnp.bfloat16)
        dq_ref[:, at[0]] = (grad_q * SCALE).T.astype(jnp.bfloat16)


def own_pass(mask, pack, row_stats, own, swap, outer, cond, far_cond):
    rows, width = own.shape
    heads = width // 2 // HEAD_DIM
    keys = rows + 2 * FACE + 2 * cond.shape[0]
    half = jax.ShapeDtypeStruct((rows, width // 2), jnp.bfloat16)
    return pl.pallas_call(
        own_kernel,
        out_shape=(half, half, jax.ShapeDtypeStruct((rows, width), jnp.float32)),
        in_specs=[SMEM] + [VMEM] * 7,
        out_specs=(VMEM,) * 3,
        compiler_params=params(),
        cost_estimate=cost(rows, keys, heads, 5, 16 * own.size),
        name="own_pass",
    )(mask, pack, row_stats, own, swap, outer, cond, far_cond)


def per_device(queries, keys_values, cond_kv, face_mask, d_out):
    size = lax.axis_size("tile")
    rows, width = queries.shape
    chips = size // CORES
    cond_rows = cond_kv.shape[0]
    even = lax.axis_index("tile") % CORES == 0
    swap_cores = other_core(size)
    across = [(t, t + 1) for t in range(1, size - 1, CORES)]
    across += [(b, a) for a, b in across]

    copies = spread(cond_kv, chips)
    cond = lax.all_to_all(copies, "tile", 0, 0, axis_index_groups=same_core(size), tiled=True)
    cond = cond.reshape(chips * cond_rows, 2 * width)

    own = lax.optimization_barrier(keys_values.reshape(rows, 2 * width))
    edge = lax.dynamic_slice_in_dim(own, jnp.where(even, 0, rows - FACE), FACE, axis=0)
    outer = lax.ppermute(edge, "tile", across)
    pack = pack_queries(queries, d_out, own)
    swap = lax.ppermute(pack, "tile", swap_cores)
    near = near_stats(face_mask, pack, own, outer)
    inner = inner_stats(face_mask, pack, swap)

    mine = cond_stats(pack, swap, cond, near, inner)
    theirs = lax.ppermute(mine, "tile", swap_cores)
    grads, row_stats = grads_pass(pack, swap, cond, mine, theirs)
    blocks = grads.reshape(chips, cond_rows, 2 * width)
    parts = lax.all_to_all(blocks, "tile", 0, 0, axis_index_groups=same_core(size), tiled=True)
    grad_cond = total(parts)

    late_cond, row_stats = lax.optimization_barrier((cond, row_stats))
    far_cond = lax.ppermute(late_cond, "tile", swap_cores)
    far_cond, row_stats = lax.optimization_barrier((far_cond, row_stats))
    to_inner, to_outer = face_pass(face_mask, pack, row_stats, swap, outer)
    to_inner, to_outer, row_stats = lax.optimization_barrier((to_inner, to_outer, row_stats))
    from_outer = lax.ppermute(to_outer, "tile", across)
    from_inner = lax.ppermute(to_inner, "tile", swap_cores)
    attended, grad_q, keep = own_pass(
        face_mask, pack, row_stats, own, swap, outer, cond, far_cond
    )
    low = jnp.where(even, from_outer, from_inner).astype(jnp.float32)
    high = jnp.where(even, from_inner, from_outer).astype(jnp.float32)
    keep = keep + jnp.concatenate([low, high], axis=0)
    grad_kv = keep.astype(jnp.bfloat16).reshape(rows, 2, width)
    return attended, grad_q, grad_kv, grad_cond


def solution(mesh):
    return jax.shard_map(
        per_device,
        mesh=mesh,
        in_specs=(
            P("tile", "head"),
            P("tile", None, "head"),
            P("tile", None, "head"),
            P("tile", None),
            P("tile", "head"),
        ),
        out_specs=(
            P("tile", "head"),
            P("tile", "head"),
            P("tile", None, "head"),
            P("tile", None, "head"),
        ),
        check_vma=False,
    )
```

```python
import functools

import jax
import jax.numpy as jnp
from jax import lax
from jax.experimental import pallas as pl
from jax.experimental.pallas import tpu as pltpu
from jax.sharding import PartitionSpec as P

HEAD_DIM = 128
FACE = 128
CORES = 2
RUN = 4
SCALE = HEAD_DIM**-0.5
LOG2E = 1.4426950408889634
NEG_LARGE = -1e30
STAT_ROWS = 16

NT = (((1,), (1,)), ((), ()))
TN = (((0,), (0,)), ((), ()))


def dot(a, b, dims=(((1,), (0,)), ((), ()))):
    return lax.dot_general(a, b, dims, preferred_element_type=jnp.float32)


def other_core(size):
    return [(t, t ^ 1) for t in range(size)]


def place(z, y, core):
    return (z * RUN + y) * CORES + core


def same_core(size):
    half = size // (2 * RUN * CORES)
    return [
        [place(z + far * half, y, c) for z in range(half) for y in range(RUN) for far in range(2)]
        for c in range(CORES)
    ]


def half_rings(size):
    half = size // (2 * RUN * CORES)
    groups = []
    for c in range(CORES):
        shift = c * half // 2
        for far in range(2):
            zs = [z + half * ((z < shift) != bool(far)) for z in range(half)]
            groups.append([place(z, y, c) for z in zs for y in range(RUN)])
    return groups


def half_way(size):
    return [(t, (t + size // 2) % size) for t in range(size)]


def params(mib=16):
    return pltpu.CompilerParams(vmem_limit_bytes=mib * 1024 * 1024)


VMEM = pl.BlockSpec(memory_space=pltpu.VMEM)
LIGHT = pl.CostEstimate(flops=1, bytes_accessed=1, transcendentals=0)
HEAVY = pl.CostEstimate(flops=6_000_000_000, bytes_accessed=0, transcendentals=0)
SMEM = pl.BlockSpec(memory_space=pltpu.SMEM)


def spread_kernel(cond_ref, far_ref, out_ref):
    rows = cond_ref.shape[0]
    first = lax.axis_index("tile") < lax.axis_size("tile") // 2
    mine, theirs = [
        jnp.concatenate([ref[:, 0, :], ref[:, 1, :]], axis=1) for ref in (cond_ref, far_ref)
    ]
    pair = jnp.concatenate(
        [jnp.where(first, mine, theirs), jnp.where(first, theirs, mine)], axis=0
    )
    out_ref[...] = jnp.broadcast_to(pair[None], out_ref.shape)


def spread(cond_kv, far, copies):
    rows, _, width = cond_kv.shape
    return pl.pallas_call(
        spread_kernel,
        out_shape=jax.ShapeDtypeStruct((copies, 2 * rows, 2 * width), cond_kv.dtype),
        in_specs=[VMEM, VMEM],
        out_specs=VMEM,
        compiler_params=params(),
        name="spread",
    )(cond_kv, far)


def pack_kernel(q_ref, d_ref, own_ref, out_ref):
    rows, width = q_ref.shape
    even = lax.axis_index("tile") % CORES == 0
    start = pl.multiple_of(jnp.where(even, rows - FACE, 0), FACE)
    out_ref[:rows, :width] = q_ref[...]
    out_ref[:rows, width:] = d_ref[...]
    out_ref[rows:, :] = own_ref[pl.ds(start, FACE), :]


def pack_queries(queries, d_out, own):
    rows, width = own.shape
    return pl.pallas_call(
        pack_kernel,
        out_shape=jax.ShapeDtypeStruct((rows + FACE, width), own.dtype),
        in_specs=[VMEM] * 3,
        out_specs=VMEM,
        compiler_params=params(),
        cost_estimate=LIGHT,
        name="pack_queries",
    )(queries, d_out, own)


def total_kernel(parts_ref, out_ref):
    width = out_ref.shape[2]
    total = jnp.sum(parts_ref[...].astype(jnp.float32), axis=0)
    out_ref[:, 0, :] = total[:, :width]
    out_ref[:, 1, :] = total[:, width:]


def total(parts):
    _, rows, width = parts.shape
    return pl.pallas_call(
        total_kernel,
        out_shape=jax.ShapeDtypeStruct((rows, 2, width // 2), jnp.float32),
        in_specs=[VMEM],
        out_specs=VMEM,
        compiler_params=params(),
        name="total",
    )(parts)


def cost(queries, keys, heads, products, size):
    return pl.CostEstimate(
        flops=2 * products * heads * queries * keys * HEAD_DIM,
        bytes_accessed=size,
        transcendentals=heads * queries * keys,
    )


def face_bias(mask_ref):
    tile = lax.axis_index("tile")
    last = lax.axis_size("tile") - 1
    lower = jnp.where((mask_ref[0, 0] == 1) & (tile > 0), 0.0, NEG_LARGE)
    upper = jnp.where((mask_ref[0, 1] == 1) & (tile < last), 0.0, NEG_LARGE)
    even = tile % CORES == 0
    inner = jnp.where(even, upper, lower)
    outer = jnp.where(even, lower, upper)
    return inner.astype(jnp.float32), outer.astype(jnp.float32)


def columns(head, width):
    return [pl.ds(half * width + head * HEAD_DIM, HEAD_DIM) for half in range(2)]


def raised_stats(scores, grads):
    top = functools.reduce(jnp.maximum, [jnp.max(s, axis=0, keepdims=True) for s in scores])
    total = 0.0
    weighted = 0.0
    for s, g in zip(scores, grads):
        e = jnp.exp2(s - top)
        total = total + jnp.sum(e, axis=0, keepdims=True)
        weighted = weighted + jnp.sum(e * g, axis=0, keepdims=True)
    return top, total, weighted


def near_stats_kernel(mask_ref, pack_ref, own_ref, outer_ref, stat_ref):
    rows = stat_ref.shape[1]
    width = pack_ref.shape[1] // 2
    _, outer_bias = face_bias(mask_ref)
    for head in range(width // HEAD_DIM):
        at = columns(head, width)
        q, d = pack_ref[:rows, at[0]], pack_ref[:rows, at[1]]
        scores, grads = [], []
        for ref, bias in ((own_ref, None), (outer_ref, outer_bias)):
            s = dot(ref[:, at[0]], q, NT) * (SCALE * LOG2E)
            scores.append(s if bias is None else s + bias)
            grads.append(dot(ref[:, at[1]], d, NT))
        for i, row in enumerate(raised_stats(scores, grads)):
            stat_ref[pl.ds(3 * head + i, 1), :] = row


def near_stats(mask, pack, own, outer):
    rows, width = own.shape
    return pl.pallas_call(
        near_stats_kernel,
        out_shape=jax.ShapeDtypeStruct((STAT_ROWS, rows), jnp.float32),
        in_specs=[SMEM, VMEM, VMEM, VMEM],
        out_specs=VMEM,
        compiler_params=params(),
        cost_estimate=HEAVY,
        name="near_stats",
    )(mask, pack, own, outer)


def inner_stats_kernel(mask_ref, pack_ref, swap_ref, stat_ref):
    rows = stat_ref.shape[1]
    width = pack_ref.shape[1] // 2
    inner_bias, _ = face_bias(mask_ref)
    for head in range(width // HEAD_DIM):
        at = columns(head, width)
        s = dot(swap_ref[rows:, at[0]], pack_ref[:rows, at[0]], NT) * (SCALE * LOG2E) + inner_bias
        g = dot(swap_ref[rows:, at[1]], pack_ref[:rows, at[1]], NT)
        for i, row in enumerate(raised_stats([s], [g])):
            stat_ref[pl.ds(3 * head + i, 1), :] = row


def inner_stats(mask, pack, swap):
    rows, heads = pack.shape[0] - FACE, pack.shape[1] // 2 // HEAD_DIM
    return pl.pallas_call(
        inner_stats_kernel,
        out_shape=jax.ShapeDtypeStruct((STAT_ROWS, rows), jnp.float32),
        in_specs=[SMEM, VMEM, VMEM],
        out_specs=VMEM,
        compiler_params=params(),
        cost_estimate=cost(rows, FACE, heads, 2, 4 * pack.size),
        name="inner_stats",
    )(mask, pack, swap)


def cond_stats_kernel(pack_ref, swap_ref, cond_ref, near_ref, inner_ref, stat_ref):
    rows = near_ref.shape[1]
    width = pack_ref.shape[1] // 2
    stat_ref[0] = near_ref[...]
    stat_ref[1] = inner_ref[...]
    for head in range(width // HEAD_DIM):
        at = columns(head, width)
        key, value = cond_ref[:, at[0]], cond_ref[:, at[1]]
        for side, ref in enumerate((pack_ref, swap_ref)):
            s = dot(key, ref[:rows, at[0]], NT) * (SCALE * LOG2E)
            g = dot(value, ref[:rows, at[1]], NT)
            for i, row in enumerate(raised_stats([s], [g])):
                stat_ref[2 + side, pl.ds(3 * head + i, 1), :] = row


def cond_stats(pack, swap, cond, near, inner):
    rows = near.shape[1]
    heads = pack.shape[1] // 2 // HEAD_DIM
    return pl.pallas_call(
        cond_stats_kernel,
        out_shape=jax.ShapeDtypeStruct((4, STAT_ROWS, rows), jnp.float32),
        in_specs=[VMEM] * 5,
        out_specs=VMEM,
        compiler_params=params(),
        cost_estimate=cost(2 * rows, cond.shape[0], heads, 2, 6 * pack.size),
        name="cond_stats",
    )(pack, swap, cond, near, inner)


def head_pass(key, value, q, d, level, delta, bias=None):
    s = dot(key, q, NT) * (SCALE * LOG2E)
    if bias is not None:
        s = s + bias
    p = jnp.exp2(s - level)
    grad_s = (p * (dot(value, d, NT) - delta)).astype(jnp.bfloat16)
    return p.astype(jnp.bfloat16), grad_s


def grads_kernel(pack_ref, swap_ref, cond_ref, mine_ref, their_ref, out_ref, row_ref):
    rows = row_ref.shape[1]
    width = pack_ref.shape[1] // 2
    for head in range(width // HEAD_DIM):
        at = columns(head, width)
        key, value = cond_ref[:, at[0]], cond_ref[:, at[1]]
        grad_k = 0.0
        grad_v = 0.0
        for side, ref in enumerate((pack_ref, swap_ref)):
            home, away = (mine_ref, their_ref) if side == 0 else (their_ref, mine_ref)
            parts = [
                [r[pl.ds(3 * head + i, 1), :] for i in range(3)]
                for r in (home.at[0], home.at[1], home.at[2], away.at[3])
            ]
            top = functools.reduce(jnp.maximum, [p[0] for p in parts])
            total = sum(p[1] * jnp.exp2(p[0] - top) for p in parts)
            weighted = sum(p[2] * jnp.exp2(p[0] - top) for p in parts)
            level = top + jnp.log2(total)
            delta = weighted / total
            q, d = ref[:rows, at[0]], ref[:rows, at[1]]
            p, grad_s = head_pass(key, value, q, d, level, delta)
            grad_k = grad_k + dot(grad_s, q)
            grad_v = grad_v + dot(p, d)
            if side == 0:
                row_ref[pl.ds(2 * head, 1), :] = level
                row_ref[pl.ds(2 * head + 1, 1), :] = delta
        out_ref[:, at[0]] = (grad_k * SCALE).astype(out_ref.dtype)
        out_ref[:, at[1]] = grad_v.astype(out_ref.dtype)


def grads_pass(pack, swap, cond, mine, theirs):
    rows = mine.shape[2]
    heads = pack.shape[1] // 2 // HEAD_DIM
    return pl.pallas_call(
        grads_kernel,
        out_shape=(
            jax.ShapeDtypeStruct(cond.shape, jnp.bfloat16),
            jax.ShapeDtypeStruct((STAT_ROWS, rows), jnp.float32),
        ),
        in_specs=[VMEM] * 5,
        out_specs=(VMEM,) * 2,
        compiler_params=params(),
        cost_estimate=cost(2 * rows, cond.shape[0], heads, 4, 8 * pack.size),
        name="grads_pass",
    )(pack, swap, cond, mine, theirs)


def face_kernel(mask_ref, pack_ref, row_ref, swap_ref, outer_ref, to_inner_ref, to_outer_ref):
    rows = row_ref.shape[1]
    width = pack_ref.shape[1] // 2
    inner_bias, outer_bias = face_bias(mask_ref)
    faces = (
        (swap_ref.at[rows:], inner_bias, to_inner_ref),
        (outer_ref, outer_bias, to_outer_ref),
    )
    for head in range(width // HEAD_DIM):
        at = columns(head, width)
        q, d = pack_ref[:rows, at[0]], pack_ref[:rows, at[1]]
        level, delta = [row_ref[pl.ds(2 * head + i, 1), :] for i in range(2)]
        for face, bias, out in faces:
            p, grad_s = head_pass(face[:, at[0]], face[:, at[1]], q, d, level, delta, bias)
            out[:, at[0]] = (dot(grad_s, q) * SCALE).astype(out.dtype)
            out[:, at[1]] = dot(p, d).astype(out.dtype)


def face_pass(mask, pack, row_stats, swap, outer):
    rows = row_stats.shape[1]
    heads = pack.shape[1] // 2 // HEAD_DIM
    face = jax.ShapeDtypeStruct(outer.shape, jnp.bfloat16)
    return pl.pallas_call(
        face_kernel,
        out_shape=(face, face),
        in_specs=[SMEM] + [VMEM] * 4,
        out_specs=(VMEM,) * 2,
        compiler_params=params(),
        cost_estimate=cost(rows, 2 * FACE, heads, 6, 10 * pack.size),
        name="face_pass",
    )(mask, pack, row_stats, swap, outer)


def own_kernel(
    mask_ref, pack_ref, row_ref, own_ref, swap_ref, outer_ref, cond_ref, far_cond_ref,
    att_ref, dq_ref, keep_ref,
):
    rows = row_ref.shape[1]
    width = pack_ref.shape[1] // 2
    inner_bias, outer_bias = face_bias(mask_ref)
    segments = (
        (own_ref, None),
        (swap_ref.at[rows:], inner_bias),
        (outer_ref, outer_bias),
        (cond_ref, None),
        (far_cond_ref, None),
    )
    for head in range(width // HEAD_DIM):
        at = columns(head, width)
        q, d = pack_ref[:rows, at[0]], pack_ref[:rows, at[1]]
        level, delta = [row_ref[pl.ds(2 * head + i, 1), :] for i in range(2)]
        att = 0.0
        grad_q = 0.0
        for ref, bias in segments:
            key, value = ref[:, at[0]], ref[:, at[1]]
            p, grad_s = head_pass(key, value, q, d, level, delta, bias)
            if ref is own_ref:
                keep_ref[:, at[0]] = dot(grad_s, q) * SCALE
                keep_ref[:, at[1]] = dot(p, d)
            att = att + dot(value, p, TN)
            grad_q = grad_q + dot(key, grad_s, TN)
        att_ref[:, at[0]] = att.T.astype(jnp.bfloat16)
        dq_ref[:, at[0]] = (grad_q * SCALE).T.astype(jnp.bfloat16)


def own_pass(mask, pack, row_stats, own, swap, outer, cond, far_cond):
    rows, width = own.shape
    heads = width // 2 // HEAD_DIM
    keys = rows + 2 * FACE + 2 * cond.shape[0]
    half = jax.ShapeDtypeStruct((rows, width // 2), jnp.bfloat16)
    return pl.pallas_call(
        own_kernel,
        out_shape=(half, half, jax.ShapeDtypeStruct((rows, width), jnp.float32)),
        in_specs=[SMEM] + [VMEM] * 7,
        out_specs=(VMEM,) * 3,
        compiler_params=params(),
        cost_estimate=cost(rows, keys, heads, 5, 16 * own.size),
        name="own_pass",
    )(mask, pack, row_stats, own, swap, outer, cond, far_cond)


def per_device(queries, keys_values, cond_kv, face_mask, d_out):
    size = lax.axis_size("tile")
    rows, width = queries.shape
    chips = size // CORES
    cond_rows = cond_kv.shape[0]
    even = lax.axis_index("tile") % CORES == 0
    swap_cores = other_core(size)
    across = [(t, t + 1) for t in range(1, size - 1, CORES)]
    across += [(b, a) for a, b in across]

    copies = spread(cond_kv, lax.ppermute(cond_kv, "tile", half_way(size)), chips // 2)
    cond = lax.all_to_all(copies, "tile", 0, 0, axis_index_groups=half_rings(size), tiled=True)
    cond = cond.reshape(chips * cond_rows, 2 * width)

    own = lax.optimization_barrier(keys_values.reshape(rows, 2 * width))
    edge = lax.dynamic_slice_in_dim(own, jnp.where(even, 0, rows - FACE), FACE, axis=0)
    outer = lax.ppermute(edge, "tile", across)
    pack = pack_queries(queries, d_out, own)
    swap = lax.ppermute(pack, "tile", swap_cores)
    near = near_stats(face_mask, pack, own, outer)
    inner = inner_stats(face_mask, pack, swap)

    mine = cond_stats(pack, swap, cond, near, inner)
    mine, late_cond = lax.optimization_barrier((mine, cond))
    theirs = lax.ppermute(mine, "tile", swap_cores)
    grads, row_stats = grads_pass(pack, swap, cond, mine, theirs)
    blocks = grads.reshape(chips, cond_rows, 2 * width)
    parts = lax.all_to_all(blocks, "tile", 0, 0, axis_index_groups=same_core(size), tiled=True)
    grad_cond = total(parts)

    far_cond = lax.ppermute(late_cond, "tile", swap_cores)
    far_cond, row_stats = lax.optimization_barrier((far_cond, row_stats))
    to_inner, to_outer = face_pass(face_mask, pack, row_stats, swap, outer)
    to_inner, to_outer, row_stats = lax.optimization_barrier((to_inner, to_outer, row_stats))
    from_outer = lax.ppermute(to_outer, "tile", across)
    from_inner = lax.ppermute(to_inner, "tile", swap_cores)
    attended, grad_q, keep = own_pass(
        face_mask, pack, row_stats, own, swap, outer, cond, far_cond
    )
    low = jnp.where(even, from_outer, from_inner).astype(jnp.float32)
    high = jnp.where(even, from_inner, from_outer).astype(jnp.float32)
    keep = keep + jnp.concatenate([low, high], axis=0)
    grad_kv = keep.astype(jnp.bfloat16).reshape(rows, 2, width)
    return attended, grad_q, grad_kv, grad_cond


def solution(mesh):
    return jax.shard_map(
        per_device,
        mesh=mesh,
        in_specs=(
            P("tile", "head"),
            P("tile", None, "head"),
            P("tile", None, "head"),
            P("tile", None),
            P("tile", "head"),
        ),
        out_specs=(
            P("tile", "head"),
            P("tile", "head"),
            P("tile", None, "head"),
            P("tile", None, "head"),
        ),
        check_vma=False,
    )
```

```python
import functools

import jax
import jax.numpy as jnp
from jax import lax
from jax.experimental import pallas as pl
from jax.experimental.pallas import tpu as pltpu
from jax.sharding import PartitionSpec as P

HEAD_DIM = 128
FACE = 128
CORES = 2
RUN = 4
STRIDE = 3
SCALE = HEAD_DIM**-0.5
LOG2E = 1.4426950408889634
NEG_LARGE = -1e30
STAT_ROWS = 16

NT = (((1,), (1,)), ((), ()))
TN = (((0,), (0,)), ((), ()))


def dot(a, b, dims=(((1,), (0,)), ((), ()))):
    return lax.dot_general(a, b, dims, preferred_element_type=jnp.float32)


def other_core(size):
    return [(t, t ^ 1) for t in range(size)]


def same_core(size):
    depth = size // (RUN * CORES)
    return [
        [((STRIDE * z % depth) * RUN + y) * CORES + c for y in range(RUN) for z in range(depth)]
        for c in range(CORES)
    ]


def params(mib=16):
    return pltpu.CompilerParams(vmem_limit_bytes=mib * 1024 * 1024)


VMEM = pl.BlockSpec(memory_space=pltpu.VMEM)
LIGHT = pl.CostEstimate(flops=1, bytes_accessed=1, transcendentals=0)
HEAVY = pl.CostEstimate(flops=6_000_000_000, bytes_accessed=0, transcendentals=0)
SMEM = pl.BlockSpec(memory_space=pltpu.SMEM)


def spread_kernel(cond_ref, out_ref):
    rows, _, width = cond_ref.shape
    flat = jnp.concatenate([cond_ref[:, 0, :], cond_ref[:, 1, :]], axis=1)
    out_ref[...] = jnp.broadcast_to(flat[None], out_ref.shape)


def spread(cond_kv, copies):
    rows, _, width = cond_kv.shape
    return pl.pallas_call(
        spread_kernel,
        out_shape=jax.ShapeDtypeStruct((copies, rows, 2 * width), cond_kv.dtype),
        in_specs=[VMEM],
        out_specs=VMEM,
        compiler_params=params(),
        name="spread",
    )(cond_kv)


def pack_kernel(q_ref, d_ref, own_ref, out_ref):
    rows, width = q_ref.shape
    even = lax.axis_index("tile") % CORES == 0
    start = pl.multiple_of(jnp.where(even, rows - FACE, 0), FACE)
    out_ref[:rows, :width] = q_ref[...]
    out_ref[:rows, width:] = d_ref[...]
    out_ref[rows:, :] = own_ref[pl.ds(start, FACE), :]


def pack_queries(queries, d_out, own):
    rows, width = own.shape
    return pl.pallas_call(
        pack_kernel,
        out_shape=jax.ShapeDtypeStruct((rows + FACE, width), own.dtype),
        in_specs=[VMEM] * 3,
        out_specs=VMEM,
        compiler_params=params(),
        cost_estimate=LIGHT,
        name="pack_queries",
    )(queries, d_out, own)


def total_kernel(parts_ref, out_ref):
    width = out_ref.shape[2]
    total = jnp.sum(parts_ref[...].astype(jnp.float32), axis=0)
    out_ref[:, 0, :] = total[:, :width]
    out_ref[:, 1, :] = total[:, width:]


def total(parts):
    _, rows, width = parts.shape
    return pl.pallas_call(
        total_kernel,
        out_shape=jax.ShapeDtypeStruct((rows, 2, width // 2), jnp.float32),
        in_specs=[VMEM],
        out_specs=VMEM,
        compiler_params=params(),
        name="total",
    )(parts)


def cost(queries, keys, heads, products, size):
    return pl.CostEstimate(
        flops=2 * products * heads * queries * keys * HEAD_DIM,
        bytes_accessed=size,
        transcendentals=heads * queries * keys,
    )


def face_bias(mask_ref):
    tile = lax.axis_index("tile")
    last = lax.axis_size("tile") - 1
    lower = jnp.where((mask_ref[0, 0] == 1) & (tile > 0), 0.0, NEG_LARGE)
    upper = jnp.where((mask_ref[0, 1] == 1) & (tile < last), 0.0, NEG_LARGE)
    even = tile % CORES == 0
    inner = jnp.where(even, upper, lower)
    outer = jnp.where(even, lower, upper)
    return inner.astype(jnp.float32), outer.astype(jnp.float32)


def columns(head, width):
    return [pl.ds(half * width + head * HEAD_DIM, HEAD_DIM) for half in range(2)]


def raised_stats(scores, grads):
    top = functools.reduce(jnp.maximum, [jnp.max(s, axis=0, keepdims=True) for s in scores])
    total = 0.0
    weighted = 0.0
    for s, g in zip(scores, grads):
        e = jnp.exp2(s - top)
        total = total + jnp.sum(e, axis=0, keepdims=True)
        weighted = weighted + jnp.sum(e * g, axis=0, keepdims=True)
    return top, total, weighted


def near_stats_kernel(mask_ref, pack_ref, own_ref, outer_ref, stat_ref):
    rows = stat_ref.shape[1]
    width = pack_ref.shape[1] // 2
    _, outer_bias = face_bias(mask_ref)
    for head in range(width // HEAD_DIM):
        at = columns(head, width)
        q, d = pack_ref[:rows, at[0]], pack_ref[:rows, at[1]]
        scores, grads = [], []
        for ref, bias in ((own_ref, None), (outer_ref, outer_bias)):
            s = dot(ref[:, at[0]], q, NT) * (SCALE * LOG2E)
            scores.append(s if bias is None else s + bias)
            grads.append(dot(ref[:, at[1]], d, NT))
        for i, row in enumerate(raised_stats(scores, grads)):
            stat_ref[pl.ds(3 * head + i, 1), :] = row


def near_stats(mask, pack, own, outer):
    rows, width = own.shape
    return pl.pallas_call(
        near_stats_kernel,
        out_shape=jax.ShapeDtypeStruct((STAT_ROWS, rows), jnp.float32),
        in_specs=[SMEM, VMEM, VMEM, VMEM],
        out_specs=VMEM,
        compiler_params=params(),
        cost_estimate=HEAVY,
        name="near_stats",
    )(mask, pack, own, outer)


def inner_stats_kernel(mask_ref, pack_ref, swap_ref, stat_ref):
    rows = stat_ref.shape[1]
    width = pack_ref.shape[1] // 2
    inner_bias, _ = face_bias(mask_ref)
    for head in range(width // HEAD_DIM):
        at = columns(head, width)
        s = dot(swap_ref[rows:, at[0]], pack_ref[:rows, at[0]], NT) * (SCALE * LOG2E) + inner_bias
        g = dot(swap_ref[rows:, at[1]], pack_ref[:rows, at[1]], NT)
        for i, row in enumerate(raised_stats([s], [g])):
            stat_ref[pl.ds(3 * head + i, 1), :] = row


def inner_stats(mask, pack, swap):
    rows, heads = pack.shape[0] - FACE, pack.shape[1] // 2 // HEAD_DIM
    return pl.pallas_call(
        inner_stats_kernel,
        out_shape=jax.ShapeDtypeStruct((STAT_ROWS, rows), jnp.float32),
        in_specs=[SMEM, VMEM, VMEM],
        out_specs=VMEM,
        compiler_params=params(),
        cost_estimate=cost(rows, FACE, heads, 2, 4 * pack.size),
        name="inner_stats",
    )(mask, pack, swap)


def cond_stats_kernel(pack_ref, swap_ref, cond_ref, near_ref, inner_ref, stat_ref):
    rows = near_ref.shape[1]
    width = pack_ref.shape[1] // 2
    stat_ref[0] = near_ref[...]
    stat_ref[1] = inner_ref[...]
    for head in range(width // HEAD_DIM):
        at = columns(head, width)
        key, value = cond_ref[:, at[0]], cond_ref[:, at[1]]
        for side, ref in enumerate((pack_ref, swap_ref)):
            s = dot(key, ref[:rows, at[0]], NT) * (SCALE * LOG2E)
            g = dot(value, ref[:rows, at[1]], NT)
            for i, row in enumerate(raised_stats([s], [g])):
                stat_ref[2 + side, pl.ds(3 * head + i, 1), :] = row


def cond_stats(pack, swap, cond, near, inner):
    rows = near.shape[1]
    heads = pack.shape[1] // 2 // HEAD_DIM
    return pl.pallas_call(
        cond_stats_kernel,
        out_shape=jax.ShapeDtypeStruct((4, STAT_ROWS, rows), jnp.float32),
        in_specs=[VMEM] * 5,
        out_specs=VMEM,
        compiler_params=params(),
        cost_estimate=cost(2 * rows, cond.shape[0], heads, 2, 6 * pack.size),
        name="cond_stats",
    )(pack, swap, cond, near, inner)


def head_pass(key, value, q, d, level, delta, bias=None):
    s = dot(key, q, NT) * (SCALE * LOG2E)
    if bias is not None:
        s = s + bias
    p = jnp.exp2(s - level)
    grad_s = (p * (dot(value, d, NT) - delta)).astype(jnp.bfloat16)
    return p.astype(jnp.bfloat16), grad_s


def grads_kernel(pack_ref, swap_ref, cond_ref, mine_ref, their_ref, out_ref, row_ref):
    rows = row_ref.shape[1]
    width = pack_ref.shape[1] // 2
    for head in range(width // HEAD_DIM):
        at = columns(head, width)
        key, value = cond_ref[:, at[0]], cond_ref[:, at[1]]
        grad_k = 0.0
        grad_v = 0.0
        for side, ref in enumerate((pack_ref, swap_ref)):
            home, away = (mine_ref, their_ref) if side == 0 else (their_ref, mine_ref)
            parts = [
                [r[pl.ds(3 * head + i, 1), :] for i in range(3)]
                for r in (home.at[0], home.at[1], home.at[2], away.at[3])
            ]
            top = functools.reduce(jnp.maximum, [p[0] for p in parts])
            total = sum(p[1] * jnp.exp2(p[0] - top) for p in parts)
            weighted = sum(p[2] * jnp.exp2(p[0] - top) for p in parts)
            level = top + jnp.log2(total)
            delta = weighted / total
            q, d = ref[:rows, at[0]], ref[:rows, at[1]]
            p, grad_s = head_pass(key, value, q, d, level, delta)
            grad_k = grad_k + dot(grad_s, q)
            grad_v = grad_v + dot(p, d)
            if side == 0:
                row_ref[pl.ds(2 * head, 1), :] = level
                row_ref[pl.ds(2 * head + 1, 1), :] = delta
        out_ref[:, at[0]] = (grad_k * SCALE).astype(out_ref.dtype)
        out_ref[:, at[1]] = grad_v.astype(out_ref.dtype)


def grads_pass(pack, swap, cond, mine, theirs):
    rows = mine.shape[2]
    heads = pack.shape[1] // 2 // HEAD_DIM
    return pl.pallas_call(
        grads_kernel,
        out_shape=(
            jax.ShapeDtypeStruct(cond.shape, jnp.bfloat16),
            jax.ShapeDtypeStruct((STAT_ROWS, rows), jnp.float32),
        ),
        in_specs=[VMEM] * 5,
        out_specs=(VMEM,) * 2,
        compiler_params=params(),
        cost_estimate=cost(2 * rows, cond.shape[0], heads, 4, 8 * pack.size),
        name="grads_pass",
    )(pack, swap, cond, mine, theirs)


def face_kernel(mask_ref, pack_ref, row_ref, swap_ref, outer_ref, to_inner_ref, to_outer_ref):
    rows = row_ref.shape[1]
    width = pack_ref.shape[1] // 2
    inner_bias, outer_bias = face_bias(mask_ref)
    faces = (
        (swap_ref.at[rows:], inner_bias, to_inner_ref),
        (outer_ref, outer_bias, to_outer_ref),
    )
    for head in range(width // HEAD_DIM):
        at = columns(head, width)
        q, d = pack_ref[:rows, at[0]], pack_ref[:rows, at[1]]
        level, delta = [row_ref[pl.ds(2 * head + i, 1), :] for i in range(2)]
        for face, bias, out in faces:
            p, grad_s = head_pass(face[:, at[0]], face[:, at[1]], q, d, level, delta, bias)
            out[:, at[0]] = (dot(grad_s, q) * SCALE).astype(out.dtype)
            out[:, at[1]] = dot(p, d).astype(out.dtype)


def face_pass(mask, pack, row_stats, swap, outer):
    rows = row_stats.shape[1]
    heads = pack.shape[1] // 2 // HEAD_DIM
    face = jax.ShapeDtypeStruct(outer.shape, jnp.bfloat16)
    return pl.pallas_call(
        face_kernel,
        out_shape=(face, face),
        in_specs=[SMEM] + [VMEM] * 4,
        out_specs=(VMEM,) * 2,
        compiler_params=params(),
        cost_estimate=cost(rows, 2 * FACE, heads, 6, 10 * pack.size),
        name="face_pass",
    )(mask, pack, row_stats, swap, outer)


def own_kernel(
    mask_ref, pack_ref, row_ref, own_ref, swap_ref, outer_ref, cond_ref, far_cond_ref,
    att_ref, dq_ref, keep_ref,
):
    rows = row_ref.shape[1]
    width = pack_ref.shape[1] // 2
    inner_bias, outer_bias = face_bias(mask_ref)
    segments = (
        (own_ref, None),
        (swap_ref.at[rows:], inner_bias),
        (outer_ref, outer_bias),
        (cond_ref, None),
        (far_cond_ref, None),
    )
    for head in range(width // HEAD_DIM):
        at = columns(head, width)
        q, d = pack_ref[:rows, at[0]], pack_ref[:rows, at[1]]
        level, delta = [row_ref[pl.ds(2 * head + i, 1), :] for i in range(2)]
        att = 0.0
        grad_q = 0.0
        for ref, bias in segments:
            key, value = ref[:, at[0]], ref[:, at[1]]
            p, grad_s = head_pass(key, value, q, d, level, delta, bias)
            if ref is own_ref:
                keep_ref[:, at[0]] = dot(grad_s, q) * SCALE
                keep_ref[:, at[1]] = dot(p, d)
            att = att + dot(value, p, TN)
            grad_q = grad_q + dot(key, grad_s, TN)
        att_ref[:, at[0]] = att.T.astype(jnp.bfloat16)
        dq_ref[:, at[0]] = (grad_q * SCALE).T.astype(jnp.bfloat16)


def own_pass(mask, pack, row_stats, own, swap, outer, cond, far_cond):
    rows, width = own.shape
    heads = width // 2 // HEAD_DIM
    keys = rows + 2 * FACE + 2 * cond.shape[0]
    half = jax.ShapeDtypeStruct((rows, width // 2), jnp.bfloat16)
    return pl.pallas_call(
        own_kernel,
        out_shape=(half, half, jax.ShapeDtypeStruct((rows, width), jnp.float32)),
        in_specs=[SMEM] + [VMEM] * 7,
        out_specs=(VMEM,) * 3,
        compiler_params=params(),
        cost_estimate=cost(rows, keys, heads, 5, 16 * own.size),
        name="own_pass",
    )(mask, pack, row_stats, own, swap, outer, cond, far_cond)


def per_device(queries, keys_values, cond_kv, face_mask, d_out):
    size = lax.axis_size("tile")
    rows, width = queries.shape
    chips = size // CORES
    cond_rows = cond_kv.shape[0]
    even = lax.axis_index("tile") % CORES == 0
    swap_cores = other_core(size)
    across = [(t, t + 1) for t in range(1, size - 1, CORES)]
    across += [(b, a) for a, b in across]

    copies = spread(cond_kv, chips)
    cond = lax.all_to_all(copies, "tile", 0, 0, axis_index_groups=same_core(size), tiled=True)
    cond = cond.reshape(chips * cond_rows, 2 * width)

    own = lax.optimization_barrier(keys_values.reshape(rows, 2 * width))
    edge = lax.dynamic_slice_in_dim(own, jnp.where(even, 0, rows - FACE), FACE, axis=0)
    outer = lax.ppermute(edge, "tile", across)
    pack = pack_queries(queries, d_out, own)
    swap = lax.ppermute(pack, "tile", swap_cores)
    near = near_stats(face_mask, pack, own, outer)
    inner = inner_stats(face_mask, pack, swap)

    mine = cond_stats(pack, swap, cond, near, inner)
    theirs = lax.ppermute(mine, "tile", swap_cores)
    grads, row_stats = grads_pass(pack, swap, cond, mine, theirs)
    blocks = grads.reshape(chips, cond_rows, 2 * width)
    parts = lax.all_to_all(blocks, "tile", 0, 0, axis_index_groups=same_core(size), tiled=True)
    grad_cond = total(parts)

    late_cond, row_stats = lax.optimization_barrier((cond, row_stats))
    far_cond = lax.ppermute(late_cond, "tile", swap_cores)
    to_inner, to_outer = face_pass(face_mask, pack, row_stats, swap, outer)
    to_inner, to_outer, row_stats = lax.optimization_barrier((to_inner, to_outer, row_stats))
    from_outer = lax.ppermute(to_outer, "tile", across)
    from_inner = lax.ppermute(to_inner, "tile", swap_cores)
    attended, grad_q, keep = own_pass(
        face_mask, pack, row_stats, own, swap, outer, cond, far_cond
    )
    low = jnp.where(even, from_outer, from_inner).astype(jnp.float32)
    high = jnp.where(even, from_inner, from_outer).astype(jnp.float32)
    keep = keep + jnp.concatenate([low, high], axis=0)
    grad_kv = keep.astype(jnp.bfloat16).reshape(rows, 2, width)
    return attended, grad_q, grad_kv, grad_cond


def solution(mesh):
    return jax.shard_map(
        per_device,
        mesh=mesh,
        in_specs=(
            P("tile", "head"),
            P("tile", None, "head"),
            P("tile", None, "head"),
            P("tile", None),
            P("tile", "head"),
        ),
        out_specs=(
            P("tile", "head"),
            P("tile", "head"),
            P("tile", None, "head"),
            P("tile", None, "head"),
        ),
        check_vma=False,
    )
```

```python
import functools

import jax
import jax.numpy as jnp
from jax import lax
from jax.experimental import pallas as pl
from jax.experimental.pallas import tpu as pltpu
from jax.sharding import PartitionSpec as P

HEAD_DIM = 128
FACE = 128
CORES = 2
RUN = 4
STRIDE = 3
SCALE = HEAD_DIM**-0.5
LOG2E = 1.4426950408889634
NEG_LARGE = -1e30
STAT_ROWS = 16

NT = (((1,), (1,)), ((), ()))
TN = (((0,), (0,)), ((), ()))


def dot(a, b, dims=(((1,), (0,)), ((), ()))):
    return lax.dot_general(a, b, dims, preferred_element_type=jnp.float32)


def other_core(size):
    return [(t, t ^ 1) for t in range(size)]


def same_core(size):
    depth = size // (RUN * CORES)
    return [
        [((STRIDE * z % depth) * RUN + y) * CORES + c for y in range(RUN) for z in range(depth)]
        for c in range(CORES)
    ]


def params(mib=16):
    return pltpu.CompilerParams(vmem_limit_bytes=mib * 1024 * 1024)


VMEM = pl.BlockSpec(memory_space=pltpu.VMEM)
LIGHT = pl.CostEstimate(flops=1, bytes_accessed=1, transcendentals=0)
HEAVY = pl.CostEstimate(flops=6_000_000_000, bytes_accessed=0, transcendentals=0)
SMEM = pl.BlockSpec(memory_space=pltpu.SMEM)


def spread_kernel(cond_ref, out_ref):
    rows, _, width = cond_ref.shape
    flat = jnp.concatenate([cond_ref[:, 0, :], cond_ref[:, 1, :]], axis=1)
    out_ref[...] = jnp.broadcast_to(flat[None], out_ref.shape)


def spread(cond_kv, copies):
    rows, _, width = cond_kv.shape
    return pl.pallas_call(
        spread_kernel,
        out_shape=jax.ShapeDtypeStruct((copies, rows, 2 * width), cond_kv.dtype),
        in_specs=[VMEM],
        out_specs=VMEM,
        compiler_params=params(),
        name="spread",
    )(cond_kv)


def pack_kernel(q_ref, d_ref, own_ref, out_ref):
    rows, width = q_ref.shape
    even = lax.axis_index("tile") % CORES == 0
    start = pl.multiple_of(jnp.where(even, rows - FACE, 0), FACE)
    out_ref[:rows, :width] = q_ref[...]
    out_ref[:rows, width:] = d_ref[...]
    out_ref[rows:, :] = own_ref[pl.ds(start, FACE), :]


def pack_queries(queries, d_out, own):
    rows, width = own.shape
    return pl.pallas_call(
        pack_kernel,
        out_shape=jax.ShapeDtypeStruct((rows + FACE, width), own.dtype),
        in_specs=[VMEM] * 3,
        out_specs=VMEM,
        compiler_params=params(),
        cost_estimate=LIGHT,
        name="pack_queries",
    )(queries, d_out, own)


def total_kernel(parts_ref, out_ref):
    width = out_ref.shape[2]
    total = jnp.sum(parts_ref[...].astype(jnp.float32), axis=0)
    out_ref[:, 0, :] = total[:, :width]
    out_ref[:, 1, :] = total[:, width:]


def total(parts):
    _, rows, width = parts.shape
    return pl.pallas_call(
        total_kernel,
        out_shape=jax.ShapeDtypeStruct((rows, 2, width // 2), jnp.float32),
        in_specs=[VMEM],
        out_specs=VMEM,
        compiler_params=params(),
        name="total",
    )(parts)


def cost(queries, keys, heads, products, size):
    return pl.CostEstimate(
        flops=2 * products * heads * queries * keys * HEAD_DIM,
        bytes_accessed=size,
        transcendentals=heads * queries * keys,
    )


def face_bias(mask_ref):
    tile = lax.axis_index("tile")
    last = lax.axis_size("tile") - 1
    lower = jnp.where((mask_ref[0, 0] == 1) & (tile > 0), 0.0, NEG_LARGE)
    upper = jnp.where((mask_ref[0, 1] == 1) & (tile < last), 0.0, NEG_LARGE)
    even = tile % CORES == 0
    inner = jnp.where(even, upper, lower)
    outer = jnp.where(even, lower, upper)
    return inner.astype(jnp.float32), outer.astype(jnp.float32)


def columns(head, width):
    return [pl.ds(half * width + head * HEAD_DIM, HEAD_DIM) for half in range(2)]


def raised_stats(scores, grads):
    top = functools.reduce(jnp.maximum, [jnp.max(s, axis=0, keepdims=True) for s in scores])
    total = 0.0
    weighted = 0.0
    for s, g in zip(scores, grads):
        e = jnp.exp2(s - top)
        total = total + jnp.sum(e, axis=0, keepdims=True)
        weighted = weighted + jnp.sum(e * g, axis=0, keepdims=True)
    return top, total, weighted


def near_stats_kernel(mask_ref, pack_ref, own_ref, outer_ref, stat_ref):
    rows = stat_ref.shape[1]
    width = pack_ref.shape[1] // 2
    _, outer_bias = face_bias(mask_ref)
    for head in range(width // HEAD_DIM):
        at = columns(head, width)
        q, d = pack_ref[:rows, at[0]], pack_ref[:rows, at[1]]
        scores, grads = [], []
        for ref, bias in ((own_ref, None), (outer_ref, outer_bias)):
            s = dot(ref[:, at[0]], q, NT) * (SCALE * LOG2E)
            scores.append(s if bias is None else s + bias)
            grads.append(dot(ref[:, at[1]], d, NT))
        for i, row in enumerate(raised_stats(scores, grads)):
            stat_ref[pl.ds(3 * head + i, 1), :] = row


def near_stats(mask, pack, own, outer):
    rows, width = own.shape
    return pl.pallas_call(
        near_stats_kernel,
        out_shape=jax.ShapeDtypeStruct((STAT_ROWS, rows), jnp.float32),
        in_specs=[SMEM, VMEM, VMEM, VMEM],
        out_specs=VMEM,
        compiler_params=params(),
        cost_estimate=HEAVY,
        name="near_stats",
    )(mask, pack, own, outer)


def inner_stats_kernel(mask_ref, pack_ref, swap_ref, stat_ref):
    rows = stat_ref.shape[1]
    width = pack_ref.shape[1] // 2
    inner_bias, _ = face_bias(mask_ref)
    for head in range(width // HEAD_DIM):
        at = columns(head, width)
        s = dot(swap_ref[rows:, at[0]], pack_ref[:rows, at[0]], NT) * (SCALE * LOG2E) + inner_bias
        g = dot(swap_ref[rows:, at[1]], pack_ref[:rows, at[1]], NT)
        for i, row in enumerate(raised_stats([s], [g])):
            stat_ref[pl.ds(3 * head + i, 1), :] = row


def inner_stats(mask, pack, swap):
    rows = pack.shape[0] - FACE
    return pl.pallas_call(
        inner_stats_kernel,
        out_shape=jax.ShapeDtypeStruct((STAT_ROWS, rows), jnp.float32),
        in_specs=[SMEM, VMEM, VMEM],
        out_specs=VMEM,
        compiler_params=params(),
        cost_estimate=LIGHT,
        name="inner_stats",
    )(mask, pack, swap)


def cond_stats_kernel(pack_ref, swap_ref, cond_ref, near_ref, inner_ref, stat_ref):
    rows = near_ref.shape[1]
    width = pack_ref.shape[1] // 2
    stat_ref[0] = near_ref[...]
    stat_ref[1] = inner_ref[...]
    for head in range(width // HEAD_DIM):
        at = columns(head, width)
        key, value = cond_ref[:, at[0]], cond_ref[:, at[1]]
        for side, ref in enumerate((pack_ref, swap_ref)):
            s = dot(key, ref[:rows, at[0]], NT) * (SCALE * LOG2E)
            g = dot(value, ref[:rows, at[1]], NT)
            for i, row in enumerate(raised_stats([s], [g])):
                stat_ref[2 + side, pl.ds(3 * head + i, 1), :] = row


def cond_stats(pack, swap, cond, near, inner):
    rows = near.shape[1]
    heads = pack.shape[1] // 2 // HEAD_DIM
    return pl.pallas_call(
        cond_stats_kernel,
        out_shape=jax.ShapeDtypeStruct((4, STAT_ROWS, rows), jnp.float32),
        in_specs=[VMEM] * 5,
        out_specs=VMEM,
        compiler_params=params(),
        cost_estimate=cost(2 * rows, cond.shape[0], heads, 2, 6 * pack.size),
        name="cond_stats",
    )(pack, swap, cond, near, inner)


def head_pass(key, value, q, d, level, delta, bias=None):
    s = dot(key, q, NT) * (SCALE * LOG2E)
    if bias is not None:
        s = s + bias
    p = jnp.exp2(s - level)
    grad_s = (p * (dot(value, d, NT) - delta)).astype(jnp.bfloat16)
    return p.astype(jnp.bfloat16), grad_s


def grads_kernel(pack_ref, swap_ref, cond_ref, mine_ref, their_ref, out_ref, row_ref):
    rows = row_ref.shape[1]
    width = pack_ref.shape[1] // 2
    for head in range(width // HEAD_DIM):
        at = columns(head, width)
        key, value = cond_ref[:, at[0]], cond_ref[:, at[1]]
        grad_k = 0.0
        grad_v = 0.0
        for side, ref in enumerate((pack_ref, swap_ref)):
            home, away = (mine_ref, their_ref) if side == 0 else (their_ref, mine_ref)
            parts = [
                [r[pl.ds(3 * head + i, 1), :] for i in range(3)]
                for r in (home.at[0], home.at[1], home.at[2], away.at[3])
            ]
            top = functools.reduce(jnp.maximum, [p[0] for p in parts])
            total = sum(p[1] * jnp.exp2(p[0] - top) for p in parts)
            weighted = sum(p[2] * jnp.exp2(p[0] - top) for p in parts)
            level = top + jnp.log2(total)
            delta = weighted / total
            q, d = ref[:rows, at[0]], ref[:rows, at[1]]
            p, grad_s = head_pass(key, value, q, d, level, delta)
            grad_k = grad_k + dot(grad_s, q)
            grad_v = grad_v + dot(p, d)
            if side == 0:
                row_ref[pl.ds(2 * head, 1), :] = level
                row_ref[pl.ds(2 * head + 1, 1), :] = delta
        out_ref[:, at[0]] = (grad_k * SCALE).astype(out_ref.dtype)
        out_ref[:, at[1]] = grad_v.astype(out_ref.dtype)


def grads_pass(pack, swap, cond, mine, theirs):
    rows = mine.shape[2]
    heads = pack.shape[1] // 2 // HEAD_DIM
    return pl.pallas_call(
        grads_kernel,
        out_shape=(
            jax.ShapeDtypeStruct(cond.shape, jnp.bfloat16),
            jax.ShapeDtypeStruct((STAT_ROWS, rows), jnp.float32),
        ),
        in_specs=[VMEM] * 5,
        out_specs=(VMEM,) * 2,
        compiler_params=params(),
        cost_estimate=cost(2 * rows, cond.shape[0], heads, 4, 8 * pack.size),
        name="grads_pass",
    )(pack, swap, cond, mine, theirs)


def face_kernel(
    mask_ref, pack_ref, row_ref, swap_ref, outer_ref, _gate_ref, to_inner_ref, to_outer_ref
):
    rows = row_ref.shape[1]
    width = pack_ref.shape[1] // 2
    inner_bias, outer_bias = face_bias(mask_ref)
    faces = (
        (swap_ref.at[rows:], inner_bias, to_inner_ref),
        (outer_ref, outer_bias, to_outer_ref),
    )
    for head in range(width // HEAD_DIM):
        at = columns(head, width)
        q, d = pack_ref[:rows, at[0]], pack_ref[:rows, at[1]]
        level, delta = [row_ref[pl.ds(2 * head + i, 1), :] for i in range(2)]
        for face, bias, out in faces:
            p, grad_s = head_pass(face[:, at[0]], face[:, at[1]], q, d, level, delta, bias)
            out[:, at[0]] = (dot(grad_s, q) * SCALE).astype(out.dtype)
            out[:, at[1]] = dot(p, d).astype(out.dtype)


def face_pass(mask, pack, row_stats, swap, outer, gate):
    rows = row_stats.shape[1]
    heads = pack.shape[1] // 2 // HEAD_DIM
    face = jax.ShapeDtypeStruct(outer.shape, jnp.bfloat16)
    return pl.pallas_call(
        face_kernel,
        out_shape=(face, face),
        in_specs=[SMEM] + [VMEM] * 5,
        out_specs=(VMEM,) * 2,
        compiler_params=params(),
        cost_estimate=cost(rows, 2 * FACE, heads, 6, 10 * pack.size),
        name="face_pass",
    )(mask, pack, row_stats, swap, outer, gate)


def own_kernel(
    mask_ref, pack_ref, row_ref, own_ref, swap_ref, outer_ref, cond_ref, far_cond_ref,
    att_ref, dq_ref, keep_ref,
):
    rows = row_ref.shape[1]
    width = pack_ref.shape[1] // 2
    inner_bias, outer_bias = face_bias(mask_ref)
    segments = (
        (own_ref, None),
        (swap_ref.at[rows:], inner_bias),
        (outer_ref, outer_bias),
        (cond_ref, None),
        (far_cond_ref, None),
    )
    for head in range(width // HEAD_DIM):
        at = columns(head, width)
        q, d = pack_ref[:rows, at[0]], pack_ref[:rows, at[1]]
        level, delta = [row_ref[pl.ds(2 * head + i, 1), :] for i in range(2)]
        att = 0.0
        grad_q = 0.0
        for ref, bias in segments:
            key, value = ref[:, at[0]], ref[:, at[1]]
            p, grad_s = head_pass(key, value, q, d, level, delta, bias)
            if ref is own_ref:
                keep_ref[:, at[0]] = dot(grad_s, q) * SCALE
                keep_ref[:, at[1]] = dot(p, d)
            att = att + dot(value, p, TN)
            grad_q = grad_q + dot(key, grad_s, TN)
        att_ref[:, at[0]] = att.T.astype(jnp.bfloat16)
        dq_ref[:, at[0]] = (grad_q * SCALE).T.astype(jnp.bfloat16)


def own_pass(mask, pack, row_stats, own, swap, outer, cond, far_cond):
    rows, width = own.shape
    heads = width // 2 // HEAD_DIM
    keys = rows + 2 * FACE + 2 * cond.shape[0]
    half = jax.ShapeDtypeStruct((rows, width // 2), jnp.bfloat16)
    return pl.pallas_call(
        own_kernel,
        out_shape=(half, half, jax.ShapeDtypeStruct((rows, width), jnp.float32)),
        in_specs=[SMEM] + [VMEM] * 7,
        out_specs=(VMEM,) * 3,
        compiler_params=params(),
        cost_estimate=cost(rows, keys, heads, 5, 16 * own.size),
        name="own_pass",
    )(mask, pack, row_stats, own, swap, outer, cond, far_cond)


def per_device(queries, keys_values, cond_kv, face_mask, d_out):
    size = lax.axis_size("tile")
    rows, width = queries.shape
    chips = size // CORES
    cond_rows = cond_kv.shape[0]
    even = lax.axis_index("tile") % CORES == 0
    swap_cores = other_core(size)
    across = [(t, t + 1) for t in range(1, size - 1, CORES)]
    across += [(b, a) for a, b in across]

    copies = spread(cond_kv, chips)
    cond = lax.all_to_all(copies, "tile", 0, 0, axis_index_groups=same_core(size), tiled=True)
    cond = cond.reshape(chips * cond_rows, 2 * width)

    own = lax.optimization_barrier(keys_values.reshape(rows, 2 * width))
    edge = lax.dynamic_slice_in_dim(own, jnp.where(even, 0, rows - FACE), FACE, axis=0)
    outer = lax.ppermute(edge, "tile", across)
    pack = pack_queries(queries, d_out, own)
    swap = lax.ppermute(pack, "tile", swap_cores)
    near = near_stats(face_mask, pack, own, outer)
    inner = inner_stats(face_mask, pack, swap)

    mine = cond_stats(pack, swap, cond, near, inner)
    theirs = lax.ppermute(mine, "tile", swap_cores)
    grads, row_stats = grads_pass(pack, swap, cond, mine, theirs)
    blocks = grads.reshape(chips, cond_rows, 2 * width)
    parts = lax.all_to_all(blocks, "tile", 0, 0, axis_index_groups=same_core(size), tiled=True)
    grad_cond = total(parts)

    gate = lax.ppermute(row_stats, "tile", [(0, 1)])
    late_cond, gate = lax.optimization_barrier((cond, gate))
    far_cond = lax.ppermute(late_cond, "tile", swap_cores)
    to_inner, to_outer = face_pass(face_mask, pack, row_stats, swap, outer, gate)
    to_inner, to_outer, row_stats = lax.optimization_barrier((to_inner, to_outer, row_stats))
    from_outer = lax.ppermute(to_outer, "tile", across)
    from_inner = lax.ppermute(to_inner, "tile", swap_cores)
    attended, grad_q, keep = own_pass(
        face_mask, pack, row_stats, own, swap, outer, cond, far_cond
    )
    low = jnp.where(even, from_outer, from_inner).astype(jnp.float32)
    high = jnp.where(even, from_inner, from_outer).astype(jnp.float32)
    keep = keep + jnp.concatenate([low, high], axis=0)
    grad_kv = keep.astype(jnp.bfloat16).reshape(rows, 2, width)
    return attended, grad_q, grad_kv, grad_cond


def solution(mesh):
    return jax.shard_map(
        per_device,
        mesh=mesh,
        in_specs=(
            P("tile", "head"),
            P("tile", None, "head"),
            P("tile", None, "head"),
            P("tile", None),
            P("tile", "head"),
        ),
        out_specs=(
            P("tile", "head"),
            P("tile", "head"),
            P("tile", None, "head"),
            P("tile", None, "head"),
        ),
        check_vma=False,
    )
```

```python
import functools

import jax
import jax.numpy as jnp
from jax import lax
from jax.experimental import pallas as pl
from jax.experimental.pallas import tpu as pltpu
from jax.sharding import PartitionSpec as P

HEAD_DIM = 128
FACE = 128
CORES = 2
RUN = 4
STRIDE = 3
SCALE = HEAD_DIM**-0.5
LOG2E = 1.4426950408889634
NEG_LARGE = -1e30
STAT_ROWS = 16

NT = (((1,), (1,)), ((), ()))
TN = (((0,), (0,)), ((), ()))


def dot(a, b, dims=(((1,), (0,)), ((), ()))):
    return lax.dot_general(a, b, dims, preferred_element_type=jnp.float32)


def other_core(size):
    return [(t, t ^ 1) for t in range(size)]


def same_core(size):
    depth = size // (RUN * CORES)
    return [
        [((STRIDE * z % depth) * RUN + y) * CORES + c for y in range(RUN) for z in range(depth)]
        for c in range(CORES)
    ]


def params(mib=16):
    return pltpu.CompilerParams(vmem_limit_bytes=mib * 1024 * 1024)


VMEM = pl.BlockSpec(memory_space=pltpu.VMEM)
LIGHT = pl.CostEstimate(flops=1, bytes_accessed=1, transcendentals=0)
HEAVY = pl.CostEstimate(flops=6_000_000_000, bytes_accessed=0, transcendentals=0)
SMEM = pl.BlockSpec(memory_space=pltpu.SMEM)


def spread_kernel(cond_ref, out_ref):
    rows, _, width = cond_ref.shape
    flat = jnp.concatenate([cond_ref[:, 0, :], cond_ref[:, 1, :]], axis=1)
    out_ref[...] = jnp.broadcast_to(flat[None], out_ref.shape)


def spread(cond_kv, copies):
    rows, _, width = cond_kv.shape
    return pl.pallas_call(
        spread_kernel,
        out_shape=jax.ShapeDtypeStruct((copies, rows, 2 * width), cond_kv.dtype),
        in_specs=[VMEM],
        out_specs=VMEM,
        compiler_params=params(),
        name="spread",
    )(cond_kv)


def pack_kernel(q_ref, d_ref, own_ref, out_ref):
    rows, width = q_ref.shape
    even = lax.axis_index("tile") % CORES == 0
    start = pl.multiple_of(jnp.where(even, rows - FACE, 0), FACE)
    out_ref[:rows, :width] = q_ref[...]
    out_ref[:rows, width:] = d_ref[...]
    out_ref[rows:, :] = own_ref[pl.ds(start, FACE), :]


def pack_queries(queries, d_out, own):
    rows, width = own.shape
    return pl.pallas_call(
        pack_kernel,
        out_shape=jax.ShapeDtypeStruct((rows + FACE, width), own.dtype),
        in_specs=[VMEM] * 3,
        out_specs=VMEM,
        compiler_params=params(),
        cost_estimate=LIGHT,
        name="pack_queries",
    )(queries, d_out, own)


def total_kernel(parts_ref, out_ref):
    width = out_ref.shape[2]
    total = jnp.sum(parts_ref[...].astype(jnp.float32), axis=0)
    out_ref[:, 0, :] = total[:, :width]
    out_ref[:, 1, :] = total[:, width:]


def total(parts):
    _, rows, width = parts.shape
    return pl.pallas_call(
        total_kernel,
        out_shape=jax.ShapeDtypeStruct((rows, 2, width // 2), jnp.float32),
        in_specs=[VMEM],
        out_specs=VMEM,
        compiler_params=params(),
        name="total",
    )(parts)


def cost(queries, keys, heads, products, size):
    return pl.CostEstimate(
        flops=2 * products * heads * queries * keys * HEAD_DIM,
        bytes_accessed=size,
        transcendentals=heads * queries * keys,
    )


def face_bias(mask_ref):
    tile = lax.axis_index("tile")
    last = lax.axis_size("tile") - 1
    lower = jnp.where((mask_ref[0, 0] == 1) & (tile > 0), 0.0, NEG_LARGE)
    upper = jnp.where((mask_ref[0, 1] == 1) & (tile < last), 0.0, NEG_LARGE)
    even = tile % CORES == 0
    inner = jnp.where(even, upper, lower)
    outer = jnp.where(even, lower, upper)
    return inner.astype(jnp.float32), outer.astype(jnp.float32)


def columns(head, width):
    return [pl.ds(half * width + head * HEAD_DIM, HEAD_DIM) for half in range(2)]


def raised_stats(scores, grads):
    top = functools.reduce(jnp.maximum, [jnp.max(s, axis=0, keepdims=True) for s in scores])
    total = 0.0
    weighted = 0.0
    for s, g in zip(scores, grads):
        e = jnp.exp2(s - top)
        total = total + jnp.sum(e, axis=0, keepdims=True)
        weighted = weighted + jnp.sum(e * g, axis=0, keepdims=True)
    return top, total, weighted


def near_stats_kernel(mask_ref, pack_ref, own_ref, outer_ref, stat_ref):
    rows = stat_ref.shape[1]
    width = pack_ref.shape[1] // 2
    _, outer_bias = face_bias(mask_ref)
    for head in range(width // HEAD_DIM):
        at = columns(head, width)
        q, d = pack_ref[:rows, at[0]], pack_ref[:rows, at[1]]
        scores, grads = [], []
        for ref, bias in ((own_ref, None), (outer_ref, outer_bias)):
            s = dot(ref[:, at[0]], q, NT) * (SCALE * LOG2E)
            scores.append(s if bias is None else s + bias)
            grads.append(dot(ref[:, at[1]], d, NT))
        for i, row in enumerate(raised_stats(scores, grads)):
            stat_ref[pl.ds(3 * head + i, 1), :] = row


def near_stats(mask, pack, own, outer):
    rows, width = own.shape
    return pl.pallas_call(
        near_stats_kernel,
        out_shape=jax.ShapeDtypeStruct((STAT_ROWS, rows), jnp.float32),
        in_specs=[SMEM, VMEM, VMEM, VMEM],
        out_specs=VMEM,
        compiler_params=params(),
        cost_estimate=HEAVY,
        name="near_stats",
    )(mask, pack, own, outer)


def inner_stats_kernel(mask_ref, pack_ref, swap_ref, stat_ref):
    rows = stat_ref.shape[1]
    width = pack_ref.shape[1] // 2
    inner_bias, _ = face_bias(mask_ref)
    for head in range(width // HEAD_DIM):
        at = columns(head, width)
        s = dot(swap_ref[rows:, at[0]], pack_ref[:rows, at[0]], NT) * (SCALE * LOG2E) + inner_bias
        g = dot(swap_ref[rows:, at[1]], pack_ref[:rows, at[1]], NT)
        for i, row in enumerate(raised_stats([s], [g])):
            stat_ref[pl.ds(3 * head + i, 1), :] = row


def inner_stats(mask, pack, swap):
    rows, heads = pack.shape[0] - FACE, pack.shape[1] // 2 // HEAD_DIM
    return pl.pallas_call(
        inner_stats_kernel,
        out_shape=jax.ShapeDtypeStruct((STAT_ROWS, rows), jnp.float32),
        in_specs=[SMEM, VMEM, VMEM],
        out_specs=VMEM,
        compiler_params=params(),
        cost_estimate=cost(rows, FACE, heads, 2, 4 * pack.size),
        name="inner_stats",
    )(mask, pack, swap)


def cond_stats_kernel(pack_ref, swap_ref, cond_ref, near_ref, inner_ref, stat_ref):
    rows = near_ref.shape[1]
    width = pack_ref.shape[1] // 2
    stat_ref[0] = near_ref[...]
    stat_ref[1] = inner_ref[...]
    for head in range(width // HEAD_DIM):
        at = columns(head, width)
        key, value = cond_ref[:, at[0]], cond_ref[:, at[1]]
        for side, ref in enumerate((pack_ref, swap_ref)):
            s = dot(key, ref[:rows, at[0]], NT) * (SCALE * LOG2E)
            g = dot(value, ref[:rows, at[1]], NT)
            for i, row in enumerate(raised_stats([s], [g])):
                stat_ref[2 + side, pl.ds(3 * head + i, 1), :] = row


def cond_stats(pack, swap, cond, near, inner):
    rows = near.shape[1]
    heads = pack.shape[1] // 2 // HEAD_DIM
    return pl.pallas_call(
        cond_stats_kernel,
        out_shape=jax.ShapeDtypeStruct((4, STAT_ROWS, rows), jnp.float32),
        in_specs=[VMEM] * 5,
        out_specs=VMEM,
        compiler_params=params(),
        cost_estimate=cost(2 * rows, cond.shape[0], heads, 2, 6 * pack.size),
        name="cond_stats",
    )(pack, swap, cond, near, inner)


def head_pass(key, value, q, d, level, delta, bias=None):
    s = dot(key, q, NT) * (SCALE * LOG2E)
    if bias is not None:
        s = s + bias
    p = jnp.exp2(s - level)
    grad_s = (p * (dot(value, d, NT) - delta)).astype(jnp.bfloat16)
    return p.astype(jnp.bfloat16), grad_s


def grads_kernel(pack_ref, swap_ref, cond_ref, mine_ref, their_ref, out_ref, row_ref):
    rows = row_ref.shape[1]
    width = pack_ref.shape[1] // 2
    for head in range(width // HEAD_DIM):
        at = columns(head, width)
        key, value = cond_ref[:, at[0]], cond_ref[:, at[1]]
        grad_k = 0.0
        grad_v = 0.0
        for side, ref in enumerate((pack_ref, swap_ref)):
            home, away = (mine_ref, their_ref) if side == 0 else (their_ref, mine_ref)
            parts = [
                [r[pl.ds(3 * head + i, 1), :] for i in range(3)]
                for r in (home.at[0], home.at[1], home.at[2], away.at[3])
            ]
            top = functools.reduce(jnp.maximum, [p[0] for p in parts])
            total = sum(p[1] * jnp.exp2(p[0] - top) for p in parts)
            weighted = sum(p[2] * jnp.exp2(p[0] - top) for p in parts)
            level = top + jnp.log2(total)
            delta = weighted / total
            q, d = ref[:rows, at[0]], ref[:rows, at[1]]
            p, grad_s = head_pass(key, value, q, d, level, delta)
            grad_k = grad_k + dot(grad_s, q)
            grad_v = grad_v + dot(p, d)
            if side == 0:
                row_ref[pl.ds(2 * head, 1), :] = level
                row_ref[pl.ds(2 * head + 1, 1), :] = delta
        out_ref[:, at[0]] = (grad_k * SCALE).astype(out_ref.dtype)
        out_ref[:, at[1]] = grad_v.astype(out_ref.dtype)


def grads_pass(pack, swap, cond, mine, theirs):
    rows = mine.shape[2]
    heads = pack.shape[1] // 2 // HEAD_DIM
    return pl.pallas_call(
        grads_kernel,
        out_shape=(
            jax.ShapeDtypeStruct(cond.shape, jnp.bfloat16),
            jax.ShapeDtypeStruct((STAT_ROWS, rows), jnp.float32),
        ),
        in_specs=[VMEM] * 5,
        out_specs=(VMEM,) * 2,
        compiler_params=params(),
        cost_estimate=cost(2 * rows, cond.shape[0], heads, 4, 8 * pack.size),
        name="grads_pass",
    )(pack, swap, cond, mine, theirs)


def face_kernel(mask_ref, pack_ref, row_ref, swap_ref, outer_ref, to_inner_ref, to_outer_ref):
    rows = row_ref.shape[1]
    width = pack_ref.shape[1] // 2
    inner_bias, outer_bias = face_bias(mask_ref)
    faces = (
        (swap_ref.at[rows:], inner_bias, to_inner_ref),
        (outer_ref, outer_bias, to_outer_ref),
    )
    for head in range(width // HEAD_DIM):
        at = columns(head, width)
        q, d = pack_ref[:rows, at[0]], pack_ref[:rows, at[1]]
        level, delta = [row_ref[pl.ds(2 * head + i, 1), :] for i in range(2)]
        for face, bias, out in faces:
            p, grad_s = head_pass(face[:, at[0]], face[:, at[1]], q, d, level, delta, bias)
            out[:, at[0]] = (dot(grad_s, q) * SCALE).astype(out.dtype)
            out[:, at[1]] = dot(p, d).astype(out.dtype)


def face_pass(mask, pack, row_stats, swap, outer):
    rows = row_stats.shape[1]
    face = jax.ShapeDtypeStruct(outer.shape, jnp.bfloat16)
    return pl.pallas_call(
        face_kernel,
        out_shape=(face, face),
        in_specs=[SMEM] + [VMEM] * 4,
        out_specs=(VMEM,) * 2,
        compiler_params=params(),
        cost_estimate=LIGHT,
        name="face_pass",
    )(mask, pack, row_stats, swap, outer)


def own_kernel(
    mask_ref, pack_ref, row_ref, own_ref, swap_ref, outer_ref, cond_ref, far_cond_ref,
    att_ref, dq_ref, keep_ref,
):
    rows = row_ref.shape[1]
    width = pack_ref.shape[1] // 2
    inner_bias, outer_bias = face_bias(mask_ref)
    segments = (
        (own_ref, None),
        (swap_ref.at[rows:], inner_bias),
        (outer_ref, outer_bias),
        (cond_ref, None),
        (far_cond_ref, None),
    )
    for head in range(width // HEAD_DIM):
        at = columns(head, width)
        q, d = pack_ref[:rows, at[0]], pack_ref[:rows, at[1]]
        level, delta = [row_ref[pl.ds(2 * head + i, 1), :] for i in range(2)]
        att = 0.0
        grad_q = 0.0
        for ref, bias in segments:
            key, value = ref[:, at[0]], ref[:, at[1]]
            p, grad_s = head_pass(key, value, q, d, level, delta, bias)
            if ref is own_ref:
                keep_ref[:, at[0]] = dot(grad_s, q) * SCALE
                keep_ref[:, at[1]] = dot(p, d)
            att = att + dot(value, p, TN)
            grad_q = grad_q + dot(key, grad_s, TN)
        att_ref[:, at[0]] = att.T.astype(jnp.bfloat16)
        dq_ref[:, at[0]] = (grad_q * SCALE).T.astype(jnp.bfloat16)


def own_pass(mask, pack, row_stats, own, swap, outer, cond, far_cond):
    rows, width = own.shape
    half = jax.ShapeDtypeStruct((rows, width // 2), jnp.bfloat16)
    return pl.pallas_call(
        own_kernel,
        out_shape=(half, half, jax.ShapeDtypeStruct((rows, width), jnp.float32)),
        in_specs=[SMEM] + [VMEM] * 7,
        out_specs=(VMEM,) * 3,
        compiler_params=params(),
        cost_estimate=LIGHT,
        name="own_pass",
    )(mask, pack, row_stats, own, swap, outer, cond, far_cond)


def per_device(queries, keys_values, cond_kv, face_mask, d_out):
    size = lax.axis_size("tile")
    rows, width = queries.shape
    chips = size // CORES
    cond_rows = cond_kv.shape[0]
    even = lax.axis_index("tile") % CORES == 0
    swap_cores = other_core(size)
    across = [(t, t + 1) for t in range(1, size - 1, CORES)]
    across += [(b, a) for a, b in across]

    copies = spread(cond_kv, chips)
    cond = lax.all_to_all(copies, "tile", 0, 0, axis_index_groups=same_core(size), tiled=True)
    cond = cond.reshape(chips * cond_rows, 2 * width)

    own = lax.optimization_barrier(keys_values.reshape(rows, 2 * width))
    edge = lax.dynamic_slice_in_dim(own, jnp.where(even, 0, rows - FACE), FACE, axis=0)
    outer = lax.ppermute(edge, "tile", across)
    pack = pack_queries(queries, d_out, own)
    swap = lax.ppermute(pack, "tile", swap_cores)
    near = near_stats(face_mask, pack, own, outer)
    inner = inner_stats(face_mask, pack, swap)

    mine = cond_stats(pack, swap, cond, near, inner)
    theirs = lax.ppermute(mine, "tile", swap_cores)
    grads, row_stats = grads_pass(pack, swap, cond, mine, theirs)
    blocks = grads.reshape(chips, cond_rows, 2 * width)
    parts = lax.all_to_all(blocks, "tile", 0, 0, axis_index_groups=same_core(size), tiled=True)
    grad_cond = total(parts)

    late_cond, row_stats = lax.optimization_barrier((cond, row_stats))
    far_cond = lax.ppermute(late_cond, "tile", swap_cores)
    to_inner, to_outer = face_pass(face_mask, pack, row_stats, swap, outer)
    from_outer = lax.ppermute(to_outer, "tile", across)
    from_inner = lax.ppermute(to_inner, "tile", swap_cores)
    attended, grad_q, keep = own_pass(
        face_mask, pack, row_stats, own, swap, outer, cond, far_cond
    )
    low = jnp.where(even, from_outer, from_inner).astype(jnp.float32)
    high = jnp.where(even, from_inner, from_outer).astype(jnp.float32)
    keep = keep + jnp.concatenate([low, high], axis=0)
    grad_kv = keep.astype(jnp.bfloat16).reshape(rows, 2, width)
    return attended, grad_q, grad_kv, grad_cond


def solution(mesh):
    return jax.shard_map(
        per_device,
        mesh=mesh,
        in_specs=(
            P("tile", "head"),
            P("tile", None, "head"),
            P("tile", None, "head"),
            P("tile", None),
            P("tile", "head"),
        ),
        out_specs=(
            P("tile", "head"),
            P("tile", "head"),
            P("tile", None, "head"),
            P("tile", None, "head"),
        ),
        check_vma=False,
    )
```

```python
import functools

import jax
import jax.numpy as jnp
from jax import lax
from jax.experimental import pallas as pl
from jax.experimental.pallas import tpu as pltpu
from jax.sharding import PartitionSpec as P

HEAD_DIM = 128
FACE = 128
CORES = 2
RUN = 4
STRIDE = 3
SCALE = HEAD_DIM**-0.5
LOG2E = 1.4426950408889634
NEG_LARGE = -1e30
STAT_ROWS = 16

NT = (((1,), (1,)), ((), ()))
TN = (((0,), (0,)), ((), ()))


def dot(a, b, dims=(((1,), (0,)), ((), ()))):
    return lax.dot_general(a, b, dims, preferred_element_type=jnp.float32)


def other_core(size):
    return [(t, t ^ 1) for t in range(size)]


def same_core(size):
    depth = size // (RUN * CORES)
    return [
        [((STRIDE * z % depth) * RUN + y) * CORES + c for y in range(RUN) for z in range(depth)]
        for c in range(CORES)
    ]


def params(mib=16):
    return pltpu.CompilerParams(vmem_limit_bytes=mib * 1024 * 1024)


VMEM = pl.BlockSpec(memory_space=pltpu.VMEM)
LIGHT = pl.CostEstimate(flops=1, bytes_accessed=1, transcendentals=0)
HEAVY = pl.CostEstimate(flops=6_000_000_000, bytes_accessed=0, transcendentals=0)
SMEM = pl.BlockSpec(memory_space=pltpu.SMEM)


def spread_kernel(cond_ref, out_ref):
    rows, _, width = cond_ref.shape
    flat = jnp.concatenate([cond_ref[:, 0, :], cond_ref[:, 1, :]], axis=1)
    out_ref[...] = jnp.broadcast_to(flat[None], out_ref.shape)


def spread(cond_kv, copies):
    rows, _, width = cond_kv.shape
    return pl.pallas_call(
        spread_kernel,
        out_shape=jax.ShapeDtypeStruct((copies, rows, 2 * width), cond_kv.dtype),
        in_specs=[VMEM],
        out_specs=VMEM,
        compiler_params=params(),
        name="spread",
    )(cond_kv)


def pack_kernel(q_ref, d_ref, own_ref, out_ref):
    rows, width = q_ref.shape
    even = lax.axis_index("tile") % CORES == 0
    start = pl.multiple_of(jnp.where(even, rows - FACE, 0), FACE)
    out_ref[:rows, :width] = q_ref[...]
    out_ref[:rows, width:] = d_ref[...]
    out_ref[rows:, :] = own_ref[pl.ds(start, FACE), :]


def pack_queries(queries, d_out, own):
    rows, width = own.shape
    return pl.pallas_call(
        pack_kernel,
        out_shape=jax.ShapeDtypeStruct((rows + FACE, width), own.dtype),
        in_specs=[VMEM] * 3,
        out_specs=VMEM,
        compiler_params=params(),
        cost_estimate=LIGHT,
        name="pack_queries",
    )(queries, d_out, own)


def total_kernel(parts_ref, out_ref):
    width = out_ref.shape[2]
    total = jnp.sum(parts_ref[...].astype(jnp.float32), axis=0)
    out_ref[:, 0, :] = total[:, :width]
    out_ref[:, 1, :] = total[:, width:]


def total(parts):
    _, rows, width = parts.shape
    return pl.pallas_call(
        total_kernel,
        out_shape=jax.ShapeDtypeStruct((rows, 2, width // 2), jnp.float32),
        in_specs=[VMEM],
        out_specs=VMEM,
        compiler_params=params(),
        name="total",
    )(parts)


def cost(queries, keys, heads, products, size):
    return pl.CostEstimate(
        flops=2 * products * heads * queries * keys * HEAD_DIM,
        bytes_accessed=size,
        transcendentals=heads * queries * keys,
    )


def face_bias(mask_ref):
    tile = lax.axis_index("tile")
    last = lax.axis_size("tile") - 1
    lower = jnp.where((mask_ref[0, 0] == 1) & (tile > 0), 0.0, NEG_LARGE)
    upper = jnp.where((mask_ref[0, 1] == 1) & (tile < last), 0.0, NEG_LARGE)
    even = tile % CORES == 0
    inner = jnp.where(even, upper, lower)
    outer = jnp.where(even, lower, upper)
    return inner.astype(jnp.float32), outer.astype(jnp.float32)


def columns(head, width):
    return [pl.ds(half * width + head * HEAD_DIM, HEAD_DIM) for half in range(2)]


def raised_stats(scores, grads):
    top = functools.reduce(jnp.maximum, [jnp.max(s, axis=0, keepdims=True) for s in scores])
    total = 0.0
    weighted = 0.0
    for s, g in zip(scores, grads):
        e = jnp.exp2(s - top)
        total = total + jnp.sum(e, axis=0, keepdims=True)
        weighted = weighted + jnp.sum(e * g, axis=0, keepdims=True)
    return top, total, weighted


def near_stats_kernel(mask_ref, pack_ref, own_ref, outer_ref, stat_ref):
    rows = stat_ref.shape[1]
    width = pack_ref.shape[1] // 2
    _, outer_bias = face_bias(mask_ref)
    for head in range(width // HEAD_DIM):
        at = columns(head, width)
        q, d = pack_ref[:rows, at[0]], pack_ref[:rows, at[1]]
        scores, grads = [], []
        for ref, bias in ((own_ref, None), (outer_ref, outer_bias)):
            s = dot(ref[:, at[0]], q, NT) * (SCALE * LOG2E)
            scores.append(s if bias is None else s + bias)
            grads.append(dot(ref[:, at[1]], d, NT))
        for i, row in enumerate(raised_stats(scores, grads)):
            stat_ref[pl.ds(3 * head + i, 1), :] = row


def near_stats(mask, pack, own, outer):
    rows, width = own.shape
    return pl.pallas_call(
        near_stats_kernel,
        out_shape=jax.ShapeDtypeStruct((STAT_ROWS, rows), jnp.float32),
        in_specs=[SMEM, VMEM, VMEM, VMEM],
        out_specs=VMEM,
        compiler_params=params(),
        cost_estimate=HEAVY,
        name="near_stats",
    )(mask, pack, own, outer)


def inner_stats_kernel(mask_ref, pack_ref, swap_ref, stat_ref):
    rows = stat_ref.shape[1]
    width = pack_ref.shape[1] // 2
    inner_bias, _ = face_bias(mask_ref)
    for head in range(width // HEAD_DIM):
        at = columns(head, width)
        s = dot(swap_ref[rows:, at[0]], pack_ref[:rows, at[0]], NT) * (SCALE * LOG2E) + inner_bias
        g = dot(swap_ref[rows:, at[1]], pack_ref[:rows, at[1]], NT)
        for i, row in enumerate(raised_stats([s], [g])):
            stat_ref[pl.ds(3 * head + i, 1), :] = row


def inner_stats(mask, pack, swap):
    rows, heads = pack.shape[0] - FACE, pack.shape[1] // 2 // HEAD_DIM
    return pl.pallas_call(
        inner_stats_kernel,
        out_shape=jax.ShapeDtypeStruct((STAT_ROWS, rows), jnp.float32),
        in_specs=[SMEM, VMEM, VMEM],
        out_specs=VMEM,
        compiler_params=params(),
        cost_estimate=cost(rows, FACE, heads, 2, 4 * pack.size),
        name="inner_stats",
    )(mask, pack, swap)


def cond_stats_kernel(pack_ref, swap_ref, cond_ref, near_ref, inner_ref, stat_ref):
    rows = near_ref.shape[1]
    width = pack_ref.shape[1] // 2
    stat_ref[0] = near_ref[...]
    stat_ref[1] = inner_ref[...]
    for head in range(width // HEAD_DIM):
        at = columns(head, width)
        key, value = cond_ref[:, at[0]], cond_ref[:, at[1]]
        for side, ref in enumerate((pack_ref, swap_ref)):
            s = dot(key, ref[:rows, at[0]], NT) * (SCALE * LOG2E)
            g = dot(value, ref[:rows, at[1]], NT)
            for i, row in enumerate(raised_stats([s], [g])):
                stat_ref[2 + side, pl.ds(3 * head + i, 1), :] = row


def cond_stats(pack, swap, cond, near, inner):
    rows = near.shape[1]
    heads = pack.shape[1] // 2 // HEAD_DIM
    return pl.pallas_call(
        cond_stats_kernel,
        out_shape=jax.ShapeDtypeStruct((4, STAT_ROWS, rows), jnp.float32),
        in_specs=[VMEM] * 5,
        out_specs=VMEM,
        compiler_params=params(),
        cost_estimate=cost(2 * rows, cond.shape[0], heads, 2, 6 * pack.size),
        name="cond_stats",
    )(pack, swap, cond, near, inner)


def head_pass(key, value, q, d, level, delta, bias=None):
    s = dot(key, q, NT) * (SCALE * LOG2E)
    if bias is not None:
        s = s + bias
    p = jnp.exp2(s - level)
    grad_s = (p * (dot(value, d, NT) - delta)).astype(jnp.bfloat16)
    return p.astype(jnp.bfloat16), grad_s


def grads_kernel(pack_ref, swap_ref, cond_ref, mine_ref, their_ref, out_ref, row_ref):
    rows = row_ref.shape[1]
    width = pack_ref.shape[1] // 2
    for head in range(width // HEAD_DIM):
        at = columns(head, width)
        key, value = cond_ref[:, at[0]], cond_ref[:, at[1]]
        grad_k = 0.0
        grad_v = 0.0
        for side, ref in enumerate((pack_ref, swap_ref)):
            home, away = (mine_ref, their_ref) if side == 0 else (their_ref, mine_ref)
            parts = [
                [r[pl.ds(3 * head + i, 1), :] for i in range(3)]
                for r in (home.at[0], home.at[1], home.at[2], away.at[3])
            ]
            top = functools.reduce(jnp.maximum, [p[0] for p in parts])
            total = sum(p[1] * jnp.exp2(p[0] - top) for p in parts)
            weighted = sum(p[2] * jnp.exp2(p[0] - top) for p in parts)
            level = top + jnp.log2(total)
            delta = weighted / total
            q, d = ref[:rows, at[0]], ref[:rows, at[1]]
            p, grad_s = head_pass(key, value, q, d, level, delta)
            grad_k = grad_k + dot(grad_s, q)
            grad_v = grad_v + dot(p, d)
            if side == 0:
                row_ref[pl.ds(2 * head, 1), :] = level
                row_ref[pl.ds(2 * head + 1, 1), :] = delta
        out_ref[:, at[0]] = (grad_k * SCALE).astype(out_ref.dtype)
        out_ref[:, at[1]] = grad_v.astype(out_ref.dtype)


def grads_pass(pack, swap, cond, mine, theirs):
    rows = mine.shape[2]
    heads = pack.shape[1] // 2 // HEAD_DIM
    return pl.pallas_call(
        grads_kernel,
        out_shape=(
            jax.ShapeDtypeStruct(cond.shape, jnp.bfloat16),
            jax.ShapeDtypeStruct((STAT_ROWS, rows), jnp.float32),
        ),
        in_specs=[VMEM] * 5,
        out_specs=(VMEM,) * 2,
        compiler_params=params(),
        cost_estimate=cost(2 * rows, cond.shape[0], heads, 4, 8 * pack.size),
        name="grads_pass",
    )(pack, swap, cond, mine, theirs)


def face_kernel(
    mask_ref, pack_ref, row_ref, swap_ref, outer_ref, to_inner_ref, to_outer_ref, sum_ref
):
    rows = row_ref.shape[1]
    width = pack_ref.shape[1] // 2
    inner_bias, outer_bias = face_bias(mask_ref)
    faces = (
        (swap_ref.at[rows:], inner_bias, to_inner_ref),
        (outer_ref, outer_bias, to_outer_ref),
    )
    for head in range(width // HEAD_DIM):
        at = columns(head, width)
        q, d = pack_ref[:rows, at[0]], pack_ref[:rows, at[1]]
        level, delta = [row_ref[pl.ds(2 * head + i, 1), :] for i in range(2)]
        att = 0.0
        grad_q = 0.0
        for face, bias, out in faces:
            key, value = face[:, at[0]], face[:, at[1]]
            p, grad_s = head_pass(key, value, q, d, level, delta, bias)
            out[:, at[0]] = (dot(grad_s, q) * SCALE).astype(out.dtype)
            out[:, at[1]] = dot(p, d).astype(out.dtype)
            att = att + dot(value, p, TN)
            grad_q = grad_q + dot(key, grad_s, TN)
        sum_ref[at[0], :] = grad_q
        sum_ref[at[1], :] = att


def face_pass(mask, pack, row_stats, swap, outer):
    rows = row_stats.shape[1]
    face = jax.ShapeDtypeStruct(outer.shape, jnp.bfloat16)
    return pl.pallas_call(
        face_kernel,
        out_shape=(face, face, jax.ShapeDtypeStruct((pack.shape[1], rows), jnp.float32)),
        in_specs=[SMEM] + [VMEM] * 4,
        out_specs=(VMEM,) * 3,
        compiler_params=params(),
        cost_estimate=LIGHT,
        name="face_pass",
    )(mask, pack, row_stats, swap, outer)


def own_kernel(
    pack_ref, row_ref, sum_ref, own_ref, cond_ref, far_cond_ref, att_ref, dq_ref, keep_ref
):
    rows = row_ref.shape[1]
    width = pack_ref.shape[1] // 2
    for head in range(width // HEAD_DIM):
        at = columns(head, width)
        q, d = pack_ref[:rows, at[0]], pack_ref[:rows, at[1]]
        level, delta = [row_ref[pl.ds(2 * head + i, 1), :] for i in range(2)]
        grad_q = sum_ref[at[0], :]
        att = sum_ref[at[1], :]
        for ref in (own_ref, cond_ref, far_cond_ref):
            key, value = ref[:, at[0]], ref[:, at[1]]
            p, grad_s = head_pass(key, value, q, d, level, delta)
            if ref is own_ref:
                keep_ref[:, at[0]] = dot(grad_s, q) * SCALE
                keep_ref[:, at[1]] = dot(p, d)
            att = att + dot(value, p, TN)
            grad_q = grad_q + dot(key, grad_s, TN)
        att_ref[:, at[0]] = att.T.astype(jnp.bfloat16)
        dq_ref[:, at[0]] = (grad_q * SCALE).T.astype(jnp.bfloat16)


def own_pass(pack, row_stats, sums, own, cond, far_cond):
    rows, width = own.shape
    half = jax.ShapeDtypeStruct((rows, width // 2), jnp.bfloat16)
    return pl.pallas_call(
        own_kernel,
        out_shape=(half, half, jax.ShapeDtypeStruct((rows, width), jnp.float32)),
        in_specs=[VMEM] * 6,
        out_specs=(VMEM,) * 3,
        compiler_params=params(),
        cost_estimate=LIGHT,
        name="own_pass",
    )(pack, row_stats, sums, own, cond, far_cond)


def per_device(queries, keys_values, cond_kv, face_mask, d_out):
    size = lax.axis_size("tile")
    rows, width = queries.shape
    chips = size // CORES
    cond_rows = cond_kv.shape[0]
    even = lax.axis_index("tile") % CORES == 0
    swap_cores = other_core(size)
    across = [(t, t + 1) for t in range(1, size - 1, CORES)]
    across += [(b, a) for a, b in across]

    copies = spread(cond_kv, chips)
    cond = lax.all_to_all(copies, "tile", 0, 0, axis_index_groups=same_core(size), tiled=True)
    cond = cond.reshape(chips * cond_rows, 2 * width)

    own = lax.optimization_barrier(keys_values.reshape(rows, 2 * width))
    edge = lax.dynamic_slice_in_dim(own, jnp.where(even, 0, rows - FACE), FACE, axis=0)
    outer = lax.ppermute(edge, "tile", across)
    pack = pack_queries(queries, d_out, own)
    swap = lax.ppermute(pack, "tile", swap_cores)
    near = near_stats(face_mask, pack, own, outer)
    inner = inner_stats(face_mask, pack, swap)

    mine = cond_stats(pack, swap, cond, near, inner)
    theirs = lax.ppermute(mine, "tile", swap_cores)
    grads, row_stats = grads_pass(pack, swap, cond, mine, theirs)
    blocks = grads.reshape(chips, cond_rows, 2 * width)
    parts = lax.all_to_all(blocks, "tile", 0, 0, axis_index_groups=same_core(size), tiled=True)
    grad_cond = total(parts)

    late_cond, row_stats = lax.optimization_barrier((cond, row_stats))
    far_cond = lax.ppermute(late_cond, "tile", swap_cores)
    to_inner, to_outer, sums = face_pass(face_mask, pack, row_stats, swap, outer)
    from_outer = lax.ppermute(to_outer, "tile", across)
    from_inner = lax.ppermute(to_inner, "tile", swap_cores)
    attended, grad_q, keep = own_pass(pack, row_stats, sums, own, cond, far_cond)
    keep, from_outer, from_inner = lax.optimization_barrier((keep, from_outer, from_inner))
    low = jnp.where(even, from_outer, from_inner).astype(jnp.float32)
    high = jnp.where(even, from_inner, from_outer).astype(jnp.float32)
    keep = keep + jnp.concatenate([low, high], axis=0)
    grad_kv = keep.astype(jnp.bfloat16).reshape(rows, 2, width)
    return attended, grad_q, grad_kv, grad_cond


def solution(mesh):
    return jax.shard_map(
        per_device,
        mesh=mesh,
        in_specs=(
            P("tile", "head"),
            P("tile", None, "head"),
            P("tile", None, "head"),
            P("tile", None),
            P("tile", "head"),
        ),
        out_specs=(
            P("tile", "head"),
            P("tile", "head"),
            P("tile", None, "head"),
            P("tile", None, "head"),
        ),
        check_vma=False,
    )
```

```python
import functools

import jax
import jax.numpy as jnp
from jax import lax
from jax.experimental import pallas as pl
from jax.experimental.pallas import tpu as pltpu
from jax.sharding import PartitionSpec as P

HEAD_DIM = 128
FACE = 128
CORES = 2
RUN = 4
STRIDE = 3
SCALE = HEAD_DIM**-0.5
LOG2E = 1.4426950408889634
NEG_LARGE = -1e30
STAT_ROWS = 16

NT = (((1,), (1,)), ((), ()))
TN = (((0,), (0,)), ((), ()))


def dot(a, b, dims=(((1,), (0,)), ((), ()))):
    return lax.dot_general(a, b, dims, preferred_element_type=jnp.float32)


def other_core(size):
    return [(t, t ^ 1) for t in range(size)]


def same_core(size):
    depth = size // (RUN * CORES)
    return [
        [((STRIDE * z % depth) * RUN + y) * CORES + c for y in range(RUN) for z in range(depth)]
        for c in range(CORES)
    ]


def params(mib=16):
    return pltpu.CompilerParams(vmem_limit_bytes=mib * 1024 * 1024)


VMEM = pl.BlockSpec(memory_space=pltpu.VMEM)
LIGHT = pl.CostEstimate(flops=1, bytes_accessed=1, transcendentals=0)
HEAVY = pl.CostEstimate(flops=6_000_000_000, bytes_accessed=0, transcendentals=0)
SMEM = pl.BlockSpec(memory_space=pltpu.SMEM)


def spread_kernel(cond_ref, out_ref):
    rows, _, width = cond_ref.shape
    flat = jnp.concatenate([cond_ref[:, 0, :], cond_ref[:, 1, :]], axis=1)
    out_ref[...] = jnp.broadcast_to(flat[None], out_ref.shape)


def spread(cond_kv, copies):
    rows, _, width = cond_kv.shape
    return pl.pallas_call(
        spread_kernel,
        out_shape=jax.ShapeDtypeStruct((copies, rows, 2 * width), cond_kv.dtype),
        in_specs=[VMEM],
        out_specs=VMEM,
        compiler_params=params(),
        name="spread",
    )(cond_kv)


def pack_kernel(q_ref, d_ref, own_ref, out_ref):
    rows, width = q_ref.shape
    even = lax.axis_index("tile") % CORES == 0
    start = pl.multiple_of(jnp.where(even, rows - FACE, 0), FACE)
    out_ref[:rows, :width] = q_ref[...]
    out_ref[:rows, width:] = d_ref[...]
    out_ref[rows:, :] = own_ref[pl.ds(start, FACE), :]


def pack_queries(queries, d_out, own):
    rows, width = own.shape
    return pl.pallas_call(
        pack_kernel,
        out_shape=jax.ShapeDtypeStruct((rows + FACE, width), own.dtype),
        in_specs=[VMEM] * 3,
        out_specs=VMEM,
        compiler_params=params(),
        cost_estimate=LIGHT,
        name="pack_queries",
    )(queries, d_out, own)


def total_kernel(parts_ref, out_ref):
    width = out_ref.shape[2]
    total = jnp.sum(parts_ref[...].astype(jnp.float32), axis=0)
    out_ref[:, 0, :] = total[:, :width]
    out_ref[:, 1, :] = total[:, width:]


def total(parts):
    _, rows, width = parts.shape
    return pl.pallas_call(
        total_kernel,
        out_shape=jax.ShapeDtypeStruct((rows, 2, width // 2), jnp.float32),
        in_specs=[VMEM],
        out_specs=VMEM,
        compiler_params=params(),
        name="total",
    )(parts)


def cost(queries, keys, heads, products, size):
    return pl.CostEstimate(
        flops=2 * products * heads * queries * keys * HEAD_DIM,
        bytes_accessed=size,
        transcendentals=heads * queries * keys,
    )


def face_bias(mask_ref):
    tile = lax.axis_index("tile")
    last = lax.axis_size("tile") - 1
    lower = jnp.where((mask_ref[0, 0] == 1) & (tile > 0), 0.0, NEG_LARGE)
    upper = jnp.where((mask_ref[0, 1] == 1) & (tile < last), 0.0, NEG_LARGE)
    even = tile % CORES == 0
    inner = jnp.where(even, upper, lower)
    outer = jnp.where(even, lower, upper)
    return inner.astype(jnp.float32), outer.astype(jnp.float32)


def columns(head, width):
    return [pl.ds(half * width + head * HEAD_DIM, HEAD_DIM) for half in range(2)]


def raised_stats(scores, grads):
    top = functools.reduce(jnp.maximum, [jnp.max(s, axis=0, keepdims=True) for s in scores])
    total = 0.0
    weighted = 0.0
    for s, g in zip(scores, grads):
        e = jnp.exp2(s - top)
        total = total + jnp.sum(e, axis=0, keepdims=True)
        weighted = weighted + jnp.sum(e * g, axis=0, keepdims=True)
    return top, total, weighted


def near_stats_kernel(mask_ref, pack_ref, own_ref, outer_ref, stat_ref):
    rows = stat_ref.shape[1]
    width = pack_ref.shape[1] // 2
    _, outer_bias = face_bias(mask_ref)
    for head in range(width // HEAD_DIM):
        at = columns(head, width)
        q, d = pack_ref[:rows, at[0]], pack_ref[:rows, at[1]]
        scores, grads = [], []
        for ref, bias in ((own_ref, None), (outer_ref, outer_bias)):
            s = dot(ref[:, at[0]], q, NT) * (SCALE * LOG2E)
            scores.append(s if bias is None else s + bias)
            grads.append(dot(ref[:, at[1]], d, NT))
        for i, row in enumerate(raised_stats(scores, grads)):
            stat_ref[pl.ds(3 * head + i, 1), :] = row


def near_stats(mask, pack, own, outer):
    rows, width = own.shape
    return pl.pallas_call(
        near_stats_kernel,
        out_shape=jax.ShapeDtypeStruct((STAT_ROWS, rows), jnp.float32),
        in_specs=[SMEM, VMEM, VMEM, VMEM],
        out_specs=VMEM,
        compiler_params=params(),
        cost_estimate=HEAVY,
        name="near_stats",
    )(mask, pack, own, outer)


def inner_stats_kernel(mask_ref, pack_ref, swap_ref, stat_ref):
    rows = stat_ref.shape[1]
    width = pack_ref.shape[1] // 2
    inner_bias, _ = face_bias(mask_ref)
    for head in range(width // HEAD_DIM):
        at = columns(head, width)
        s = dot(swap_ref[rows:, at[0]], pack_ref[:rows, at[0]], NT) * (SCALE * LOG2E) + inner_bias
        g = dot(swap_ref[rows:, at[1]], pack_ref[:rows, at[1]], NT)
        for i, row in enumerate(raised_stats([s], [g])):
            stat_ref[pl.ds(3 * head + i, 1), :] = row


def inner_stats(mask, pack, swap):
    rows, heads = pack.shape[0] - FACE, pack.shape[1] // 2 // HEAD_DIM
    return pl.pallas_call(
        inner_stats_kernel,
        out_shape=jax.ShapeDtypeStruct((STAT_ROWS, rows), jnp.float32),
        in_specs=[SMEM, VMEM, VMEM],
        out_specs=VMEM,
        compiler_params=params(),
        cost_estimate=cost(rows, FACE, heads, 2, 4 * pack.size),
        name="inner_stats",
    )(mask, pack, swap)


def cond_stats_kernel(pack_ref, swap_ref, cond_ref, near_ref, inner_ref, stat_ref):
    rows = near_ref.shape[1]
    width = pack_ref.shape[1] // 2
    stat_ref[0] = near_ref[...]
    stat_ref[1] = inner_ref[...]
    for head in range(width // HEAD_DIM):
        at = columns(head, width)
        key, value = cond_ref[:, at[0]], cond_ref[:, at[1]]
        for side, ref in enumerate((pack_ref, swap_ref)):
            s = dot(key, ref[:rows, at[0]], NT) * (SCALE * LOG2E)
            g = dot(value, ref[:rows, at[1]], NT)
            for i, row in enumerate(raised_stats([s], [g])):
                stat_ref[2 + side, pl.ds(3 * head + i, 1), :] = row


def cond_stats(pack, swap, cond, near, inner):
    rows = near.shape[1]
    heads = pack.shape[1] // 2 // HEAD_DIM
    return pl.pallas_call(
        cond_stats_kernel,
        out_shape=jax.ShapeDtypeStruct((4, STAT_ROWS, rows), jnp.float32),
        in_specs=[VMEM] * 5,
        out_specs=VMEM,
        compiler_params=params(),
        cost_estimate=cost(2 * rows, cond.shape[0], heads, 2, 6 * pack.size),
        name="cond_stats",
    )(pack, swap, cond, near, inner)


def head_pass(key, value, q, d, level, delta, bias=None):
    s = dot(key, q, NT) * (SCALE * LOG2E)
    if bias is not None:
        s = s + bias
    p = jnp.exp2(s - level)
    grad_s = (p * (dot(value, d, NT) - delta)).astype(jnp.bfloat16)
    return p.astype(jnp.bfloat16), grad_s


def grads_kernel(pack_ref, swap_ref, cond_ref, mine_ref, their_ref, out_ref, row_ref):
    rows = row_ref.shape[1]
    width = pack_ref.shape[1] // 2
    for head in range(width // HEAD_DIM):
        at = columns(head, width)
        key, value = cond_ref[:, at[0]], cond_ref[:, at[1]]
        grad_k = 0.0
        grad_v = 0.0
        for side, ref in enumerate((pack_ref, swap_ref)):
            home, away = (mine_ref, their_ref) if side == 0 else (their_ref, mine_ref)
            parts = [
                [r[pl.ds(3 * head + i, 1), :] for i in range(3)]
                for r in (home.at[0], home.at[1], home.at[2], away.at[3])
            ]
            top = functools.reduce(jnp.maximum, [p[0] for p in parts])
            total = sum(p[1] * jnp.exp2(p[0] - top) for p in parts)
            weighted = sum(p[2] * jnp.exp2(p[0] - top) for p in parts)
            level = top + jnp.log2(total)
            delta = weighted / total
            q, d = ref[:rows, at[0]], ref[:rows, at[1]]
            p, grad_s = head_pass(key, value, q, d, level, delta)
            grad_k = grad_k + dot(grad_s, q)
            grad_v = grad_v + dot(p, d)
            if side == 0:
                row_ref[pl.ds(2 * head, 1), :] = level
                row_ref[pl.ds(2 * head + 1, 1), :] = delta
        out_ref[:, at[0]] = (grad_k * SCALE).astype(out_ref.dtype)
        out_ref[:, at[1]] = grad_v.astype(out_ref.dtype)


def grads_pass(pack, swap, cond, mine, theirs):
    rows = mine.shape[2]
    heads = pack.shape[1] // 2 // HEAD_DIM
    return pl.pallas_call(
        grads_kernel,
        out_shape=(
            jax.ShapeDtypeStruct(cond.shape, jnp.bfloat16),
            jax.ShapeDtypeStruct((STAT_ROWS, rows), jnp.float32),
        ),
        in_specs=[VMEM] * 5,
        out_specs=(VMEM,) * 2,
        compiler_params=params(),
        cost_estimate=cost(2 * rows, cond.shape[0], heads, 4, 8 * pack.size),
        name="grads_pass",
    )(pack, swap, cond, mine, theirs)


def face_kernel(
    mask_ref, pack_ref, row_ref, swap_ref, outer_ref, to_inner_ref, to_outer_ref, sum_ref
):
    rows = row_ref.shape[1]
    width = pack_ref.shape[1] // 2
    inner_bias, outer_bias = face_bias(mask_ref)
    faces = (
        (swap_ref.at[rows:], inner_bias, to_inner_ref),
        (outer_ref, outer_bias, to_outer_ref),
    )
    for head in range(width // HEAD_DIM):
        at = columns(head, width)
        q, d = pack_ref[:rows, at[0]], pack_ref[:rows, at[1]]
        level, delta = [row_ref[pl.ds(2 * head + i, 1), :] for i in range(2)]
        att = 0.0
        grad_q = 0.0
        for face, bias, out in faces:
            key, value = face[:, at[0]], face[:, at[1]]
            p, grad_s = head_pass(key, value, q, d, level, delta, bias)
            out[:, at[0]] = (dot(grad_s, q) * SCALE).astype(out.dtype)
            out[:, at[1]] = dot(p, d).astype(out.dtype)
            att = att + dot(value, p, TN)
            grad_q = grad_q + dot(key, grad_s, TN)
        sum_ref[at[0], :] = grad_q
        sum_ref[at[1], :] = att


def face_pass(mask, pack, row_stats, swap, outer):
    rows = row_stats.shape[1]
    face = jax.ShapeDtypeStruct(outer.shape, jnp.bfloat16)
    return pl.pallas_call(
        face_kernel,
        out_shape=(face, face, jax.ShapeDtypeStruct((pack.shape[1], rows), jnp.float32)),
        in_specs=[SMEM] + [VMEM] * 4,
        out_specs=(VMEM,) * 3,
        compiler_params=params(),
        cost_estimate=LIGHT,
        name="face_pass",
    )(mask, pack, row_stats, swap, outer)


def own_kernel(
    pack_ref, row_ref, sum_ref, own_ref, cond_ref, far_cond_ref, att_ref, dq_ref, keep_ref
):
    rows = row_ref.shape[1]
    width = pack_ref.shape[1] // 2
    for head in range(width // HEAD_DIM):
        at = columns(head, width)
        q, d = pack_ref[:rows, at[0]], pack_ref[:rows, at[1]]
        level, delta = [row_ref[pl.ds(2 * head + i, 1), :] for i in range(2)]
        grad_q = sum_ref[at[0], :]
        att = sum_ref[at[1], :]
        for ref in (own_ref, cond_ref, far_cond_ref):
            key, value = ref[:, at[0]], ref[:, at[1]]
            p, grad_s = head_pass(key, value, q, d, level, delta)
            if ref is own_ref:
                keep_ref[:, at[0]] = dot(grad_s, q) * SCALE
                keep_ref[:, at[1]] = dot(p, d)
            att = att + dot(value, p, TN)
            grad_q = grad_q + dot(key, grad_s, TN)
        att_ref[:, at[0]] = att.T.astype(jnp.bfloat16)
        dq_ref[:, at[0]] = (grad_q * SCALE).T.astype(jnp.bfloat16)


def own_pass(pack, row_stats, sums, own, cond, far_cond):
    rows, width = own.shape
    half = jax.ShapeDtypeStruct((rows, width // 2), jnp.bfloat16)
    return pl.pallas_call(
        own_kernel,
        out_shape=(half, half, jax.ShapeDtypeStruct((rows, width), jnp.float32)),
        in_specs=[VMEM] * 6,
        out_specs=(VMEM,) * 3,
        compiler_params=params(),
        cost_estimate=LIGHT,
        name="own_pass",
    )(pack, row_stats, sums, own, cond, far_cond)


def per_device(queries, keys_values, cond_kv, face_mask, d_out):
    size = lax.axis_size("tile")
    rows, width = queries.shape
    chips = size // CORES
    cond_rows = cond_kv.shape[0]
    even = lax.axis_index("tile") % CORES == 0
    swap_cores = other_core(size)
    across = [(t, t + 1) for t in range(1, size - 1, CORES)]
    across += [(b, a) for a, b in across]

    copies = spread(cond_kv, chips)
    cond = lax.all_to_all(copies, "tile", 0, 0, axis_index_groups=same_core(size), tiled=True)
    cond = cond.reshape(chips * cond_rows, 2 * width)

    own = lax.optimization_barrier(keys_values.reshape(rows, 2 * width))
    edge = lax.dynamic_slice_in_dim(keys_values, jnp.where(even, 0, rows - FACE), FACE, axis=0)
    outer = lax.ppermute(edge.reshape(FACE, 2 * width), "tile", across)
    pack = pack_queries(queries, d_out, own)
    swap = lax.ppermute(pack, "tile", swap_cores)
    near = near_stats(face_mask, pack, own, outer)
    inner = inner_stats(face_mask, pack, swap)

    mine = cond_stats(pack, swap, cond, near, inner)
    theirs = lax.ppermute(mine, "tile", swap_cores)
    grads, row_stats = grads_pass(pack, swap, cond, mine, theirs)
    blocks = grads.reshape(chips, cond_rows, 2 * width)
    parts = lax.all_to_all(blocks, "tile", 0, 0, axis_index_groups=same_core(size), tiled=True)
    grad_cond = total(parts)

    to_inner, to_outer, sums = face_pass(face_mask, pack, row_stats, swap, outer)
    late_cond, sums = lax.optimization_barrier((cond, sums))
    far_cond = lax.ppermute(late_cond, "tile", swap_cores)
    from_outer = lax.ppermute(to_outer, "tile", across)
    from_inner = lax.ppermute(to_inner, "tile", swap_cores)
    attended, grad_q, keep = own_pass(pack, row_stats, sums, own, cond, far_cond)
    keep, from_outer, from_inner = lax.optimization_barrier((keep, from_outer, from_inner))
    low = jnp.where(even, from_outer, from_inner).astype(jnp.float32)
    high = jnp.where(even, from_inner, from_outer).astype(jnp.float32)
    keep = keep + jnp.concatenate([low, high], axis=0)
    grad_kv = keep.astype(jnp.bfloat16).reshape(rows, 2, width)
    return attended, grad_q, grad_kv, grad_cond


def solution(mesh):
    return jax.shard_map(
        per_device,
        mesh=mesh,
        in_specs=(
            P("tile", "head"),
            P("tile", None, "head"),
            P("tile", None, "head"),
            P("tile", None),
            P("tile", "head"),
        ),
        out_specs=(
            P("tile", "head"),
            P("tile", "head"),
            P("tile", None, "head"),
            P("tile", None, "head"),
        ),
        check_vma=False,
    )
```

```python
import functools

import jax
import jax.numpy as jnp
from jax import lax
from jax.experimental import pallas as pl
from jax.experimental.pallas import tpu as pltpu
from jax.sharding import PartitionSpec as P

HEAD_DIM = 128
FACE = 128
CORES = 2
RUN = 4
STRIDE = 3
SCALE = HEAD_DIM**-0.5
LOG2E = 1.4426950408889634
NEG_LARGE = -1e30
STAT_ROWS = 16

NT = (((1,), (1,)), ((), ()))
TN = (((0,), (0,)), ((), ()))


def dot(a, b, dims=(((1,), (0,)), ((), ()))):
    return lax.dot_general(a, b, dims, preferred_element_type=jnp.float32)


def other_core(size):
    return [(t, t ^ 1) for t in range(size)]


def same_core(size):
    depth = size // (RUN * CORES)
    return [
        [((STRIDE * z % depth) * RUN + y) * CORES + c for y in range(RUN) for z in range(depth)]
        for c in range(CORES)
    ]


def params(mib=16):
    return pltpu.CompilerParams(vmem_limit_bytes=mib * 1024 * 1024)


VMEM = pl.BlockSpec(memory_space=pltpu.VMEM)
LIGHT = pl.CostEstimate(flops=1, bytes_accessed=1, transcendentals=0)
HEAVY = pl.CostEstimate(flops=6_000_000_000, bytes_accessed=0, transcendentals=0)
SMEM = pl.BlockSpec(memory_space=pltpu.SMEM)


def spread_kernel(cond_ref, out_ref):
    rows, _, width = cond_ref.shape
    flat = jnp.concatenate([cond_ref[:, 0, :], cond_ref[:, 1, :]], axis=1)
    out_ref[...] = jnp.broadcast_to(flat[None], out_ref.shape)


def spread(cond_kv, copies):
    rows, _, width = cond_kv.shape
    return pl.pallas_call(
        spread_kernel,
        out_shape=jax.ShapeDtypeStruct((copies, rows, 2 * width), cond_kv.dtype),
        in_specs=[VMEM],
        out_specs=VMEM,
        compiler_params=params(),
        name="spread",
    )(cond_kv)


def pack_kernel(q_ref, d_ref, own_ref, out_ref):
    rows, width = q_ref.shape
    even = lax.axis_index("tile") % CORES == 0
    start = pl.multiple_of(jnp.where(even, rows - FACE, 0), FACE)
    out_ref[:rows, :width] = q_ref[...]
    out_ref[:rows, width:] = d_ref[...]
    out_ref[rows:, :] = own_ref[pl.ds(start, FACE), :]


def pack_queries(queries, d_out, own):
    rows, width = own.shape
    return pl.pallas_call(
        pack_kernel,
        out_shape=jax.ShapeDtypeStruct((rows + FACE, width), own.dtype),
        in_specs=[VMEM] * 3,
        out_specs=VMEM,
        compiler_params=params(),
        cost_estimate=LIGHT,
        name="pack_queries",
    )(queries, d_out, own)


def total_kernel(parts_ref, out_ref):
    width = out_ref.shape[2]
    total = jnp.sum(parts_ref[...].astype(jnp.float32), axis=0)
    out_ref[:, 0, :] = total[:, :width]
    out_ref[:, 1, :] = total[:, width:]


def total(parts):
    _, rows, width = parts.shape
    return pl.pallas_call(
        total_kernel,
        out_shape=jax.ShapeDtypeStruct((rows, 2, width // 2), jnp.float32),
        in_specs=[VMEM],
        out_specs=VMEM,
        compiler_params=params(),
        name="total",
    )(parts)


def cost(queries, keys, heads, products, size):
    return pl.CostEstimate(
        flops=2 * products * heads * queries * keys * HEAD_DIM,
        bytes_accessed=size,
        transcendentals=heads * queries * keys,
    )


def face_bias(mask_ref):
    tile = lax.axis_index("tile")
    last = lax.axis_size("tile") - 1
    lower = jnp.where((mask_ref[0, 0] == 1) & (tile > 0), 0.0, NEG_LARGE)
    upper = jnp.where((mask_ref[0, 1] == 1) & (tile < last), 0.0, NEG_LARGE)
    even = tile % CORES == 0
    inner = jnp.where(even, upper, lower)
    outer = jnp.where(even, lower, upper)
    return inner.astype(jnp.float32), outer.astype(jnp.float32)


def columns(head, width):
    return [pl.ds(half * width + head * HEAD_DIM, HEAD_DIM) for half in range(2)]


def raised_stats(scores, grads):
    top = functools.reduce(jnp.maximum, [jnp.max(s, axis=0, keepdims=True) for s in scores])
    total = 0.0
    weighted = 0.0
    for s, g in zip(scores, grads):
        e = jnp.exp2(s - top)
        total = total + jnp.sum(e, axis=0, keepdims=True)
        weighted = weighted + jnp.sum(e * g, axis=0, keepdims=True)
    return top, total, weighted


def near_stats_kernel(mask_ref, pack_ref, own_ref, outer_ref, stat_ref):
    rows = stat_ref.shape[1]
    width = pack_ref.shape[1] // 2
    _, outer_bias = face_bias(mask_ref)
    for head in range(width // HEAD_DIM):
        at = columns(head, width)
        q, d = pack_ref[:rows, at[0]], pack_ref[:rows, at[1]]
        scores, grads = [], []
        for ref, bias in ((own_ref, None), (outer_ref, outer_bias)):
            s = dot(ref[:, at[0]], q, NT) * (SCALE * LOG2E)
            scores.append(s if bias is None else s + bias)
            grads.append(dot(ref[:, at[1]], d, NT))
        for i, row in enumerate(raised_stats(scores, grads)):
            stat_ref[pl.ds(3 * head + i, 1), :] = row


def near_stats(mask, pack, own, outer):
    rows, width = own.shape
    return pl.pallas_call(
        near_stats_kernel,
        out_shape=jax.ShapeDtypeStruct((STAT_ROWS, rows), jnp.float32),
        in_specs=[SMEM, VMEM, VMEM, VMEM],
        out_specs=VMEM,
        compiler_params=params(),
        cost_estimate=HEAVY,
        name="near_stats",
    )(mask, pack, own, outer)


def inner_stats_kernel(mask_ref, pack_ref, swap_ref, stat_ref):
    rows = stat_ref.shape[1]
    width = pack_ref.shape[1] // 2
    inner_bias, _ = face_bias(mask_ref)
    for head in range(width // HEAD_DIM):
        at = columns(head, width)
        s = dot(swap_ref[rows:, at[0]], pack_ref[:rows, at[0]], NT) * (SCALE * LOG2E) + inner_bias
        g = dot(swap_ref[rows:, at[1]], pack_ref[:rows, at[1]], NT)
        for i, row in enumerate(raised_stats([s], [g])):
            stat_ref[pl.ds(3 * head + i, 1), :] = row


def inner_stats(mask, pack, swap):
    rows, heads = pack.shape[0] - FACE, pack.shape[1] // 2 // HEAD_DIM
    return pl.pallas_call(
        inner_stats_kernel,
        out_shape=jax.ShapeDtypeStruct((STAT_ROWS, rows), jnp.float32),
        in_specs=[SMEM, VMEM, VMEM],
        out_specs=VMEM,
        compiler_params=params(),
        cost_estimate=cost(rows, FACE, heads, 2, 4 * pack.size),
        name="inner_stats",
    )(mask, pack, swap)


def cond_stats_kernel(pack_ref, swap_ref, cond_ref, near_ref, inner_ref, stat_ref, out_ref):
    rows = near_ref.shape[1]
    width = pack_ref.shape[1] // 2
    cond_rows = cond_ref.shape[0]
    out_ref[:cond_rows, :] = cond_ref[...]
    stat_ref[...] = jnp.zeros_like(stat_ref)
    stat_ref[0] = near_ref[...]
    stat_ref[1] = inner_ref[...]
    for head in range(width // HEAD_DIM):
        at = columns(head, width)
        key, value = cond_ref[:, at[0]], cond_ref[:, at[1]]
        for side, ref in enumerate((pack_ref, swap_ref)):
            s = dot(key, ref[:rows, at[0]], NT) * (SCALE * LOG2E)
            g = dot(value, ref[:rows, at[1]], NT)
            for i, row in enumerate(raised_stats([s], [g])):
                stat_ref[2 + side, pl.ds(3 * head + i, 1), :] = row
    rest = stat_ref[...].reshape(4 * STAT_ROWS, rows)
    for part in range(3):
        rounded = rest.astype(jnp.bfloat16)
        out_ref[cond_rows:, pl.ds(part * rows, rows)] = rounded
        rest = rest - rounded.astype(jnp.float32)


def cond_stats(pack, swap, cond, near, inner):
    rows = near.shape[1]
    heads = pack.shape[1] // 2 // HEAD_DIM
    sent = (cond.shape[0] + 4 * STAT_ROWS, max(cond.shape[1], 3 * rows))
    return pl.pallas_call(
        cond_stats_kernel,
        out_shape=(
            jax.ShapeDtypeStruct((4, STAT_ROWS, rows), jnp.float32),
            jax.ShapeDtypeStruct(sent, jnp.bfloat16),
        ),
        in_specs=[VMEM] * 5,
        out_specs=(VMEM, VMEM),
        compiler_params=params(),
        cost_estimate=cost(2 * rows, cond.shape[0], heads, 2, 6 * pack.size),
        name="cond_stats",
    )(pack, swap, cond, near, inner)


def head_pass(key, value, q, d, level, delta, bias=None):
    s = dot(key, q, NT) * (SCALE * LOG2E)
    if bias is not None:
        s = s + bias
    p = jnp.exp2(s - level)
    grad_s = (p * (dot(value, d, NT) - delta)).astype(jnp.bfloat16)
    return p.astype(jnp.bfloat16), grad_s


def grads_kernel(
    pack_ref, swap_ref, cond_ref, mine_ref, sent_ref, out_ref, row_ref, their_ref
):
    rows = row_ref.shape[1]
    width = pack_ref.shape[1] // 2
    cond_rows = cond_ref.shape[0]
    parts = [
        sent_ref[cond_rows:, pl.ds(part * rows, rows)].astype(jnp.float32) for part in range(3)
    ]
    their_ref[...] = ((parts[2] + parts[1]) + parts[0]).reshape(their_ref.shape)
    for head in range(width // HEAD_DIM):
        at = columns(head, width)
        key, value = cond_ref[:, at[0]], cond_ref[:, at[1]]
        grad_k = 0.0
        grad_v = 0.0
        for side, ref in enumerate((pack_ref, swap_ref)):
            home, away = (mine_ref, their_ref) if side == 0 else (their_ref, mine_ref)
            parts = [
                [r[pl.ds(3 * head + i, 1), :] for i in range(3)]
                for r in (home.at[0], home.at[1], home.at[2], away.at[3])
            ]
            top = functools.reduce(jnp.maximum, [p[0] for p in parts])
            total = sum(p[1] * jnp.exp2(p[0] - top) for p in parts)
            weighted = sum(p[2] * jnp.exp2(p[0] - top) for p in parts)
            level = top + jnp.log2(total)
            delta = weighted / total
            q, d = ref[:rows, at[0]], ref[:rows, at[1]]
            p, grad_s = head_pass(key, value, q, d, level, delta)
            grad_k = grad_k + dot(grad_s, q)
            grad_v = grad_v + dot(p, d)
            if side == 0:
                row_ref[pl.ds(2 * head, 1), :] = level
                row_ref[pl.ds(2 * head + 1, 1), :] = delta
        out_ref[:, at[0]] = (grad_k * SCALE).astype(out_ref.dtype)
        out_ref[:, at[1]] = grad_v.astype(out_ref.dtype)


def grads_pass(pack, swap, cond, mine, theirs):
    rows = mine.shape[2]
    heads = pack.shape[1] // 2 // HEAD_DIM
    return pl.pallas_call(
        grads_kernel,
        out_shape=(
            jax.ShapeDtypeStruct(cond.shape, jnp.bfloat16),
            jax.ShapeDtypeStruct((STAT_ROWS, rows), jnp.float32),
        ),
        in_specs=[VMEM] * 5,
        out_specs=(VMEM,) * 2,
        scratch_shapes=[pltpu.VMEM(mine.shape, jnp.float32)],
        compiler_params=params(),
        cost_estimate=cost(2 * rows, cond.shape[0], heads, 4, 8 * pack.size),
        name="grads_pass",
    )(pack, swap, cond, mine, theirs)


def face_kernel(
    mask_ref, pack_ref, row_ref, swap_ref, outer_ref, to_inner_ref, to_outer_ref, sum_ref
):
    rows = row_ref.shape[1]
    width = pack_ref.shape[1] // 2
    inner_bias, outer_bias = face_bias(mask_ref)
    faces = (
        (swap_ref.at[rows:], inner_bias, to_inner_ref),
        (outer_ref, outer_bias, to_outer_ref),
    )
    for head in range(width // HEAD_DIM):
        at = columns(head, width)
        q, d = pack_ref[:rows, at[0]], pack_ref[:rows, at[1]]
        level, delta = [row_ref[pl.ds(2 * head + i, 1), :] for i in range(2)]
        att = 0.0
        grad_q = 0.0
        for face, bias, out in faces:
            key, value = face[:, at[0]], face[:, at[1]]
            p, grad_s = head_pass(key, value, q, d, level, delta, bias)
            out[:, at[0]] = (dot(grad_s, q) * SCALE).astype(out.dtype)
            out[:, at[1]] = dot(p, d).astype(out.dtype)
            att = att + dot(value, p, TN)
            grad_q = grad_q + dot(key, grad_s, TN)
        sum_ref[at[0], :] = grad_q
        sum_ref[at[1], :] = att


def face_pass(mask, pack, row_stats, swap, outer):
    rows = row_stats.shape[1]
    face = jax.ShapeDtypeStruct(outer.shape, jnp.bfloat16)
    return pl.pallas_call(
        face_kernel,
        out_shape=(face, face, jax.ShapeDtypeStruct((pack.shape[1], rows), jnp.float32)),
        in_specs=[SMEM] + [VMEM] * 4,
        out_specs=(VMEM,) * 3,
        compiler_params=params(),
        cost_estimate=LIGHT,
        name="face_pass",
    )(mask, pack, row_stats, swap, outer)


def own_kernel(
    pack_ref, row_ref, sum_ref, own_ref, cond_ref, far_cond_ref, att_ref, dq_ref, keep_ref
):
    rows = row_ref.shape[1]
    width = pack_ref.shape[1] // 2
    far_ref = far_cond_ref.at[: cond_ref.shape[0]]
    for head in range(width // HEAD_DIM):
        at = columns(head, width)
        q, d = pack_ref[:rows, at[0]], pack_ref[:rows, at[1]]
        level, delta = [row_ref[pl.ds(2 * head + i, 1), :] for i in range(2)]
        grad_q = sum_ref[at[0], :]
        att = sum_ref[at[1], :]
        for ref in (own_ref, cond_ref, far_ref):
            key, value = ref[:, at[0]], ref[:, at[1]]
            p, grad_s = head_pass(key, value, q, d, level, delta)
            if ref is own_ref:
                keep_ref[:, at[0]] = dot(grad_s, q) * SCALE
                keep_ref[:, at[1]] = dot(p, d)
            att = att + dot(value, p, TN)
            grad_q = grad_q + dot(key, grad_s, TN)
        att_ref[:, at[0]] = att.T.astype(jnp.bfloat16)
        dq_ref[:, at[0]] = (grad_q * SCALE).T.astype(jnp.bfloat16)


def own_pass(pack, row_stats, sums, own, cond, far_cond):
    rows, width = own.shape
    half = jax.ShapeDtypeStruct((rows, width // 2), jnp.bfloat16)
    return pl.pallas_call(
        own_kernel,
        out_shape=(half, half, jax.ShapeDtypeStruct((rows, width), jnp.float32)),
        in_specs=[VMEM] * 6,
        out_specs=(VMEM,) * 3,
        compiler_params=params(),
        cost_estimate=LIGHT,
        name="own_pass",
    )(pack, row_stats, sums, own, cond, far_cond)


def per_device(queries, keys_values, cond_kv, face_mask, d_out):
    size = lax.axis_size("tile")
    rows, width = queries.shape
    chips = size // CORES
    cond_rows = cond_kv.shape[0]
    even = lax.axis_index("tile") % CORES == 0
    swap_cores = other_core(size)
    across = [(t, t + 1) for t in range(1, size - 1, CORES)]
    across += [(b, a) for a, b in across]

    copies = spread(cond_kv, chips)
    cond = lax.all_to_all(copies, "tile", 0, 0, axis_index_groups=same_core(size), tiled=True)
    cond = cond.reshape(chips * cond_rows, 2 * width)

    own = lax.optimization_barrier(keys_values.reshape(rows, 2 * width))
    edge = lax.dynamic_slice_in_dim(own, jnp.where(even, 0, rows - FACE), FACE, axis=0)
    outer = lax.ppermute(edge, "tile", across)
    pack = pack_queries(queries, d_out, own)
    swap = lax.ppermute(pack, "tile", swap_cores)
    near = near_stats(face_mask, pack, own, outer)
    inner = inner_stats(face_mask, pack, swap)

    mine, sent = cond_stats(pack, swap, cond, near, inner)
    theirs = lax.ppermute(sent, "tile", swap_cores)
    grads, row_stats = grads_pass(pack, swap, cond, mine, theirs)
    blocks = grads.reshape(chips, cond_rows, 2 * width)
    parts = lax.all_to_all(blocks, "tile", 0, 0, axis_index_groups=same_core(size), tiled=True)
    grad_cond = total(parts)

    to_inner, to_outer, sums = face_pass(face_mask, pack, row_stats, swap, outer)
    from_outer = lax.ppermute(to_outer, "tile", across)
    from_inner = lax.ppermute(to_inner, "tile", swap_cores)
    attended, grad_q, keep = own_pass(pack, row_stats, sums, own, cond, theirs)
    keep, from_outer, from_inner = lax.optimization_barrier((keep, from_outer, from_inner))
    low = jnp.where(even, from_outer, from_inner).astype(jnp.float32)
    high = jnp.where(even, from_inner, from_outer).astype(jnp.float32)
    keep = keep + jnp.concatenate([low, high], axis=0)
    grad_kv = keep.astype(jnp.bfloat16).reshape(rows, 2, width)
    return attended, grad_q, grad_kv, grad_cond


def solution(mesh):
    return jax.shard_map(
        per_device,
        mesh=mesh,
        in_specs=(
            P("tile", "head"),
            P("tile", None, "head"),
            P("tile", None, "head"),
            P("tile", None),
            P("tile", "head"),
        ),
        out_specs=(
            P("tile", "head"),
            P("tile", "head"),
            P("tile", None, "head"),
            P("tile", None, "head"),
        ),
        check_vma=False,
    )
```

```python
import functools

import jax
import jax.numpy as jnp
from jax import lax
from jax.experimental import pallas as pl
from jax.experimental.pallas import tpu as pltpu
from jax.sharding import PartitionSpec as P

HEAD_DIM = 128
FACE = 128
CORES = 2
RUN = 4
STRIDE = 3
SCALE = HEAD_DIM**-0.5
LOG2E = 1.4426950408889634
NEG_LARGE = -1e30
STAT_ROWS = 16

NT = (((1,), (1,)), ((), ()))
TN = (((0,), (0,)), ((), ()))


def dot(a, b, dims=(((1,), (0,)), ((), ()))):
    return lax.dot_general(a, b, dims, preferred_element_type=jnp.float32)


def other_core(size):
    return [(t, t ^ 1) for t in range(size)]


def same_core(size):
    depth = size // (RUN * CORES)
    return [
        [((step * z % depth) * RUN + y) * CORES + c for y in range(RUN) for z in range(depth)]
        for c, step in enumerate((STRIDE, -STRIDE))
    ]


def params(mib=16):
    return pltpu.CompilerParams(vmem_limit_bytes=mib * 1024 * 1024)


VMEM = pl.BlockSpec(memory_space=pltpu.VMEM)
LIGHT = pl.CostEstimate(flops=1, bytes_accessed=1, transcendentals=0)
HEAVY = pl.CostEstimate(flops=6_000_000_000, bytes_accessed=0, transcendentals=0)
SMEM = pl.BlockSpec(memory_space=pltpu.SMEM)


def spread_kernel(cond_ref, out_ref):
    rows, _, width = cond_ref.shape
    flat = jnp.concatenate([cond_ref[:, 0, :], cond_ref[:, 1, :]], axis=1)
    out_ref[...] = jnp.broadcast_to(flat[None], out_ref.shape)


def spread(cond_kv, copies):
    rows, _, width = cond_kv.shape
    return pl.pallas_call(
        spread_kernel,
        out_shape=jax.ShapeDtypeStruct((copies, rows, 2 * width), cond_kv.dtype),
        in_specs=[VMEM],
        out_specs=VMEM,
        compiler_params=params(),
        name="spread",
    )(cond_kv)


def pack_kernel(q_ref, d_ref, own_ref, out_ref):
    rows, width = q_ref.shape
    even = lax.axis_index("tile") % CORES == 0
    start = pl.multiple_of(jnp.where(even, rows - FACE, 0), FACE)
    out_ref[:rows, :width] = q_ref[...]
    out_ref[:rows, width:] = d_ref[...]
    out_ref[rows:, :] = own_ref[pl.ds(start, FACE), :]


def pack_queries(queries, d_out, own):
    rows, width = own.shape
    return pl.pallas_call(
        pack_kernel,
        out_shape=jax.ShapeDtypeStruct((rows + FACE, width), own.dtype),
        in_specs=[VMEM] * 3,
        out_specs=VMEM,
        compiler_params=params(),
        cost_estimate=LIGHT,
        name="pack_queries",
    )(queries, d_out, own)


def total_kernel(parts_ref, out_ref):
    width = out_ref.shape[2]
    total = jnp.sum(parts_ref[...].astype(jnp.float32), axis=0)
    out_ref[:, 0, :] = total[:, :width]
    out_ref[:, 1, :] = total[:, width:]


def total(parts):
    _, rows, width = parts.shape
    return pl.pallas_call(
        total_kernel,
        out_shape=jax.ShapeDtypeStruct((rows, 2, width // 2), jnp.float32),
        in_specs=[VMEM],
        out_specs=VMEM,
        compiler_params=params(),
        name="total",
    )(parts)


def cost(queries, keys, heads, products, size):
    return pl.CostEstimate(
        flops=2 * products * heads * queries * keys * HEAD_DIM,
        bytes_accessed=size,
        transcendentals=heads * queries * keys,
    )


def face_bias(mask_ref):
    tile = lax.axis_index("tile")
    last = lax.axis_size("tile") - 1
    lower = jnp.where((mask_ref[0, 0] == 1) & (tile > 0), 0.0, NEG_LARGE)
    upper = jnp.where((mask_ref[0, 1] == 1) & (tile < last), 0.0, NEG_LARGE)
    even = tile % CORES == 0
    inner = jnp.where(even, upper, lower)
    outer = jnp.where(even, lower, upper)
    return inner.astype(jnp.float32), outer.astype(jnp.float32)


def columns(head, width):
    return [pl.ds(half * width + head * HEAD_DIM, HEAD_DIM) for half in range(2)]


def raised_stats(scores, grads):
    top = functools.reduce(jnp.maximum, [jnp.max(s, axis=0, keepdims=True) for s in scores])
    total = 0.0
    weighted = 0.0
    for s, g in zip(scores, grads):
        e = jnp.exp2(s - top)
        total = total + jnp.sum(e, axis=0, keepdims=True)
        weighted = weighted + jnp.sum(e * g, axis=0, keepdims=True)
    return top, total, weighted


def near_stats_kernel(mask_ref, pack_ref, own_ref, outer_ref, stat_ref):
    rows = stat_ref.shape[1]
    width = pack_ref.shape[1] // 2
    _, outer_bias = face_bias(mask_ref)
    for head in range(width // HEAD_DIM):
        at = columns(head, width)
        q, d = pack_ref[:rows, at[0]], pack_ref[:rows, at[1]]
        scores, grads = [], []
        for ref, bias in ((own_ref, None), (outer_ref, outer_bias)):
            s = dot(ref[:, at[0]], q, NT) * (SCALE * LOG2E)
            scores.append(s if bias is None else s + bias)
            grads.append(dot(ref[:, at[1]], d, NT))
        for i, row in enumerate(raised_stats(scores, grads)):
            stat_ref[pl.ds(3 * head + i, 1), :] = row


def near_stats(mask, pack, own, outer):
    rows, width = own.shape
    return pl.pallas_call(
        near_stats_kernel,
        out_shape=jax.ShapeDtypeStruct((STAT_ROWS, rows), jnp.float32),
        in_specs=[SMEM, VMEM, VMEM, VMEM],
        out_specs=VMEM,
        compiler_params=params(),
        cost_estimate=HEAVY,
        name="near_stats",
    )(mask, pack, own, outer)


def inner_stats_kernel(mask_ref, pack_ref, swap_ref, stat_ref):
    rows = stat_ref.shape[1]
    width = pack_ref.shape[1] // 2
    inner_bias, _ = face_bias(mask_ref)
    for head in range(width // HEAD_DIM):
        at = columns(head, width)
        s = dot(swap_ref[rows:, at[0]], pack_ref[:rows, at[0]], NT) * (SCALE * LOG2E) + inner_bias
        g = dot(swap_ref[rows:, at[1]], pack_ref[:rows, at[1]], NT)
        for i, row in enumerate(raised_stats([s], [g])):
            stat_ref[pl.ds(3 * head + i, 1), :] = row


def inner_stats(mask, pack, swap):
    rows, heads = pack.shape[0] - FACE, pack.shape[1] // 2 // HEAD_DIM
    return pl.pallas_call(
        inner_stats_kernel,
        out_shape=jax.ShapeDtypeStruct((STAT_ROWS, rows), jnp.float32),
        in_specs=[SMEM, VMEM, VMEM],
        out_specs=VMEM,
        compiler_params=params(),
        cost_estimate=cost(rows, FACE, heads, 2, 4 * pack.size),
        name="inner_stats",
    )(mask, pack, swap)


def cond_stats_kernel(pack_ref, swap_ref, cond_ref, near_ref, inner_ref, stat_ref, out_ref):
    rows = near_ref.shape[1]
    width = pack_ref.shape[1] // 2
    cond_rows = cond_ref.shape[0]
    out_ref[:cond_rows, :] = cond_ref[...]
    stat_ref[...] = jnp.zeros_like(stat_ref)
    stat_ref[0] = near_ref[...]
    stat_ref[1] = inner_ref[...]
    for head in range(width // HEAD_DIM):
        at = columns(head, width)
        key, value = cond_ref[:, at[0]], cond_ref[:, at[1]]
        for side, ref in enumerate((pack_ref, swap_ref)):
            s = dot(key, ref[:rows, at[0]], NT) * (SCALE * LOG2E)
            g = dot(value, ref[:rows, at[1]], NT)
            for i, row in enumerate(raised_stats([s], [g])):
                stat_ref[2 + side, pl.ds(3 * head + i, 1), :] = row
    rest = stat_ref[...].reshape(4 * STAT_ROWS, rows)
    for part in range(3):
        rounded = rest.astype(jnp.bfloat16)
        out_ref[cond_rows:, pl.ds(part * rows, rows)] = rounded
        rest = rest - rounded.astype(jnp.float32)


def cond_stats(pack, swap, cond, near, inner):
    rows = near.shape[1]
    heads = pack.shape[1] // 2 // HEAD_DIM
    sent = (cond.shape[0] + 4 * STAT_ROWS, max(cond.shape[1], 3 * rows))
    return pl.pallas_call(
        cond_stats_kernel,
        out_shape=(
            jax.ShapeDtypeStruct((4, STAT_ROWS, rows), jnp.float32),
            jax.ShapeDtypeStruct(sent, jnp.bfloat16),
        ),
        in_specs=[VMEM] * 5,
        out_specs=(VMEM, VMEM),
        compiler_params=params(),
        cost_estimate=cost(2 * rows, cond.shape[0], heads, 2, 6 * pack.size),
        name="cond_stats",
    )(pack, swap, cond, near, inner)


def head_pass(key, value, q, d, level, delta, bias=None):
    s = dot(key, q, NT) * (SCALE * LOG2E)
    if bias is not None:
        s = s + bias
    p = jnp.exp2(s - level)
    grad_s = (p * (dot(value, d, NT) - delta)).astype(jnp.bfloat16)
    return p.astype(jnp.bfloat16), grad_s


def grads_kernel(
    pack_ref, swap_ref, cond_ref, mine_ref, sent_ref, out_ref, row_ref, their_ref
):
    rows = row_ref.shape[1]
    width = pack_ref.shape[1] // 2
    cond_rows = cond_ref.shape[0]
    parts = [
        sent_ref[cond_rows:, pl.ds(part * rows, rows)].astype(jnp.float32) for part in range(3)
    ]
    their_ref[...] = ((parts[2] + parts[1]) + parts[0]).reshape(their_ref.shape)
    for head in range(width // HEAD_DIM):
        at = columns(head, width)
        key, value = cond_ref[:, at[0]], cond_ref[:, at[1]]
        grad_k = 0.0
        grad_v = 0.0
        for side, ref in enumerate((pack_ref, swap_ref)):
            home, away = (mine_ref, their_ref) if side == 0 else (their_ref, mine_ref)
            parts = [
                [r[pl.ds(3 * head + i, 1), :] for i in range(3)]
                for r in (home.at[0], home.at[1], home.at[2], away.at[3])
            ]
            top = functools.reduce(jnp.maximum, [p[0] for p in parts])
            total = sum(p[1] * jnp.exp2(p[0] - top) for p in parts)
            weighted = sum(p[2] * jnp.exp2(p[0] - top) for p in parts)
            level = top + jnp.log2(total)
            delta = weighted / total
            q, d = ref[:rows, at[0]], ref[:rows, at[1]]
            p, grad_s = head_pass(key, value, q, d, level, delta)
            grad_k = grad_k + dot(grad_s, q)
            grad_v = grad_v + dot(p, d)
            if side == 0:
                row_ref[pl.ds(2 * head, 1), :] = level
                row_ref[pl.ds(2 * head + 1, 1), :] = delta
        out_ref[:, at[0]] = (grad_k * SCALE).astype(out_ref.dtype)
        out_ref[:, at[1]] = grad_v.astype(out_ref.dtype)


def grads_pass(pack, swap, cond, mine, theirs):
    rows = mine.shape[2]
    heads = pack.shape[1] // 2 // HEAD_DIM
    return pl.pallas_call(
        grads_kernel,
        out_shape=(
            jax.ShapeDtypeStruct(cond.shape, jnp.bfloat16),
            jax.ShapeDtypeStruct((STAT_ROWS, rows), jnp.float32),
        ),
        in_specs=[VMEM] * 5,
        out_specs=(VMEM,) * 2,
        scratch_shapes=[pltpu.VMEM(mine.shape, jnp.float32)],
        compiler_params=params(),
        cost_estimate=cost(2 * rows, cond.shape[0], heads, 4, 8 * pack.size),
        name="grads_pass",
    )(pack, swap, cond, mine, theirs)


def face_kernel(
    mask_ref, pack_ref, row_ref, swap_ref, outer_ref, to_inner_ref, to_outer_ref, sum_ref
):
    rows = row_ref.shape[1]
    width = pack_ref.shape[1] // 2
    inner_bias, outer_bias = face_bias(mask_ref)
    faces = (
        (swap_ref.at[rows:], inner_bias, to_inner_ref),
        (outer_ref, outer_bias, to_outer_ref),
    )
    for head in range(width // HEAD_DIM):
        at = columns(head, width)
        q, d = pack_ref[:rows, at[0]], pack_ref[:rows, at[1]]
        level, delta = [row_ref[pl.ds(2 * head + i, 1), :] for i in range(2)]
        att = 0.0
        grad_q = 0.0
        for face, bias, out in faces:
            key, value = face[:, at[0]], face[:, at[1]]
            p, grad_s = head_pass(key, value, q, d, level, delta, bias)
            out[:, at[0]] = (dot(grad_s, q) * SCALE).astype(out.dtype)
            out[:, at[1]] = dot(p, d).astype(out.dtype)
            att = att + dot(value, p, TN)
            grad_q = grad_q + dot(key, grad_s, TN)
        sum_ref[at[0], :] = grad_q
        sum_ref[at[1], :] = att


def face_pass(mask, pack, row_stats, swap, outer):
    rows = row_stats.shape[1]
    face = jax.ShapeDtypeStruct(outer.shape, jnp.bfloat16)
    return pl.pallas_call(
        face_kernel,
        out_shape=(face, face, jax.ShapeDtypeStruct((pack.shape[1], rows), jnp.float32)),
        in_specs=[SMEM] + [VMEM] * 4,
        out_specs=(VMEM,) * 3,
        compiler_params=params(),
        cost_estimate=LIGHT,
        name="face_pass",
    )(mask, pack, row_stats, swap, outer)


def own_kernel(
    pack_ref, row_ref, sum_ref, own_ref, cond_ref, far_cond_ref, att_ref, dq_ref, keep_ref
):
    rows = row_ref.shape[1]
    width = pack_ref.shape[1] // 2
    far_ref = far_cond_ref.at[: cond_ref.shape[0]]
    for head in range(width // HEAD_DIM):
        at = columns(head, width)
        q, d = pack_ref[:rows, at[0]], pack_ref[:rows, at[1]]
        level, delta = [row_ref[pl.ds(2 * head + i, 1), :] for i in range(2)]
        grad_q = sum_ref[at[0], :]
        att = sum_ref[at[1], :]
        for ref in (own_ref, cond_ref, far_ref):
            key, value = ref[:, at[0]], ref[:, at[1]]
            p, grad_s = head_pass(key, value, q, d, level, delta)
            if ref is own_ref:
                keep_ref[:, at[0]] = dot(grad_s, q) * SCALE
                keep_ref[:, at[1]] = dot(p, d)
            att = att + dot(value, p, TN)
            grad_q = grad_q + dot(key, grad_s, TN)
        att_ref[:, at[0]] = att.T.astype(jnp.bfloat16)
        dq_ref[:, at[0]] = (grad_q * SCALE).T.astype(jnp.bfloat16)


def own_pass(pack, row_stats, sums, own, cond, far_cond):
    rows, width = own.shape
    half = jax.ShapeDtypeStruct((rows, width // 2), jnp.bfloat16)
    return pl.pallas_call(
        own_kernel,
        out_shape=(half, half, jax.ShapeDtypeStruct((rows, width), jnp.float32)),
        in_specs=[VMEM] * 6,
        out_specs=(VMEM,) * 3,
        compiler_params=params(),
        cost_estimate=LIGHT,
        name="own_pass",
    )(pack, row_stats, sums, own, cond, far_cond)


def per_device(queries, keys_values, cond_kv, face_mask, d_out):
    size = lax.axis_size("tile")
    rows, width = queries.shape
    chips = size // CORES
    cond_rows = cond_kv.shape[0]
    even = lax.axis_index("tile") % CORES == 0
    swap_cores = other_core(size)
    across = [(t, t + 1) for t in range(1, size - 1, CORES)]
    across += [(b, a) for a, b in across]

    copies = spread(cond_kv, chips)
    cond = lax.all_to_all(copies, "tile", 0, 0, axis_index_groups=same_core(size), tiled=True)
    cond = cond.reshape(chips * cond_rows, 2 * width)

    own = lax.optimization_barrier(keys_values.reshape(rows, 2 * width))
    edge = lax.dynamic_slice_in_dim(own, jnp.where(even, 0, rows - FACE), FACE, axis=0)
    outer = lax.ppermute(edge, "tile", across)
    pack = pack_queries(queries, d_out, own)
    swap = lax.ppermute(pack, "tile", swap_cores)
    near = near_stats(face_mask, pack, own, outer)
    inner = inner_stats(face_mask, pack, swap)

    mine, sent = cond_stats(pack, swap, cond, near, inner)
    theirs = lax.ppermute(sent, "tile", swap_cores)
    grads, row_stats = grads_pass(pack, swap, cond, mine, theirs)
    blocks = grads.reshape(chips, cond_rows, 2 * width)
    parts = lax.all_to_all(blocks, "tile", 0, 0, axis_index_groups=same_core(size), tiled=True)
    grad_cond = total(parts)

    to_inner, to_outer, sums = face_pass(face_mask, pack, row_stats, swap, outer)
    from_outer = lax.ppermute(to_outer, "tile", across)
    from_inner = lax.ppermute(to_inner, "tile", swap_cores)
    attended, grad_q, keep = own_pass(pack, row_stats, sums, own, cond, theirs)
    keep, from_outer, from_inner = lax.optimization_barrier((keep, from_outer, from_inner))
    low = jnp.where(even, from_outer, from_inner).astype(jnp.float32)
    high = jnp.where(even, from_inner, from_outer).astype(jnp.float32)
    keep = keep + jnp.concatenate([low, high], axis=0)
    grad_kv = keep.astype(jnp.bfloat16).reshape(rows, 2, width)
    return attended, grad_q, grad_kv, grad_cond


def solution(mesh):
    return jax.shard_map(
        per_device,
        mesh=mesh,
        in_specs=(
            P("tile", "head"),
            P("tile", None, "head"),
            P("tile", None, "head"),
            P("tile", None),
            P("tile", "head"),
        ),
        out_specs=(
            P("tile", "head"),
            P("tile", "head"),
            P("tile", None, "head"),
            P("tile", None, "head"),
        ),
        check_vma=False,
    )
```

```python
import functools

import jax
import jax.numpy as jnp
from jax import lax
from jax.experimental import pallas as pl
from jax.experimental.pallas import tpu as pltpu
from jax.sharding import PartitionSpec as P

HEAD_DIM = 128
FACE = 128
CORES = 2
RUN = 4
STRIDE = 3
SCALE = HEAD_DIM**-0.5
LOG2E = 1.4426950408889634
NEG_LARGE = -1e30
STAT_ROWS = 16

NT = (((1,), (1,)), ((), ()))
TN = (((0,), (0,)), ((), ()))


def dot(a, b, dims=(((1,), (0,)), ((), ()))):
    return lax.dot_general(a, b, dims, preferred_element_type=jnp.float32)


def other_core(size):
    return [(t, t ^ 1) for t in range(size)]


def same_core(size):
    depth = size // (RUN * CORES)
    return [
        [((step * z % depth) * RUN + y) * CORES + c for z in range(depth) for y in range(RUN)]
        for c, step in enumerate((STRIDE, -STRIDE))
    ]


def params(mib=16):
    return pltpu.CompilerParams(vmem_limit_bytes=mib * 1024 * 1024)


VMEM = pl.BlockSpec(memory_space=pltpu.VMEM)
LIGHT = pl.CostEstimate(flops=1, bytes_accessed=1, transcendentals=0)
HEAVY = pl.CostEstimate(flops=6_000_000_000, bytes_accessed=0, transcendentals=0)
SMEM = pl.BlockSpec(memory_space=pltpu.SMEM)


def spread_kernel(cond_ref, out_ref):
    rows, _, width = cond_ref.shape
    flat = jnp.concatenate([cond_ref[:, 0, :], cond_ref[:, 1, :]], axis=1)
    out_ref[...] = jnp.broadcast_to(flat[None], out_ref.shape)


def spread(cond_kv, copies):
    rows, _, width = cond_kv.shape
    return pl.pallas_call(
        spread_kernel,
        out_shape=jax.ShapeDtypeStruct((copies, rows, 2 * width), cond_kv.dtype),
        in_specs=[VMEM],
        out_specs=VMEM,
        compiler_params=params(),
        name="spread",
    )(cond_kv)


def pack_kernel(q_ref, d_ref, own_ref, out_ref):
    rows, width = q_ref.shape
    even = lax.axis_index("tile") % CORES == 0
    start = pl.multiple_of(jnp.where(even, rows - FACE, 0), FACE)
    out_ref[:rows, :width] = q_ref[...]
    out_ref[:rows, width:] = d_ref[...]
    out_ref[rows:, :] = own_ref[pl.ds(start, FACE), :]


def pack_queries(queries, d_out, own):
    rows, width = own.shape
    return pl.pallas_call(
        pack_kernel,
        out_shape=jax.ShapeDtypeStruct((rows + FACE, width), own.dtype),
        in_specs=[VMEM] * 3,
        out_specs=VMEM,
        compiler_params=params(),
        cost_estimate=LIGHT,
        name="pack_queries",
    )(queries, d_out, own)


def total_kernel(parts_ref, out_ref):
    width = out_ref.shape[2]
    total = jnp.sum(parts_ref[...].astype(jnp.float32), axis=0)
    out_ref[:, 0, :] = total[:, :width]
    out_ref[:, 1, :] = total[:, width:]


def total(parts):
    _, rows, width = parts.shape
    return pl.pallas_call(
        total_kernel,
        out_shape=jax.ShapeDtypeStruct((rows, 2, width // 2), jnp.float32),
        in_specs=[VMEM],
        out_specs=VMEM,
        compiler_params=params(),
        name="total",
    )(parts)


def cost(queries, keys, heads, products, size):
    return pl.CostEstimate(
        flops=2 * products * heads * queries * keys * HEAD_DIM,
        bytes_accessed=size,
        transcendentals=heads * queries * keys,
    )


def face_bias(mask_ref):
    tile = lax.axis_index("tile")
    last = lax.axis_size("tile") - 1
    lower = jnp.where((mask_ref[0, 0] == 1) & (tile > 0), 0.0, NEG_LARGE)
    upper = jnp.where((mask_ref[0, 1] == 1) & (tile < last), 0.0, NEG_LARGE)
    even = tile % CORES == 0
    inner = jnp.where(even, upper, lower)
    outer = jnp.where(even, lower, upper)
    return inner.astype(jnp.float32), outer.astype(jnp.float32)


def columns(head, width):
    return [pl.ds(half * width + head * HEAD_DIM, HEAD_DIM) for half in range(2)]


def raised_stats(scores, grads):
    top = functools.reduce(jnp.maximum, [jnp.max(s, axis=0, keepdims=True) for s in scores])
    total = 0.0
    weighted = 0.0
    for s, g in zip(scores, grads):
        e = jnp.exp2(s - top)
        total = total + jnp.sum(e, axis=0, keepdims=True)
        weighted = weighted + jnp.sum(e * g, axis=0, keepdims=True)
    return top, total, weighted


def near_stats_kernel(mask_ref, pack_ref, own_ref, outer_ref, stat_ref):
    rows = stat_ref.shape[1]
    width = pack_ref.shape[1] // 2
    _, outer_bias = face_bias(mask_ref)
    for head in range(width // HEAD_DIM):
        at = columns(head, width)
        q, d = pack_ref[:rows, at[0]], pack_ref[:rows, at[1]]
        scores, grads = [], []
        for ref, bias in ((own_ref, None), (outer_ref, outer_bias)):
            s = dot(ref[:, at[0]], q, NT) * (SCALE * LOG2E)
            scores.append(s if bias is None else s + bias)
            grads.append(dot(ref[:, at[1]], d, NT))
        for i, row in enumerate(raised_stats(scores, grads)):
            stat_ref[pl.ds(3 * head + i, 1), :] = row


def near_stats(mask, pack, own, outer):
    rows, width = own.shape
    return pl.pallas_call(
        near_stats_kernel,
        out_shape=jax.ShapeDtypeStruct((STAT_ROWS, rows), jnp.float32),
        in_specs=[SMEM, VMEM, VMEM, VMEM],
        out_specs=VMEM,
        compiler_params=params(),
        cost_estimate=HEAVY,
        name="near_stats",
    )(mask, pack, own, outer)


def inner_stats_kernel(mask_ref, pack_ref, swap_ref, stat_ref):
    rows = stat_ref.shape[1]
    width = pack_ref.shape[1] // 2
    inner_bias, _ = face_bias(mask_ref)
    for head in range(width // HEAD_DIM):
        at = columns(head, width)
        s = dot(swap_ref[rows:, at[0]], pack_ref[:rows, at[0]], NT) * (SCALE * LOG2E) + inner_bias
        g = dot(swap_ref[rows:, at[1]], pack_ref[:rows, at[1]], NT)
        for i, row in enumerate(raised_stats([s], [g])):
            stat_ref[pl.ds(3 * head + i, 1), :] = row


def inner_stats(mask, pack, swap):
    rows, heads = pack.shape[0] - FACE, pack.shape[1] // 2 // HEAD_DIM
    return pl.pallas_call(
        inner_stats_kernel,
        out_shape=jax.ShapeDtypeStruct((STAT_ROWS, rows), jnp.float32),
        in_specs=[SMEM, VMEM, VMEM],
        out_specs=VMEM,
        compiler_params=params(),
        cost_estimate=cost(rows, FACE, heads, 2, 4 * pack.size),
        name="inner_stats",
    )(mask, pack, swap)


def cond_stats_kernel(pack_ref, swap_ref, cond_ref, near_ref, inner_ref, stat_ref, out_ref):
    rows = near_ref.shape[1]
    width = pack_ref.shape[1] // 2
    cond_rows = cond_ref.shape[0]
    out_ref[:cond_rows, :] = cond_ref[...]
    stat_ref[...] = jnp.zeros_like(stat_ref)
    stat_ref[0] = near_ref[...]
    stat_ref[1] = inner_ref[...]
    for head in range(width // HEAD_DIM):
        at = columns(head, width)
        key, value = cond_ref[:, at[0]], cond_ref[:, at[1]]
        for side, ref in enumerate((pack_ref, swap_ref)):
            s = dot(key, ref[:rows, at[0]], NT) * (SCALE * LOG2E)
            g = dot(value, ref[:rows, at[1]], NT)
            for i, row in enumerate(raised_stats([s], [g])):
                stat_ref[2 + side, pl.ds(3 * head + i, 1), :] = row
    rest = stat_ref[...].reshape(4 * STAT_ROWS, rows)
    for part in range(3):
        rounded = rest.astype(jnp.bfloat16)
        out_ref[cond_rows:, pl.ds(part * rows, rows)] = rounded
        rest = rest - rounded.astype(jnp.float32)


def cond_stats(pack, swap, cond, near, inner):
    rows = near.shape[1]
    heads = pack.shape[1] // 2 // HEAD_DIM
    sent = (cond.shape[0] + 4 * STAT_ROWS, max(cond.shape[1], 3 * rows))
    return pl.pallas_call(
        cond_stats_kernel,
        out_shape=(
            jax.ShapeDtypeStruct((4, STAT_ROWS, rows), jnp.float32),
            jax.ShapeDtypeStruct(sent, jnp.bfloat16),
        ),
        in_specs=[VMEM] * 5,
        out_specs=(VMEM, VMEM),
        compiler_params=params(),
        cost_estimate=cost(2 * rows, cond.shape[0], heads, 2, 6 * pack.size),
        name="cond_stats",
    )(pack, swap, cond, near, inner)


def head_pass(key, value, q, d, level, delta, bias=None):
    s = dot(key, q, NT) * (SCALE * LOG2E)
    if bias is not None:
        s = s + bias
    p = jnp.exp2(s - level)
    grad_s = (p * (dot(value, d, NT) - delta)).astype(jnp.bfloat16)
    return p.astype(jnp.bfloat16), grad_s


def grads_kernel(
    pack_ref, swap_ref, cond_ref, mine_ref, sent_ref, out_ref, row_ref, their_ref
):
    rows = row_ref.shape[1]
    width = pack_ref.shape[1] // 2
    cond_rows = cond_ref.shape[0]
    parts = [
        sent_ref[cond_rows:, pl.ds(part * rows, rows)].astype(jnp.float32) for part in range(3)
    ]
    their_ref[...] = ((parts[2] + parts[1]) + parts[0]).reshape(their_ref.shape)
    for head in range(width // HEAD_DIM):
        at = columns(head, width)
        key, value = cond_ref[:, at[0]], cond_ref[:, at[1]]
        grad_k = 0.0
        grad_v = 0.0
        for side, ref in enumerate((pack_ref, swap_ref)):
            home, away = (mine_ref, their_ref) if side == 0 else (their_ref, mine_ref)
            parts = [
                [r[pl.ds(3 * head + i, 1), :] for i in range(3)]
                for r in (home.at[0], home.at[1], home.at[2], away.at[3])
            ]
            top = functools.reduce(jnp.maximum, [p[0] for p in parts])
            total = sum(p[1] * jnp.exp2(p[0] - top) for p in parts)
            weighted = sum(p[2] * jnp.exp2(p[0] - top) for p in parts)
            level = top + jnp.log2(total)
            delta = weighted / total
            q, d = ref[:rows, at[0]], ref[:rows, at[1]]
            p, grad_s = head_pass(key, value, q, d, level, delta)
            grad_k = grad_k + dot(grad_s, q)
            grad_v = grad_v + dot(p, d)
            if side == 0:
                row_ref[pl.ds(2 * head, 1), :] = level
                row_ref[pl.ds(2 * head + 1, 1), :] = delta
        out_ref[:, at[0]] = (grad_k * SCALE).astype(out_ref.dtype)
        out_ref[:, at[1]] = grad_v.astype(out_ref.dtype)


def grads_pass(pack, swap, cond, mine, theirs):
    rows = mine.shape[2]
    heads = pack.shape[1] // 2 // HEAD_DIM
    return pl.pallas_call(
        grads_kernel,
        out_shape=(
            jax.ShapeDtypeStruct(cond.shape, jnp.bfloat16),
            jax.ShapeDtypeStruct((STAT_ROWS, rows), jnp.float32),
        ),
        in_specs=[VMEM] * 5,
        out_specs=(VMEM,) * 2,
        scratch_shapes=[pltpu.VMEM(mine.shape, jnp.float32)],
        compiler_params=params(),
        cost_estimate=cost(2 * rows, cond.shape[0], heads, 4, 8 * pack.size),
        name="grads_pass",
    )(pack, swap, cond, mine, theirs)


def face_kernel(
    mask_ref, pack_ref, row_ref, swap_ref, outer_ref, to_inner_ref, to_outer_ref, sum_ref
):
    rows = row_ref.shape[1]
    width = pack_ref.shape[1] // 2
    inner_bias, outer_bias = face_bias(mask_ref)
    faces = (
        (swap_ref.at[rows:], inner_bias, to_inner_ref),
        (outer_ref, outer_bias, to_outer_ref),
    )
    for head in range(width // HEAD_DIM):
        at = columns(head, width)
        q, d = pack_ref[:rows, at[0]], pack_ref[:rows, at[1]]
        level, delta = [row_ref[pl.ds(2 * head + i, 1), :] for i in range(2)]
        att = 0.0
        grad_q = 0.0
        for face, bias, out in faces:
            key, value = face[:, at[0]], face[:, at[1]]
            p, grad_s = head_pass(key, value, q, d, level, delta, bias)
            out[:, at[0]] = (dot(grad_s, q) * SCALE).astype(out.dtype)
            out[:, at[1]] = dot(p, d).astype(out.dtype)
            att = att + dot(value, p, TN)
            grad_q = grad_q + dot(key, grad_s, TN)
        sum_ref[at[0], :] = grad_q
        sum_ref[at[1], :] = att


def face_pass(mask, pack, row_stats, swap, outer):
    rows = row_stats.shape[1]
    face = jax.ShapeDtypeStruct(outer.shape, jnp.bfloat16)
    return pl.pallas_call(
        face_kernel,
        out_shape=(face, face, jax.ShapeDtypeStruct((pack.shape[1], rows), jnp.float32)),
        in_specs=[SMEM] + [VMEM] * 4,
        out_specs=(VMEM,) * 3,
        compiler_params=params(),
        cost_estimate=LIGHT,
        name="face_pass",
    )(mask, pack, row_stats, swap, outer)


def own_kernel(
    pack_ref, row_ref, sum_ref, own_ref, cond_ref, far_cond_ref, att_ref, dq_ref, keep_ref
):
    rows = row_ref.shape[1]
    width = pack_ref.shape[1] // 2
    far_ref = far_cond_ref.at[: cond_ref.shape[0]]
    for head in range(width // HEAD_DIM):
        at = columns(head, width)
        q, d = pack_ref[:rows, at[0]], pack_ref[:rows, at[1]]
        level, delta = [row_ref[pl.ds(2 * head + i, 1), :] for i in range(2)]
        grad_q = sum_ref[at[0], :]
        att = sum_ref[at[1], :]
        for ref in (own_ref, cond_ref, far_ref):
            key, value = ref[:, at[0]], ref[:, at[1]]
            p, grad_s = head_pass(key, value, q, d, level, delta)
            if ref is own_ref:
                keep_ref[:, at[0]] = dot(grad_s, q) * SCALE
                keep_ref[:, at[1]] = dot(p, d)
            att = att + dot(value, p, TN)
            grad_q = grad_q + dot(key, grad_s, TN)
        att_ref[:, at[0]] = att.T.astype(jnp.bfloat16)
        dq_ref[:, at[0]] = (grad_q * SCALE).T.astype(jnp.bfloat16)


def own_pass(pack, row_stats, sums, own, cond, far_cond):
    rows, width = own.shape
    half = jax.ShapeDtypeStruct((rows, width // 2), jnp.bfloat16)
    return pl.pallas_call(
        own_kernel,
        out_shape=(half, half, jax.ShapeDtypeStruct((rows, width), jnp.float32)),
        in_specs=[VMEM] * 6,
        out_specs=(VMEM,) * 3,
        compiler_params=params(),
        cost_estimate=LIGHT,
        name="own_pass",
    )(pack, row_stats, sums, own, cond, far_cond)


def per_device(queries, keys_values, cond_kv, face_mask, d_out):
    size = lax.axis_size("tile")
    rows, width = queries.shape
    chips = size // CORES
    cond_rows = cond_kv.shape[0]
    even = lax.axis_index("tile") % CORES == 0
    swap_cores = other_core(size)
    across = [(t, t + 1) for t in range(1, size - 1, CORES)]
    across += [(b, a) for a, b in across]

    copies = spread(cond_kv, chips)
    cond = lax.all_to_all(copies, "tile", 0, 0, axis_index_groups=same_core(size), tiled=True)
    cond = cond.reshape(chips * cond_rows, 2 * width)

    own = lax.optimization_barrier(keys_values.reshape(rows, 2 * width))
    edge = lax.dynamic_slice_in_dim(own, jnp.where(even, 0, rows - FACE), FACE, axis=0)
    outer = lax.ppermute(edge, "tile", across)
    pack = pack_queries(queries, d_out, own)
    swap = lax.ppermute(pack, "tile", swap_cores)
    near = near_stats(face_mask, pack, own, outer)
    inner = inner_stats(face_mask, pack, swap)

    mine, sent = cond_stats(pack, swap, cond, near, inner)
    theirs = lax.ppermute(sent, "tile", swap_cores)
    grads, row_stats = grads_pass(pack, swap, cond, mine, theirs)
    blocks = grads.reshape(chips, cond_rows, 2 * width)
    parts = lax.all_to_all(blocks, "tile", 0, 0, axis_index_groups=same_core(size), tiled=True)
    grad_cond = total(parts)

    to_inner, to_outer, sums = face_pass(face_mask, pack, row_stats, swap, outer)
    from_outer = lax.ppermute(to_outer, "tile", across)
    from_inner = lax.ppermute(to_inner, "tile", swap_cores)
    attended, grad_q, keep = own_pass(pack, row_stats, sums, own, cond, theirs)
    keep, from_outer, from_inner = lax.optimization_barrier((keep, from_outer, from_inner))
    low = jnp.where(even, from_outer, from_inner).astype(jnp.float32)
    high = jnp.where(even, from_inner, from_outer).astype(jnp.float32)
    keep = keep + jnp.concatenate([low, high], axis=0)
    grad_kv = keep.astype(jnp.bfloat16).reshape(rows, 2, width)
    return attended, grad_q, grad_kv, grad_cond


def solution(mesh):
    return jax.shard_map(
        per_device,
        mesh=mesh,
        in_specs=(
            P("tile", "head"),
            P("tile", None, "head"),
            P("tile", None, "head"),
            P("tile", None),
            P("tile", "head"),
        ),
        out_specs=(
            P("tile", "head"),
            P("tile", "head"),
            P("tile", None, "head"),
            P("tile", None, "head"),
        ),
        check_vma=False,
    )
```

```python
import functools

import jax
import jax.numpy as jnp
from jax import lax
from jax.experimental import pallas as pl
from jax.experimental.pallas import tpu as pltpu
from jax.sharding import PartitionSpec as P

HEAD_DIM = 128
FACE = 128
CORES = 2
RUN = 4
STRIDE = 3
SCALE = HEAD_DIM**-0.5
LOG2E = 1.4426950408889634
NEG_LARGE = -1e30
STAT_ROWS = 16

NT = (((1,), (1,)), ((), ()))
TN = (((0,), (0,)), ((), ()))


def dot(a, b, dims=(((1,), (0,)), ((), ()))):
    return lax.dot_general(a, b, dims, preferred_element_type=jnp.float32)


def other_core(size):
    return [(t, t ^ 1) for t in range(size)]


def same_core(size):
    depth = size // (RUN * CORES)
    return [
        [((step * z % depth) * RUN + y) * CORES + c for y in range(RUN) for z in range(depth)]
        for c, step in enumerate((STRIDE, -STRIDE))
    ]


def params(mib=16):
    return pltpu.CompilerParams(vmem_limit_bytes=mib * 1024 * 1024)


VMEM = pl.BlockSpec(memory_space=pltpu.VMEM)
LIGHT = pl.CostEstimate(flops=1, bytes_accessed=1, transcendentals=0)
HEAVY = pl.CostEstimate(flops=6_000_000_000, bytes_accessed=0, transcendentals=0)
SMEM = pl.BlockSpec(memory_space=pltpu.SMEM)


def spread_kernel(cond_ref, out_ref):
    rows, _, width = cond_ref.shape
    flat = jnp.concatenate([cond_ref[:, 0, :], cond_ref[:, 1, :]], axis=1)
    out_ref[...] = jnp.broadcast_to(flat[None], out_ref.shape)


def spread(cond_kv, copies):
    rows, _, width = cond_kv.shape
    return pl.pallas_call(
        spread_kernel,
        out_shape=jax.ShapeDtypeStruct((copies, rows, 2 * width), cond_kv.dtype),
        in_specs=[VMEM],
        out_specs=VMEM,
        compiler_params=params(),
        name="spread",
    )(cond_kv)


def pack_kernel(q_ref, d_ref, own_ref, out_ref):
    rows, width = q_ref.shape
    even = lax.axis_index("tile") % CORES == 0
    start = pl.multiple_of(jnp.where(even, rows - FACE, 0), FACE)
    out_ref[:rows, :width] = q_ref[...]
    out_ref[:rows, width:] = d_ref[...]
    out_ref[rows:, :] = own_ref[pl.ds(start, FACE), :]


def pack_queries(queries, d_out, own):
    rows, width = own.shape
    return pl.pallas_call(
        pack_kernel,
        out_shape=jax.ShapeDtypeStruct((rows + FACE, width), own.dtype),
        in_specs=[VMEM] * 3,
        out_specs=VMEM,
        compiler_params=params(),
        cost_estimate=LIGHT,
        name="pack_queries",
    )(queries, d_out, own)


def total_kernel(parts_ref, out_ref):
    width = out_ref.shape[2]
    total = jnp.sum(parts_ref[...].astype(jnp.float32), axis=0)
    out_ref[:, 0, :] = total[:, :width]
    out_ref[:, 1, :] = total[:, width:]


def total(parts):
    _, rows, width = parts.shape
    return pl.pallas_call(
        total_kernel,
        out_shape=jax.ShapeDtypeStruct((rows, 2, width // 2), jnp.float32),
        in_specs=[VMEM],
        out_specs=VMEM,
        compiler_params=params(),
        name="total",
    )(parts)


def cost(queries, keys, heads, products, size):
    return pl.CostEstimate(
        flops=2 * products * heads * queries * keys * HEAD_DIM,
        bytes_accessed=size,
        transcendentals=heads * queries * keys,
    )


def face_bias(mask_ref):
    tile = lax.axis_index("tile")
    last = lax.axis_size("tile") - 1
    lower = jnp.where((mask_ref[0, 0] == 1) & (tile > 0), 0.0, NEG_LARGE)
    upper = jnp.where((mask_ref[0, 1] == 1) & (tile < last), 0.0, NEG_LARGE)
    even = tile % CORES == 0
    inner = jnp.where(even, upper, lower)
    outer = jnp.where(even, lower, upper)
    return inner.astype(jnp.float32), outer.astype(jnp.float32)


def columns(head, width):
    return [pl.ds(half * width + head * HEAD_DIM, HEAD_DIM) for half in range(2)]


def raised_stats(scores, grads):
    top = functools.reduce(jnp.maximum, [jnp.max(s, axis=0, keepdims=True) for s in scores])
    total = 0.0
    weighted = 0.0
    for s, g in zip(scores, grads):
        e = jnp.exp2(s - top)
        total = total + jnp.sum(e, axis=0, keepdims=True)
        weighted = weighted + jnp.sum(e * g, axis=0, keepdims=True)
    return top, total, weighted


def near_stats_kernel(mask_ref, pack_ref, own_ref, outer_ref, stat_ref):
    rows = stat_ref.shape[1]
    width = pack_ref.shape[1] // 2
    _, outer_bias = face_bias(mask_ref)
    for head in range(width // HEAD_DIM):
        at = columns(head, width)
        q, d = pack_ref[:rows, at[0]], pack_ref[:rows, at[1]]
        scores, grads = [], []
        for ref, bias in ((own_ref, None), (outer_ref, outer_bias)):
            s = dot(ref[:, at[0]], q, NT) * (SCALE * LOG2E)
            scores.append(s if bias is None else s + bias)
            grads.append(dot(ref[:, at[1]], d, NT))
        for i, row in enumerate(raised_stats(scores, grads)):
            stat_ref[pl.ds(3 * head + i, 1), :] = row


def near_stats(mask, pack, own, outer):
    rows, width = own.shape
    return pl.pallas_call(
        near_stats_kernel,
        out_shape=jax.ShapeDtypeStruct((STAT_ROWS, rows), jnp.float32),
        in_specs=[SMEM, VMEM, VMEM, VMEM],
        out_specs=VMEM,
        compiler_params=params(),
        cost_estimate=HEAVY,
        name="near_stats",
    )(mask, pack, own, outer)


def inner_stats_kernel(mask_ref, pack_ref, swap_ref, stat_ref):
    rows = stat_ref.shape[1]
    width = pack_ref.shape[1] // 2
    inner_bias, _ = face_bias(mask_ref)
    for head in range(width // HEAD_DIM):
        at = columns(head, width)
        s = dot(swap_ref[rows:, at[0]], pack_ref[:rows, at[0]], NT) * (SCALE * LOG2E) + inner_bias
        g = dot(swap_ref[rows:, at[1]], pack_ref[:rows, at[1]], NT)
        for i, row in enumerate(raised_stats([s], [g])):
            stat_ref[pl.ds(3 * head + i, 1), :] = row


def inner_stats(mask, pack, swap):
    rows = pack.shape[0] - FACE
    return pl.pallas_call(
        inner_stats_kernel,
        out_shape=jax.ShapeDtypeStruct((STAT_ROWS, rows), jnp.float32),
        in_specs=[SMEM, VMEM, VMEM],
        out_specs=VMEM,
        compiler_params=params(),
        cost_estimate=LIGHT,
        name="inner_stats",
    )(mask, pack, swap)


def cond_stats_kernel(pack_ref, swap_ref, cond_ref, near_ref, inner_ref, stat_ref, out_ref):
    rows = near_ref.shape[1]
    width = pack_ref.shape[1] // 2
    cond_rows = cond_ref.shape[0]
    out_ref[:cond_rows, :] = cond_ref[...]
    stat_ref[...] = jnp.zeros_like(stat_ref)
    stat_ref[0] = near_ref[...]
    stat_ref[1] = inner_ref[...]
    for head in range(width // HEAD_DIM):
        at = columns(head, width)
        key, value = cond_ref[:, at[0]], cond_ref[:, at[1]]
        for side, ref in enumerate((pack_ref, swap_ref)):
            s = dot(key, ref[:rows, at[0]], NT) * (SCALE * LOG2E)
            g = dot(value, ref[:rows, at[1]], NT)
            for i, row in enumerate(raised_stats([s], [g])):
                stat_ref[2 + side, pl.ds(3 * head + i, 1), :] = row
    rest = stat_ref[...].reshape(4 * STAT_ROWS, rows)
    for part in range(3):
        rounded = rest.astype(jnp.bfloat16)
        out_ref[cond_rows:, pl.ds(part * rows, rows)] = rounded
        rest = rest - rounded.astype(jnp.float32)


def cond_stats(pack, swap, cond, near, inner):
    rows = near.shape[1]
    heads = pack.shape[1] // 2 // HEAD_DIM
    sent = (cond.shape[0] + 4 * STAT_ROWS, max(cond.shape[1], 3 * rows))
    return pl.pallas_call(
        cond_stats_kernel,
        out_shape=(
            jax.ShapeDtypeStruct((4, STAT_ROWS, rows), jnp.float32),
            jax.ShapeDtypeStruct(sent, jnp.bfloat16),
        ),
        in_specs=[VMEM] * 5,
        out_specs=(VMEM, VMEM),
        compiler_params=params(),
        cost_estimate=cost(2 * rows, cond.shape[0], heads, 2, 6 * pack.size),
        name="cond_stats",
    )(pack, swap, cond, near, inner)


def head_pass(key, value, q, d, level, delta, bias=None):
    s = dot(key, q, NT) * (SCALE * LOG2E)
    if bias is not None:
        s = s + bias
    p = jnp.exp2(s - level)
    grad_s = (p * (dot(value, d, NT) - delta)).astype(jnp.bfloat16)
    return p.astype(jnp.bfloat16), grad_s


def grads_kernel(
    pack_ref, swap_ref, cond_ref, mine_ref, sent_ref, out_ref, row_ref, their_ref
):
    rows = row_ref.shape[1]
    width = pack_ref.shape[1] // 2
    cond_rows = cond_ref.shape[0]
    parts = [
        sent_ref[cond_rows:, pl.ds(part * rows, rows)].astype(jnp.float32) for part in range(3)
    ]
    their_ref[...] = ((parts[2] + parts[1]) + parts[0]).reshape(their_ref.shape)
    for head in range(width // HEAD_DIM):
        at = columns(head, width)
        key, value = cond_ref[:, at[0]], cond_ref[:, at[1]]
        grad_k = 0.0
        grad_v = 0.0
        for side, ref in enumerate((pack_ref, swap_ref)):
            home, away = (mine_ref, their_ref) if side == 0 else (their_ref, mine_ref)
            parts = [
                [r[pl.ds(3 * head + i, 1), :] for i in range(3)]
                for r in (home.at[0], home.at[1], home.at[2], away.at[3])
            ]
            top = functools.reduce(jnp.maximum, [p[0] for p in parts])
            total = sum(p[1] * jnp.exp2(p[0] - top) for p in parts)
            weighted = sum(p[2] * jnp.exp2(p[0] - top) for p in parts)
            level = top + jnp.log2(total)
            delta = weighted / total
            q, d = ref[:rows, at[0]], ref[:rows, at[1]]
            p, grad_s = head_pass(key, value, q, d, level, delta)
            grad_k = grad_k + dot(grad_s, q)
            grad_v = grad_v + dot(p, d)
            if side == 0:
                row_ref[pl.ds(2 * head, 1), :] = level
                row_ref[pl.ds(2 * head + 1, 1), :] = delta
        out_ref[:, at[0]] = (grad_k * SCALE).astype(out_ref.dtype)
        out_ref[:, at[1]] = grad_v.astype(out_ref.dtype)


def grads_pass(pack, swap, cond, mine, theirs):
    rows = mine.shape[2]
    heads = pack.shape[1] // 2 // HEAD_DIM
    return pl.pallas_call(
        grads_kernel,
        out_shape=(
            jax.ShapeDtypeStruct(cond.shape, jnp.bfloat16),
            jax.ShapeDtypeStruct((STAT_ROWS, rows), jnp.float32),
        ),
        in_specs=[VMEM] * 5,
        out_specs=(VMEM,) * 2,
        scratch_shapes=[pltpu.VMEM(mine.shape, jnp.float32)],
        compiler_params=params(),
        cost_estimate=cost(2 * rows, cond.shape[0], heads, 4, 8 * pack.size),
        name="grads_pass",
    )(pack, swap, cond, mine, theirs)


def face_kernel(
    mask_ref, pack_ref, row_ref, swap_ref, outer_ref, to_inner_ref, to_outer_ref, sum_ref
):
    rows = row_ref.shape[1]
    width = pack_ref.shape[1] // 2
    inner_bias, outer_bias = face_bias(mask_ref)
    faces = (
        (swap_ref.at[rows:], inner_bias, to_inner_ref),
        (outer_ref, outer_bias, to_outer_ref),
    )
    for head in range(width // HEAD_DIM):
        at = columns(head, width)
        q, d = pack_ref[:rows, at[0]], pack_ref[:rows, at[1]]
        level, delta = [row_ref[pl.ds(2 * head + i, 1), :] for i in range(2)]
        att = 0.0
        grad_q = 0.0
        for face, bias, out in faces:
            key, value = face[:, at[0]], face[:, at[1]]
            p, grad_s = head_pass(key, value, q, d, level, delta, bias)
            out[:, at[0]] = (dot(grad_s, q) * SCALE).astype(out.dtype)
            out[:, at[1]] = dot(p, d).astype(out.dtype)
            att = att + dot(value, p, TN)
            grad_q = grad_q + dot(key, grad_s, TN)
        sum_ref[at[0], :] = grad_q
        sum_ref[at[1], :] = att


def face_pass(mask, pack, row_stats, swap, outer):
    rows = row_stats.shape[1]
    face = jax.ShapeDtypeStruct(outer.shape, jnp.bfloat16)
    return pl.pallas_call(
        face_kernel,
        out_shape=(face, face, jax.ShapeDtypeStruct((pack.shape[1], rows), jnp.float32)),
        in_specs=[SMEM] + [VMEM] * 4,
        out_specs=(VMEM,) * 3,
        compiler_params=params(),
        cost_estimate=LIGHT,
        name="face_pass",
    )(mask, pack, row_stats, swap, outer)


def own_kernel(
    pack_ref, row_ref, sum_ref, own_ref, cond_ref, far_cond_ref, att_ref, dq_ref, keep_ref
):
    rows = row_ref.shape[1]
    width = pack_ref.shape[1] // 2
    far_ref = far_cond_ref.at[: cond_ref.shape[0]]
    for head in range(width // HEAD_DIM):
        at = columns(head, width)
        q, d = pack_ref[:rows, at[0]], pack_ref[:rows, at[1]]
        level, delta = [row_ref[pl.ds(2 * head + i, 1), :] for i in range(2)]
        grad_q = sum_ref[at[0], :]
        att = sum_ref[at[1], :]
        for ref in (own_ref, cond_ref, far_ref):
            key, value = ref[:, at[0]], ref[:, at[1]]
            p, grad_s = head_pass(key, value, q, d, level, delta)
            if ref is own_ref:
                keep_ref[:, at[0]] = dot(grad_s, q) * SCALE
                keep_ref[:, at[1]] = dot(p, d)
            att = att + dot(value, p, TN)
            grad_q = grad_q + dot(key, grad_s, TN)
        att_ref[:, at[0]] = att.T.astype(jnp.bfloat16)
        dq_ref[:, at[0]] = (grad_q * SCALE).T.astype(jnp.bfloat16)


def own_pass(pack, row_stats, sums, own, cond, far_cond):
    rows, width = own.shape
    half = jax.ShapeDtypeStruct((rows, width // 2), jnp.bfloat16)
    return pl.pallas_call(
        own_kernel,
        out_shape=(half, half, jax.ShapeDtypeStruct((rows, width), jnp.float32)),
        in_specs=[VMEM] * 6,
        out_specs=(VMEM,) * 3,
        compiler_params=params(),
        cost_estimate=LIGHT,
        name="own_pass",
    )(pack, row_stats, sums, own, cond, far_cond)


def per_device(queries, keys_values, cond_kv, face_mask, d_out):
    size = lax.axis_size("tile")
    rows, width = queries.shape
    chips = size // CORES
    cond_rows = cond_kv.shape[0]
    even = lax.axis_index("tile") % CORES == 0
    swap_cores = other_core(size)
    across = [(t, t + 1) for t in range(1, size - 1, CORES)]
    across += [(b, a) for a, b in across]

    copies = spread(cond_kv, chips)
    cond = lax.all_to_all(copies, "tile", 0, 0, axis_index_groups=same_core(size), tiled=True)
    cond = cond.reshape(chips * cond_rows, 2 * width)

    own = lax.optimization_barrier(keys_values.reshape(rows, 2 * width))
    edge = lax.dynamic_slice_in_dim(own, jnp.where(even, 0, rows - FACE), FACE, axis=0)
    outer = lax.ppermute(edge, "tile", across)
    pack = pack_queries(queries, d_out, own)
    swap = lax.ppermute(pack, "tile", swap_cores)
    near = near_stats(face_mask, pack, own, outer)
    inner = inner_stats(face_mask, pack, swap)

    mine, sent = cond_stats(pack, swap, cond, near, inner)
    theirs = lax.ppermute(sent, "tile", swap_cores)
    grads, row_stats = grads_pass(pack, swap, cond, mine, theirs)
    blocks = grads.reshape(chips, cond_rows, 2 * width)
    parts = lax.all_to_all(blocks, "tile", 0, 0, axis_index_groups=same_core(size), tiled=True)
    grad_cond = total(parts)

    to_inner, to_outer, sums = face_pass(face_mask, pack, row_stats, swap, outer)
    from_outer = lax.ppermute(to_outer, "tile", across)
    from_inner = lax.ppermute(to_inner, "tile", swap_cores)
    attended, grad_q, keep = own_pass(pack, row_stats, sums, own, cond, theirs)
    keep, from_outer, from_inner = lax.optimization_barrier((keep, from_outer, from_inner))
    low = jnp.where(even, from_outer, from_inner).astype(jnp.float32)
    high = jnp.where(even, from_inner, from_outer).astype(jnp.float32)
    keep = keep + jnp.concatenate([low, high], axis=0)
    grad_kv = keep.astype(jnp.bfloat16).reshape(rows, 2, width)
    return attended, grad_q, grad_kv, grad_cond


def solution(mesh):
    return jax.shard_map(
        per_device,
        mesh=mesh,
        in_specs=(
            P("tile", "head"),
            P("tile", None, "head"),
            P("tile", None, "head"),
            P("tile", None),
            P("tile", "head"),
        ),
        out_specs=(
            P("tile", "head"),
            P("tile", "head"),
            P("tile", None, "head"),
            P("tile", None, "head"),
        ),
        check_vma=False,
    )
```

```python
import functools

import jax
import jax.numpy as jnp
from jax import lax
from jax.experimental import pallas as pl
from jax.experimental.pallas import tpu as pltpu
from jax.sharding import PartitionSpec as P

HEAD_DIM = 128
FACE = 128
CORES = 2
RUN = 4
STRIDE = 3
SCALE = HEAD_DIM**-0.5
LOG2E = 1.4426950408889634
NEG_LARGE = -1e30
STAT_ROWS = 16

NT = (((1,), (1,)), ((), ()))
TN = (((0,), (0,)), ((), ()))


def dot(a, b, dims=(((1,), (0,)), ((), ()))):
    return lax.dot_general(a, b, dims, preferred_element_type=jnp.float32)


def other_core(size):
    return [(t, t ^ 1) for t in range(size)]


def same_core(size):
    depth = size // (RUN * CORES)
    return [
        [((step * z % depth) * RUN + y) * CORES + c for y in range(RUN) for z in range(depth)]
        for c, step in enumerate((STRIDE, -STRIDE))
    ]


def params(mib=16):
    return pltpu.CompilerParams(vmem_limit_bytes=mib * 1024 * 1024)


VMEM = pl.BlockSpec(memory_space=pltpu.VMEM)
LIGHT = pl.CostEstimate(flops=1, bytes_accessed=1, transcendentals=0)
HEAVY = pl.CostEstimate(flops=6_000_000_000, bytes_accessed=0, transcendentals=0)
SMEM = pl.BlockSpec(memory_space=pltpu.SMEM)


def spread_kernel(cond_ref, out_ref):
    rows, _, width = cond_ref.shape
    flat = jnp.concatenate([cond_ref[:, 0, :], cond_ref[:, 1, :]], axis=1)
    out_ref[...] = jnp.broadcast_to(flat[None], out_ref.shape)


def spread(cond_kv, copies):
    rows, _, width = cond_kv.shape
    return pl.pallas_call(
        spread_kernel,
        out_shape=jax.ShapeDtypeStruct((copies, rows, 2 * width), cond_kv.dtype),
        in_specs=[VMEM],
        out_specs=VMEM,
        compiler_params=params(),
        name="spread",
    )(cond_kv)


def pack_kernel(q_ref, d_ref, own_ref, out_ref):
    rows, width = q_ref.shape
    even = lax.axis_index("tile") % CORES == 0
    start = pl.multiple_of(jnp.where(even, rows - FACE, 0), FACE)
    out_ref[:rows, :width] = q_ref[...]
    out_ref[:rows, width:] = d_ref[...]
    out_ref[rows:, :] = own_ref[pl.ds(start, FACE), :]


def pack_queries(queries, d_out, own):
    rows, width = own.shape
    return pl.pallas_call(
        pack_kernel,
        out_shape=jax.ShapeDtypeStruct((rows + FACE, width), own.dtype),
        in_specs=[VMEM] * 3,
        out_specs=VMEM,
        compiler_params=params(),
        cost_estimate=LIGHT,
        name="pack_queries",
    )(queries, d_out, own)


def total_kernel(parts_ref, out_ref):
    width = out_ref.shape[2]
    total = jnp.sum(parts_ref[...].astype(jnp.float32), axis=0)
    out_ref[:, 0, :] = total[:, :width]
    out_ref[:, 1, :] = total[:, width:]


def total(parts):
    _, rows, width = parts.shape
    return pl.pallas_call(
        total_kernel,
        out_shape=jax.ShapeDtypeStruct((rows, 2, width // 2), jnp.float32),
        in_specs=[VMEM],
        out_specs=VMEM,
        compiler_params=params(),
        name="total",
    )(parts)


def cost(queries, keys, heads, products, size):
    return pl.CostEstimate(
        flops=2 * products * heads * queries * keys * HEAD_DIM,
        bytes_accessed=size,
        transcendentals=heads * queries * keys,
    )


def face_bias(mask_ref):
    tile = lax.axis_index("tile")
    last = lax.axis_size("tile") - 1
    lower = jnp.where((mask_ref[0, 0] == 1) & (tile > 0), 0.0, NEG_LARGE)
    upper = jnp.where((mask_ref[0, 1] == 1) & (tile < last), 0.0, NEG_LARGE)
    even = tile % CORES == 0
    inner = jnp.where(even, upper, lower)
    outer = jnp.where(even, lower, upper)
    return inner.astype(jnp.float32), outer.astype(jnp.float32)


def columns(head, width):
    return [pl.ds(half * width + head * HEAD_DIM, HEAD_DIM) for half in range(2)]


def raised_stats(scores, grads):
    top = functools.reduce(jnp.maximum, [jnp.max(s, axis=0, keepdims=True) for s in scores])
    total = 0.0
    weighted = 0.0
    for s, g in zip(scores, grads):
        e = jnp.exp2(s - top)
        total = total + jnp.sum(e, axis=0, keepdims=True)
        weighted = weighted + jnp.sum(e * g, axis=0, keepdims=True)
    return top, total, weighted


def near_stats_kernel(mask_ref, pack_ref, own_ref, outer_ref, stat_ref):
    rows = stat_ref.shape[1]
    width = pack_ref.shape[1] // 2
    _, outer_bias = face_bias(mask_ref)
    for head in range(width // HEAD_DIM):
        at = columns(head, width)
        q, d = pack_ref[:rows, at[0]], pack_ref[:rows, at[1]]
        scores, grads = [], []
        for ref, bias in ((own_ref, None), (outer_ref, outer_bias)):
            s = dot(ref[:, at[0]], q, NT) * (SCALE * LOG2E)
            scores.append(s if bias is None else s + bias)
            grads.append(dot(ref[:, at[1]], d, NT))
        for i, row in enumerate(raised_stats(scores, grads)):
            stat_ref[pl.ds(3 * head + i, 1), :] = row


def near_stats(mask, pack, own, outer):
    rows, width = own.shape
    return pl.pallas_call(
        near_stats_kernel,
        out_shape=jax.ShapeDtypeStruct((STAT_ROWS, rows), jnp.float32),
        in_specs=[SMEM, VMEM, VMEM, VMEM],
        out_specs=VMEM,
        compiler_params=params(),
        cost_estimate=HEAVY,
        name="near_stats",
    )(mask, pack, own, outer)


def inner_stats_kernel(mask_ref, pack_ref, swap_ref, stat_ref):
    rows = stat_ref.shape[1]
    width = pack_ref.shape[1] // 2
    inner_bias, _ = face_bias(mask_ref)
    for head in range(width // HEAD_DIM):
        at = columns(head, width)
        s = dot(swap_ref[rows:, at[0]], pack_ref[:rows, at[0]], NT) * (SCALE * LOG2E) + inner_bias
        g = dot(swap_ref[rows:, at[1]], pack_ref[:rows, at[1]], NT)
        for i, row in enumerate(raised_stats([s], [g])):
            stat_ref[pl.ds(3 * head + i, 1), :] = row


def inner_stats(mask, pack, swap):
    rows, heads = pack.shape[0] - FACE, pack.shape[1] // 2 // HEAD_DIM
    return pl.pallas_call(
        inner_stats_kernel,
        out_shape=jax.ShapeDtypeStruct((STAT_ROWS, rows), jnp.float32),
        in_specs=[SMEM, VMEM, VMEM],
        out_specs=VMEM,
        compiler_params=params(),
        cost_estimate=cost(rows, FACE, heads, 2, 4 * pack.size),
        name="inner_stats",
    )(mask, pack, swap)


def both_cores(pack_ref, swap_ref, rows, at):
    return [jnp.concatenate([ref[:rows, a] for ref in (pack_ref, swap_ref)], axis=0) for a in at]


def cond_stats_kernel(pack_ref, swap_ref, cond_ref, near_ref, inner_ref, stat_ref, out_ref):
    rows = near_ref.shape[1]
    width = pack_ref.shape[1] // 2
    cond_rows = cond_ref.shape[0]
    out_ref[:cond_rows, :] = cond_ref[...]
    stat_ref[0] = near_ref[...]
    stat_ref[1] = inner_ref[...]
    stat_ref[2:] = jnp.zeros((2,) + near_ref.shape, jnp.float32)
    for head in range(width // HEAD_DIM):
        at = columns(head, width)
        q, d = both_cores(pack_ref, swap_ref, rows, at)
        s = dot(cond_ref[:, at[0]], q, NT) * (SCALE * LOG2E)
        g = dot(cond_ref[:, at[1]], d, NT)
        for i, row in enumerate(raised_stats([s], [g])):
            for side in range(2):
                stat_ref[2 + side, pl.ds(3 * head + i, 1), :] = row[:, side * rows : (side + 1) * rows]
    rest = stat_ref[...].reshape(4 * STAT_ROWS, rows)
    for part in range(3):
        rounded = rest.astype(jnp.bfloat16)
        out_ref[cond_rows:, pl.ds(part * rows, rows)] = rounded
        rest = rest - rounded.astype(jnp.float32)


def cond_stats(pack, swap, cond, near, inner):
    rows = near.shape[1]
    heads = pack.shape[1] // 2 // HEAD_DIM
    sent = (cond.shape[0] + 4 * STAT_ROWS, max(cond.shape[1], 3 * rows))
    return pl.pallas_call(
        cond_stats_kernel,
        out_shape=(
            jax.ShapeDtypeStruct((4, STAT_ROWS, rows), jnp.float32),
            jax.ShapeDtypeStruct(sent, jnp.bfloat16),
        ),
        in_specs=[VMEM] * 5,
        out_specs=(VMEM, VMEM),
        compiler_params=params(),
        cost_estimate=cost(2 * rows, cond.shape[0], heads, 2, 6 * pack.size),
        name="cond_stats",
    )(pack, swap, cond, near, inner)


def head_pass(key, value, q, d, level, delta, bias=None):
    s = dot(key, q, NT) * (SCALE * LOG2E)
    if bias is not None:
        s = s + bias
    p = jnp.exp2(s - level)
    grad_s = (p * (dot(value, d, NT) - delta)).astype(jnp.bfloat16)
    return p.astype(jnp.bfloat16), grad_s


def grads_kernel(
    pack_ref, swap_ref, cond_ref, mine_ref, sent_ref, out_ref, row_ref, their_ref
):
    rows = row_ref.shape[1]
    width = pack_ref.shape[1] // 2
    cond_rows = cond_ref.shape[0]
    parts = [
        sent_ref[cond_rows:, pl.ds(part * rows, rows)].astype(jnp.float32) for part in range(3)
    ]
    their_ref[...] = ((parts[2] + parts[1]) + parts[0]).reshape(their_ref.shape)
    for head in range(width // HEAD_DIM):
        at = columns(head, width)
        levels, deltas = [], []
        for side in range(2):
            home, away = (mine_ref, their_ref) if side == 0 else (their_ref, mine_ref)
            parts = [
                [r[pl.ds(3 * head + i, 1), :] for i in range(3)]
                for r in (home.at[0], home.at[1], home.at[2], away.at[3])
            ]
            top = functools.reduce(jnp.maximum, [p[0] for p in parts])
            total = sum(p[1] * jnp.exp2(p[0] - top) for p in parts)
            weighted = sum(p[2] * jnp.exp2(p[0] - top) for p in parts)
            levels.append(top + jnp.log2(total))
            deltas.append(weighted / total)
        row_ref[pl.ds(2 * head, 1), :] = levels[0]
        row_ref[pl.ds(2 * head + 1, 1), :] = deltas[0]
        q, d = both_cores(pack_ref, swap_ref, rows, at)
        level, delta = [jnp.concatenate(pair, axis=1) for pair in (levels, deltas)]
        p, grad_s = head_pass(cond_ref[:, at[0]], cond_ref[:, at[1]], q, d, level, delta)
        out_ref[:, at[0]] = (dot(grad_s, q) * SCALE).astype(out_ref.dtype)
        out_ref[:, at[1]] = dot(p, d).astype(out_ref.dtype)


def grads_pass(pack, swap, cond, mine, theirs):
    rows = mine.shape[2]
    heads = pack.shape[1] // 2 // HEAD_DIM
    return pl.pallas_call(
        grads_kernel,
        out_shape=(
            jax.ShapeDtypeStruct(cond.shape, jnp.bfloat16),
            jax.ShapeDtypeStruct((STAT_ROWS, rows), jnp.float32),
        ),
        in_specs=[VMEM] * 5,
        out_specs=(VMEM,) * 2,
        scratch_shapes=[pltpu.VMEM(mine.shape, jnp.float32)],
        compiler_params=params(),
        cost_estimate=cost(2 * rows, cond.shape[0], heads, 4, 8 * pack.size),
        name="grads_pass",
    )(pack, swap, cond, mine, theirs)


def face_kernel(
    mask_ref, pack_ref, row_ref, swap_ref, outer_ref, to_inner_ref, to_outer_ref, sum_ref
):
    rows = row_ref.shape[1]
    width = pack_ref.shape[1] // 2
    inner_bias, outer_bias = face_bias(mask_ref)
    faces = (
        (swap_ref.at[rows:], inner_bias, to_inner_ref),
        (outer_ref, outer_bias, to_outer_ref),
    )
    for head in range(width // HEAD_DIM):
        at = columns(head, width)
        q, d = pack_ref[:rows, at[0]], pack_ref[:rows, at[1]]
        level, delta = [row_ref[pl.ds(2 * head + i, 1), :] for i in range(2)]
        att = 0.0
        grad_q = 0.0
        for face, bias, out in faces:
            key, value = face[:, at[0]], face[:, at[1]]
            p, grad_s = head_pass(key, value, q, d, level, delta, bias)
            out[:, at[0]] = (dot(grad_s, q) * SCALE).astype(out.dtype)
            out[:, at[1]] = dot(p, d).astype(out.dtype)
            att = att + dot(value, p, TN)
            grad_q = grad_q + dot(key, grad_s, TN)
        sum_ref[at[0], :] = grad_q
        sum_ref[at[1], :] = att


def face_pass(mask, pack, row_stats, swap, outer):
    rows = row_stats.shape[1]
    face = jax.ShapeDtypeStruct(outer.shape, jnp.bfloat16)
    return pl.pallas_call(
        face_kernel,
        out_shape=(face, face, jax.ShapeDtypeStruct((pack.shape[1], rows), jnp.float32)),
        in_specs=[SMEM] + [VMEM] * 4,
        out_specs=(VMEM,) * 3,
        compiler_params=params(),
        cost_estimate=LIGHT,
        name="face_pass",
    )(mask, pack, row_stats, swap, outer)


def own_kernel(
    pack_ref, row_ref, sum_ref, own_ref, cond_ref, far_cond_ref, att_ref, dq_ref, keep_ref
):
    rows = row_ref.shape[1]
    width = pack_ref.shape[1] // 2
    far_ref = far_cond_ref.at[: cond_ref.shape[0]]
    for head in range(width // HEAD_DIM):
        at = columns(head, width)
        q, d = pack_ref[:rows, at[0]], pack_ref[:rows, at[1]]
        level, delta = [row_ref[pl.ds(2 * head + i, 1), :] for i in range(2)]
        grad_q = sum_ref[at[0], :]
        att = sum_ref[at[1], :]
        for ref in (own_ref, cond_ref, far_ref):
            key, value = ref[:, at[0]], ref[:, at[1]]
            p, grad_s = head_pass(key, value, q, d, level, delta)
            if ref is own_ref:
                keep_ref[:, at[0]] = dot(grad_s, q) * SCALE
                keep_ref[:, at[1]] = dot(p, d)
            att = att + dot(value, p, TN)
            grad_q = grad_q + dot(key, grad_s, TN)
        att_ref[:, at[0]] = att.T.astype(jnp.bfloat16)
        dq_ref[:, at[0]] = (grad_q * SCALE).T.astype(jnp.bfloat16)


def own_pass(pack, row_stats, sums, own, cond, far_cond):
    rows, width = own.shape
    half = jax.ShapeDtypeStruct((rows, width // 2), jnp.bfloat16)
    return pl.pallas_call(
        own_kernel,
        out_shape=(half, half, jax.ShapeDtypeStruct((rows, width), jnp.float32)),
        in_specs=[VMEM] * 6,
        out_specs=(VMEM,) * 3,
        compiler_params=params(),
        cost_estimate=LIGHT,
        name="own_pass",
    )(pack, row_stats, sums, own, cond, far_cond)


def per_device(queries, keys_values, cond_kv, face_mask, d_out):
    size = lax.axis_size("tile")
    rows, width = queries.shape
    chips = size // CORES
    cond_rows = cond_kv.shape[0]
    even = lax.axis_index("tile") % CORES == 0
    swap_cores = other_core(size)
    across = [(t, t + 1) for t in range(1, size - 1, CORES)]
    across += [(b, a) for a, b in across]

    copies = spread(cond_kv, chips)
    cond = lax.all_to_all(copies, "tile", 0, 0, axis_index_groups=same_core(size), tiled=True)
    cond = cond.reshape(chips * cond_rows, 2 * width)

    own = lax.optimization_barrier(keys_values.reshape(rows, 2 * width))
    edge = lax.dynamic_slice_in_dim(own, jnp.where(even, 0, rows - FACE), FACE, axis=0)
    outer = lax.ppermute(edge, "tile", across)
    pack = pack_queries(queries, d_out, own)
    swap = lax.ppermute(pack, "tile", swap_cores)
    near = near_stats(face_mask, pack, own, outer)
    inner = inner_stats(face_mask, pack, swap)

    mine, sent = cond_stats(pack, swap, cond, near, inner)
    theirs = lax.ppermute(sent, "tile", swap_cores)
    grads, row_stats = grads_pass(pack, swap, cond, mine, theirs)
    blocks = grads.reshape(chips, cond_rows, 2 * width)
    parts = lax.all_to_all(blocks, "tile", 0, 0, axis_index_groups=same_core(size), tiled=True)
    grad_cond = total(parts)

    to_inner, to_outer, sums = face_pass(face_mask, pack, row_stats, swap, outer)
    from_outer = lax.ppermute(to_outer, "tile", across)
    from_inner = lax.ppermute(to_inner, "tile", swap_cores)
    attended, grad_q, keep = own_pass(pack, row_stats, sums, own, cond, theirs)
    keep, from_outer, from_inner = lax.optimization_barrier((keep, from_outer, from_inner))
    low = jnp.where(even, from_outer, from_inner).astype(jnp.float32)
    high = jnp.where(even, from_inner, from_outer).astype(jnp.float32)
    keep = keep + jnp.concatenate([low, high], axis=0)
    grad_kv = keep.astype(jnp.bfloat16).reshape(rows, 2, width)
    return attended, grad_q, grad_kv, grad_cond


def solution(mesh):
    return jax.shard_map(
        per_device,
        mesh=mesh,
        in_specs=(
            P("tile", "head"),
            P("tile", None, "head"),
            P("tile", None, "head"),
            P("tile", None),
            P("tile", "head"),
        ),
        out_specs=(
            P("tile", "head"),
            P("tile", "head"),
            P("tile", None, "head"),
            P("tile", None, "head"),
        ),
        check_vma=False,
    )
```
